32 devices in a mesh: group: 2 (over x), gx: 4 (over y, core), gy: 4 (over z).
Axes of the slice: x: 2, y: 2, z: 4, core: 2. Of those that a mesh axis runs over, the one named last changes fastest.
Arguments:
- wave_now: float32 [4, 64, 32, 512], P('group', None, 'gx', 'gy'), parts along dimension 0, may hold values from -6 to 46
- wave_before: float32 [4, 64, 32, 512], P('group', None, 'gx', 'gy'), parts along dimension 0, may hold values from -6 to 86
- courant: float32 [128, 32, 512], P('group', 'gx', 'gy'), parts along dimension 0, may hold values from 0.03 to 0.15
- records: bfloat16 [512, 2, 4096], P(('group', 'gx', 'gy')), parts along dimension 0, may hold values from -0.59765625 to 0.59765625
- signs: int32 [4, 256], P('group', ('gx', 'gy')), parts along dimension 0, may hold values from -1 to 1
- source_x: int32 [512], P(('group', 'gx', 'gy')), parts along dimension 0, may hold values from 0 to 31
- source_y: int32 [512], P(('group', 'gx', 'gy')), parts along dimension 0, may hold values from 0 to 511
- receiver_cell: int32 [8192], P('group'), parts along dimension 0, may hold values from 0 to 1023, as said below
Outputs:
- wave_after: float32 [4, 64, 32, 512], P('group', None, 'gx', 'gy'), parts along dimension 0
- wave_middle: float32 [4, 64, 32, 512], P('group', None, 'gx', 'gy'), parts along dimension 0
The draws below stay inside these ranges and needn't reach their ends.
There are 2 independent parts, one for each index of `group`. The reference program is written for one: setup_inputs(seed, part) draws one part's arguments, and reference() takes and returns one part's arrays. A program takes and returns all parts, laid end to end along the dimension named above; each array names one. Nothing has to cross between parts.
Inputs may be any that keep to these rules, and one draw needn't show every extreme that they name: `receiver_cell`: receivers of one tile may share a cell.
All inputs are finite; a program needn't handle non-finite values.
Results may differ from the reference program's by a relative error of at most 0.0003.
Values sent between devices are 32-bit elements; how exact they have to be, the bound alone decides.
No kernel may reach another device: no remote copies, remote signals or barrier semaphores. Data moves between devices by JAX's collectives and lax.ppermute only.
A program may use at most 192 MiB of HBM per device.

```python
import math
import jax
import jax.numpy as jnp
from jax import lax

CX = 8
CY = 128
NZ = 64
SHOT_DEV = 16
REC_DEV = 256
RDEPTH = 2
NX = 32
NY = 512
SHOTS = 256
RECV = 4096
RADIUS = 136
N_GX = 4
N_GY = 4


def smooth_part(key, peak, lowest):
    level = peak * jax.random.uniform(key, (2, 1, 1, 1), jnp.float32, lowest, 1.0)
    depth = jnp.sin(jnp.pi * (jnp.arange(NZ, dtype=jnp.float32) + 1.0) / (NZ + 1.0))
    across = jnp.sin(jnp.pi * (jnp.arange(NX, dtype=jnp.float32) + 1.0) / (NX + 1.0))
    along = jnp.sin(jnp.pi * (jnp.arange(NY, dtype=jnp.float32) + 1.0) / (NY + 1.0))
    return level * depth[None, :, None, None] * across[None, None, :, None] * along[None, None, None, :]


def rough_part(key):
    return jnp.clip(jax.random.normal(key, (2, NZ, NX, NY), jnp.float32), -6.0, 6.0)


def draw_wave_now(key, part):
    base = smooth_part(key, 40.0, 0.75)
    key = jax.random.fold_in(key, 21)
    return (base + rough_part(key)).astype(jnp.float32)


def draw_wave_before(key, part):
    base = smooth_part(key, 40.0, 0.75)
    key = jax.random.fold_in(key, 22)
    return (2.0 * base + rough_part(key)).astype(jnp.float32)


def draw_signs(key, part):
    key = jax.random.fold_in(key, 11)
    values = 2 * jax.random.randint(key, (2, SHOTS), 0, 2) - 1
    return values.at[0, 0].set(1).at[0, 1].set(-1).astype(jnp.int32)


def draw_source_x(key, part):
    key = jax.random.fold_in(key, 12)
    values = jax.random.randint(key, (SHOTS,), 0, NX)
    return values.at[0].set(NX - 1).at[1].set(0).astype(jnp.int32)


def draw_source_y(key, part):
    key = jax.random.fold_in(key, 13)
    values = jax.random.randint(key, (SHOTS,), 0, NY)
    return values.at[0].set(NY - 1).at[1].set(0).astype(jnp.int32)


def draw_receiver_cell(key, part):
    key = jax.random.fold_in(key, 14)
    values = jax.random.randint(key, (RECV,), 0, CX * CY)
    return values.at[0].set(CX * CY - 1).at[1].set(0).astype(jnp.int32)


def strengthened(array, rng, source, target, parts, factor):
    owner, partner = [(jnp.arange(array.shape[position]) // (array.shape[position] // parts)).reshape([-1 if axis == position else 1 for axis in range(array.ndim)]) for position in (source, target)]
    chosen = jax.random.permutation(rng, parts)[partner]
    strong = (owner == chosen) | (owner == (partner + parts // 2) % parts)
    return jnp.where(strong, factor * array, array)


def shard_levels(stream_key, dims, pieces, smallest, high):
    def one(axis_at, blocks):
        steps = jax.random.uniform(jax.random.fold_in(jax.random.fold_in(stream_key, 6), axis_at), (blocks,), jnp.float32, smallest / len(pieces), high / len(pieces))
        return jnp.repeat(jnp.exp(steps), dims[axis_at] // blocks).reshape((-1,) + (1,) * (len(dims) - axis_at - 1))

    gain = one(*pieces[0])
    for cut in pieces[1:]:
        gain = gain * one(*cut)
    return gain


def heavy_noise(key, dims, scale, most, shards, heavy, kind=jnp.bfloat16):
    values = scale * jax.random.normal(key, dims, jnp.float32)
    if shards:
        values = values * shard_levels(key, dims, shards, -0.22, 0.18)
    return jnp.clip(strengthened(values, jax.random.fold_in(key, 3), *heavy), -most, most).astype(kind)


def setup_inputs(seed: int = 0, part: int = 0) -> dict:
    streams_of = jax.random.split(jax.random.key(seed), 9)
    part_splits = jax.random.split(jax.random.fold_in(streams_of[8], part), 9)
    return {
        "wave_now": draw_wave_now(jax.random.fold_in(jax.random.fold_in(streams_of[8], part), 71), part),
        "wave_before": draw_wave_before(jax.random.fold_in(jax.random.fold_in(streams_of[8], part), 71), part),
        "courant": jnp.clip(jnp.exp(math.log(0.15) - 1.609438 * jax.random.uniform(part_splits[2], (NZ, NX, NY), jnp.float32) ** shard_levels(part_splits[2], (NZ, NX, NY), ((1, 4), (2, 4)), -0.2, 0.2)), 0.03, 0.15),
        "records": heavy_noise(part_splits[3], (SHOTS, 2, RECV), 0.1, 0.59765625, ((0, 16),), (0, 2, 16, 2.0)),
        "signs": draw_signs(jax.random.fold_in(jax.random.fold_in(streams_of[8], part), 71), part),
        "source_x": draw_source_x(jax.random.fold_in(jax.random.fold_in(streams_of[8], part), 71), part),
        "source_y": draw_source_y(jax.random.fold_in(jax.random.fold_in(streams_of[8], part), 71), part),
        "receiver_cell": draw_receiver_cell(jax.random.fold_in(jax.random.fold_in(streams_of[8], part), 71), part),
    }


coef_zero = -205.0 / 72.0
coef_rest = (8.0 / 5.0, -1.0 / 5.0, 8.0 / 315.0, -1.0 / 560.0)


def laplace(ext, margin):
    depth = ext.shape[1]
    wide_x = ext.shape[2] - 2 * margin
    wide_y = ext.shape[3] - 2 * margin
    padded = jnp.pad(ext, ((0, 0), (4, 4), (0, 0), (0, 0)))
    center = ext[:, :, margin:margin + wide_x, margin:margin + wide_y]
    total = 3.0 * coef_zero * center
    for step in range(1, 5):
        near = padded[:, 4 + step:4 + step + depth, margin:margin + wide_x, margin:margin + wide_y]
        near = near + padded[:, 4 - step:4 - step + depth, margin:margin + wide_x, margin:margin + wide_y]
        near = near + ext[:, :, margin + step:margin + step + wide_x, margin:margin + wide_y]
        near = near + ext[:, :, margin - step:margin - step + wide_x, margin:margin + wide_y]
        near = near + ext[:, :, margin:margin + wide_x, margin + step:margin + step + wide_y]
        near = near + ext[:, :, margin:margin + wide_x, margin - step:margin - step + wide_y]
        total = total + coef_rest[step - 1] * near
    return total


def reference(wave_now, wave_before, courant, records, signs, source_x, source_y, receiver_cell):
    tiles = N_GX * N_GY
    owner = jnp.arange(RECV, dtype=jnp.int32) // REC_DEV
    gpos_x = (owner // N_GY) * CX + receiver_cell // CY
    gpos_y = (owner % N_GY) * CY + receiver_cell % CY
    radius_sq = jnp.float32(RADIUS * RADIUS)
    rec_blocks = records.reshape(tiles, SHOT_DEV, 2, RECV)
    sign_blocks = jnp.transpose(signs.reshape(2, tiles, SHOT_DEV), (1, 0, 2)).astype(jnp.float32)
    sx_blocks = source_x.reshape(tiles, SHOT_DEV)
    sy_blocks = source_y.reshape(tiles, SHOT_DEV)

    def accumulate(carry, block):
        rec, sgn, sxb, syb = block
        dx = (gpos_x[None, :] - sxb[:, None]).astype(jnp.float32)
        dy = (gpos_y[None, :] - syb[:, None]).astype(jnp.float32)
        dist = dx * dx + dy * dy
        taper = dist / (dist + radius_sq)
        taped = rec.astype(jnp.float32) * taper[:, None, :]
        part_sum = jnp.sum(sgn[:, :, None, None] * taped[None], axis=1)
        return carry + part_sum, None

    residual, _ = lax.scan(accumulate, jnp.zeros((2, 2, RECV), jnp.float32), (rec_blocks, sign_blocks, sx_blocks, sy_blocks))
    inject = jnp.zeros((2, 2, NX, NY), jnp.float32).at[:, :, gpos_x, gpos_y].add(residual)

    def advance(current, previous, source):
        ext = jnp.pad(current, ((0, 0), (0, 0), (4, 4), (4, 4)))
        fresh = 2.0 * current - previous + courant * laplace(ext, 4)
        return fresh.at[:, RDEPTH].add(source)

    wave_middle = advance(wave_now, wave_before, inject[:, 0])
    wave_after = advance(wave_middle, wave_now, inject[:, 1])
    return wave_after, wave_middle
```

```python
import functools

import jax
import jax.numpy as jnp
from jax import lax
from jax.experimental import pallas as pl
from jax.experimental.pallas import tpu as pltpu
from jax.sharding import PartitionSpec as P

REC_DEV = 256
RDEPTH = 2
HALO = 4
AXES = ("group", "gx", "gy")

coef_zero = -205.0 / 72.0
coef_rest = (8.0 / 5.0, -1.0 / 5.0, 8.0 / 315.0, -1.0 / 560.0)

VM = pl.BlockSpec(memory_space=pltpu.VMEM)
SM = pl.BlockSpec(memory_space=pltpu.SMEM)


def rows_of(shape):
    return lax.broadcasted_iota(jnp.int32, shape, len(shape) - 2)


def lanes_of(shape):
    return lax.broadcasted_iota(jnp.int32, shape, len(shape) - 1)


def head_rows(first, second):
    return jnp.where(rows_of(first.shape) < HALO, first, pltpu.roll(second, HALO, 0))


def tail_rows(first, second):
    return jnp.where(rows_of(first.shape) < HALO, pltpu.roll(first, HALO, 0), second)


def put_columns(cells, depth, tail_ref, head_ref, field):
    wide = cells.shape[-1]
    per = wide // HALO
    slot, part = lax.rem(depth, per), lax.div(depth, per)
    mine = lanes_of(cells.shape) // HALO == slot
    head = pltpu.roll(cells, slot * HALO, 1)
    tail = pltpu.roll(cells, lax.rem(slot * HALO + HALO, wide), 1)
    head_ref[field, part] = jnp.where(mine, head, head_ref[field, part])
    tail_ref[field, part] = jnp.where(mine, tail, tail_ref[field, part])


def side_columns(next_tile, prev_tile, depth):
    wide = next_tile.shape[-1]
    slot = lax.rem(depth, wide // HALO)
    after = pltpu.roll(next_tile, lax.rem(wide - slot * HALO, wide), 1)
    before = pltpu.roll(prev_tile, wide - HALO - slot * HALO, 1)
    return jnp.where(lanes_of(next_tile.shape) < HALO, after, before)


def shifted_pair(cells, beside, step, axis):
    size = cells.shape[axis]
    place = lax.broadcasted_iota(jnp.int32, cells.shape, axis)
    up = pltpu.roll(jnp.where(place < step, beside, cells), size - step, axis)
    down = pltpu.roll(jnp.where(place >= size - step, beside, cells), step, axis)
    return up + down


def laplace(ref, field, depth, static_depth, deep, beside_x, beside_y):
    cells = ref[field, depth]
    total = 3.0 * coef_zero * cells
    for step in range(1, HALO + 1):
        near = shifted_pair(cells, beside_x, step, 0) + shifted_pair(cells, beside_y, step, 1)
        if static_depth is None or static_depth + step < deep:
            near = near + ref[field, depth + step]
        if static_depth is None or static_depth >= step:
            near = near + ref[field, depth - step]
        total = total + coef_rest[step - 1] * near
    return cells, total


def over_depth(deep, body):
    for depth in range(HALO):
        body(depth, depth)

    def inner(depth, carry):
        body(depth, None)
        return carry

    lax.fori_loop(HALO, deep - HALO, inner, 0, unroll=4)
    for depth in range(deep - HALO, deep):
        body(depth, depth)


def pack_kernel(flag_ref, now_ref, xa_ref, xb_ref, ya_ref, yb_ref, tail_ref, head_ref):
    odd_x, odd_y = flag_ref[0] == 1, flag_ref[1] == 1
    deep = now_ref.shape[1]
    tail_ref[...] = jnp.zeros_like(tail_ref)
    head_ref[...] = jnp.zeros_like(head_ref)

    def body(depth, carry):
        first, second = now_ref[0, depth], now_ref[1, depth]
        head, tail = head_rows(first, second), tail_rows(first, second)
        xa_ref[depth] = jnp.where(odd_x, head, tail)
        xb_ref[depth] = jnp.where(odd_x, tail, head)
        put_columns(first, depth, tail_ref, head_ref, 0)
        put_columns(second, depth, tail_ref, head_ref, 1)
        return carry

    lax.fori_loop(0, deep, body, 0, unroll=4)
    ya_ref[...] = jnp.where(odd_y, head_ref[...], tail_ref[...])
    yb_ref[...] = jnp.where(odd_y, tail_ref[...], head_ref[...])


def residual_kernel(tiles_y, cells_x, cells_y, radius_sq, signs_ref, sx_ref, sy_ref, records_ref, cell_ref, out_ref):
    shots = records_ref.shape[0]
    lanes = cell_ref.shape[1]
    shape = (shots, lanes)
    place = rows_of(shape)
    source_x = jnp.zeros(shape, jnp.int32)
    source_y = jnp.zeros(shape, jnp.int32)
    for shot in range(shots):
        source_x = jnp.where(place == shot, sx_ref[shot], source_x)
        source_y = jnp.where(place == shot, sy_ref[shot], source_y)
    per = REC_DEV // lanes

    def tile_step(tile, carry):
        for part in range(per):
            row = tile * per + part
            cell = jnp.broadcast_to(cell_ref[pl.ds(row, 1), :], shape)
            pos_x = lax.div(tile, tiles_y) * cells_x + lax.shift_right_logical(cell, cells_y.bit_length() - 1)
            pos_y = lax.rem(tile, tiles_y) * cells_y + (cell & (cells_y - 1))
            dx = (pos_x - source_x).astype(jnp.float32)
            dy = (pos_y - source_y).astype(jnp.float32)
            dist = dx * dx + dy * dy
            taper = dist / (dist + radius_sq)
            sums = [jnp.zeros((2, lanes), jnp.float32) for _ in range(2)]
            start = pl.multiple_of(row * lanes, lanes)
            for shot in range(shots):
                taped = records_ref[shot, :, pl.ds(start, lanes)].astype(jnp.float32) * taper[shot : shot + 1, :]
                for code in range(2):
                    sums[code] = sums[code] + signs_ref[code, shot].astype(jnp.float32) * taped
            for code in range(2):
                out_ref[tile, 2 * code : 2 * code + 2, part * lanes : (part + 1) * lanes] = sums[code]
        return carry

    lax.fori_loop(0, out_ref.shape[0], tile_step, 0)


def inject_layers(res, cell_row, cells_x, cells_y):
    count = res.shape[1]
    row = lax.shift_right_logical(cell_row, cells_y.bit_length() - 1)
    column = cell_row & (cells_y - 1)
    in_row = rows_of((cells_x, count)) == row
    spread = jnp.concatenate([jnp.where(in_row, res[q : q + 1], 0.0) for q in range(res.shape[0])], axis=0)
    hot = (rows_of((cells_y, count)) == column).astype(jnp.float32)
    out = lax.dot_general(
        spread, hot, (((1,), (1,)), ((), ())),
        precision=lax.Precision.HIGHEST, preferred_element_type=jnp.float32,
    )
    return out


def sides_x(xa, xb, odd_x, no_next, no_prev):
    after = jnp.where(odd_x, xb, xa)
    before = jnp.where(odd_x, xa, xb)
    after = jnp.where(no_next, 0.0, after)
    before = jnp.where(no_prev, 0.0, before)
    low = rows_of(after.shape) < HALO
    first = jnp.where(low, after, pltpu.roll(before, HALO, 0))
    second = jnp.where(low, pltpu.roll(after, HALO, 0), before)
    return first, second


def middle_kernel(
    flag_ref, now_ref, old_ref, courant_ref, xa_ref, xb_ref, ya_ref, yb_ref, res_ref, cell_ref,
    mid_ref, layer_ref, xa_out, xb_out, ya_out, yb_out, tail_ref, head_ref, ny_ref, py_ref,
):
    odd_x, odd_y = flag_ref[0] == 1, flag_ref[1] == 1
    no_px, no_nx, no_py, no_ny = [flag_ref[i] == 1 for i in range(2, 6)]
    deep, cells_x, cells_y = now_ref.shape[1:]
    ny_ref[...] = jnp.where(no_ny, 0.0, jnp.where(odd_y, yb_ref[...], ya_ref[...]))
    py_ref[...] = jnp.where(no_py, 0.0, jnp.where(odd_y, ya_ref[...], yb_ref[...]))
    tail_ref[...] = jnp.zeros_like(tail_ref)
    head_ref[...] = jnp.zeros_like(head_ref)
    res = res_ref[0]
    for t in range(1, res_ref.shape[0]):
        res = res + res_ref[t]
    layers = inject_layers(res, cell_ref[...], cells_x, cells_y)
    for q in range(4):
        layer_ref[q] = layers[q * cells_x : (q + 1) * cells_x]

    def body(depth, static_depth):
        sides = sides_x(xa_ref[depth], xb_ref[depth], odd_x, no_nx, no_px)
        part = depth // (cells_y // HALO) if static_depth is not None else lax.div(depth, cells_y // HALO)
        fields = []
        for field in range(2):
            beside_y = side_columns(ny_ref[field, part], py_ref[field, part], depth)
            cells, total = laplace(now_ref, field, depth, static_depth, deep, sides[field], beside_y)
            fresh = 2.0 * cells - old_ref[field, depth] + courant_ref[depth] * total
            if static_depth == RDEPTH:
                fresh = fresh + layer_ref[2 * field]
            mid_ref[field, depth] = fresh
            put_columns(fresh, depth, tail_ref, head_ref, field)
            fields.append(fresh)
        head, tail = head_rows(*fields), tail_rows(*fields)
        xa_out[depth] = jnp.where(odd_x, head, tail)
        xb_out[depth] = jnp.where(odd_x, tail, head)

    over_depth(deep, body)
    ya_out[...] = jnp.where(odd_y, head_ref[...], tail_ref[...])
    yb_out[...] = jnp.where(odd_y, tail_ref[...], head_ref[...])


def after_kernel(
    flag_ref, mid_ref, now_ref, courant_ref, xa_ref, xb_ref, ya_ref, yb_ref, layer_ref,
    out_ref, ny_ref, py_ref,
):
    odd_x, odd_y = flag_ref[0] == 1, flag_ref[1] == 1
    no_px, no_nx, no_py, no_ny = [flag_ref[i] == 1 for i in range(2, 6)]
    deep, cells_x, cells_y = now_ref.shape[1:]
    ny_ref[...] = jnp.where(no_ny, 0.0, jnp.where(odd_y, yb_ref[...], ya_ref[...]))
    py_ref[...] = jnp.where(no_py, 0.0, jnp.where(odd_y, ya_ref[...], yb_ref[...]))

    def body(depth, static_depth):
        sides = sides_x(xa_ref[depth], xb_ref[depth], odd_x, no_nx, no_px)
        part = depth // (cells_y // HALO) if static_depth is not None else lax.div(depth, cells_y // HALO)
        for field in range(2):
            beside_y = side_columns(ny_ref[field, part], py_ref[field, part], depth)
            cells, total = laplace(mid_ref, field, depth, static_depth, deep, sides[field], beside_y)
            fresh = 2.0 * cells - now_ref[field, depth] + courant_ref[depth] * total
            if static_depth == RDEPTH:
                fresh = fresh + layer_ref[2 * field + 1]
            out_ref[field, depth] = fresh

    over_depth(deep, body)


def paired(groups, count_x, count_y, partner):
    index = lambda g, x, y: (g * count_x + x) * count_y + y
    return [
        (index(g, x, y), index(*partner(g, x, y)))
        for g in range(groups)
        for x in range(count_x)
        for y in range(count_y)
    ]


def on_device(wave_now, wave_before, courant, records, signs, source_x, source_y, receiver_cell):
    _, deep, cells_x, cells_y = wave_now.shape
    groups, tiles_x, tiles_y = [lax.axis_size(axis) for axis in AXES]
    total_recv = receiver_cell.shape[0]
    tiles = total_recv // REC_DEV
    span = (cells_x * tiles_x + cells_y * tiles_y) // 4
    at_x, at_y = lax.axis_index("gx"), lax.axis_index("gy")
    flags = jnp.stack([
        at_x % 2, at_y % 2,
        (at_x == 0).astype(jnp.int32), (at_x == tiles_x - 1).astype(jnp.int32),
        (at_y == 0).astype(jnp.int32), (at_y == tiles_y - 1).astype(jnp.int32),
    ]).astype(jnp.int32)

    perms = functools.partial(paired, groups, tiles_x, tiles_y)
    swap_xa = perms(lambda g, x, y: (g, x ^ 1, y))
    swap_ya = perms(lambda g, x, y: (g, x, y ^ 1))
    swap_xb = perms(
        lambda g, x, y: ((g + groups // 2) % groups, x, y) if x in (0, tiles_x - 1) else (g, ((x + 1) ^ 1) - 1, y)
    )
    swap_yb = perms(lambda g, x, y: (g, x ^ 1, y) if y in (0, tiles_y - 1) else (g, x, ((y + 1) ^ 1) - 1))

    f32 = jnp.float32
    parts = deep * HALO // cells_y
    face_x = jax.ShapeDtypeStruct((deep, cells_x, cells_y), f32)
    face_y = jax.ShapeDtypeStruct((2, parts, cells_x, cells_y), f32)
    face_scratch = pltpu.VMEM(face_y.shape, f32)

    xa, xb, ya, yb = pl.pallas_call(
        pack_kernel,
        out_shape=(face_x, face_x, face_y, face_y),
        in_specs=[SM, VM],
        out_specs=(VM,) * 4,
        scratch_shapes=[face_scratch] * 2,
        name="pack_now",
    )(flags, wave_now)
    send = lambda value, pairs: lax.ppermute(value, AXES, pairs)
    xb_in, ya_in, yb_in, xa_in = send(xb, swap_xb), send(ya, swap_ya), send(yb, swap_yb), send(xa, swap_xa)

    lanes = 128
    cell_rows = receiver_cell.reshape(total_recv // lanes, lanes)
    partial_res = pl.pallas_call(
        functools.partial(residual_kernel, tiles_y, cells_x, cells_y, float(span * span)),
        out_shape=jax.ShapeDtypeStruct((tiles, 4, REC_DEV), f32),
        in_specs=[SM, SM, SM, VM, VM],
        out_specs=VM,
        name="residual",
    )(signs, source_x, source_y, records, cell_rows)
    res_in = lax.all_to_all(partial_res, ("gx", "gy"), 0, 0, tiled=True)
    tile = at_x * tiles_y + at_y
    own_cells = lax.dynamic_slice_in_dim(receiver_cell, tile * REC_DEV, REC_DEV, 0).reshape(1, REC_DEV)

    wave = jax.ShapeDtypeStruct(wave_now.shape, f32)
    wave_middle, layers, xa, xb, ya, yb = pl.pallas_call(
        middle_kernel,
        out_shape=(wave, jax.ShapeDtypeStruct((4, cells_x, cells_y), f32), face_x, face_x, face_y, face_y),
        in_specs=[SM] + [VM] * 9,
        out_specs=(VM,) * 6,
        scratch_shapes=[face_scratch] * 4,
        name="middle",
    )(flags, wave_now, wave_before, courant, xa_in, xb_in, ya_in, yb_in, res_in, own_cells)
    xb_in, ya_in, yb_in, xa_in = send(xb, swap_xb), send(ya, swap_ya), send(yb, swap_yb), send(xa, swap_xa)
    wave_after = pl.pallas_call(
        after_kernel,
        out_shape=wave,
        in_specs=[SM] + [VM] * 8,
        out_specs=VM,
        scratch_shapes=[face_scratch] * 2,
        name="after",
    )(flags, wave_middle, wave_now, courant, xa_in, xb_in, ya_in, yb_in, layers)
    return (wave_after, wave_middle)


def solution(mesh):
    return jax.shard_map(
        on_device,
        mesh=mesh,
        in_specs=(
            P("group", None, "gx", "gy"),
            P("group", None, "gx", "gy"),
            P("group", "gx", "gy"),
            P(("group", "gx", "gy"), None, None),
            P("group", ("gx", "gy")),
            P(("group", "gx", "gy")),
            P(("group", "gx", "gy")),
            P("group"),
        ),
        out_specs=(P("group", None, "gx", "gy"), P("group", None, "gx", "gy")),
        check_vma=False,
    )
```

```python
import functools

import jax
import jax.numpy as jnp
import ml_dtypes
import numpy as np
from jax import lax
from jax.experimental import pallas as pl
from jax.experimental.pallas import tpu as pltpu
from jax.sharding import PartitionSpec as P

REC_DEV = 256
RDEPTH = 2
HALO = 4
LANES = 128
SUB = 8
GROUP = 16
AXES = ("group", "gx", "gy")
F32, BF16 = jnp.float32, jnp.bfloat16

coef_zero = -205.0 / 72.0
coef_rest = (8.0 / 5.0, -1.0 / 5.0, 8.0 / 315.0, -1.0 / 560.0)
coef_high = [float(np.float32(c).astype(ml_dtypes.bfloat16)) for c in coef_rest]
coef_low = [float(np.float32(c - h).astype(ml_dtypes.bfloat16)) for c, h in zip(coef_rest, coef_high)]

VM = pl.BlockSpec(memory_space=pltpu.VMEM)
SM = pl.BlockSpec(memory_space=pltpu.SMEM)
PARAMS = pltpu.CompilerParams(vmem_limit_bytes=16 * 1024 * 1024)


def near_memory(value):
    return pltpu.with_memory_space_constraint(value, pltpu.VMEM)


def rows_of(shape):
    return lax.broadcasted_iota(jnp.int32, shape, len(shape) - 2)


def lanes_of(shape):
    return lax.broadcasted_iota(jnp.int32, shape, len(shape) - 1)


def dot(left, right):
    return jnp.dot(left, right, preferred_element_type=F32)


def split(value):
    first = value.astype(BF16)
    rest = value - first.astype(F32)
    second = rest.astype(BF16)
    return first, second, (rest - second.astype(F32)).astype(BF16)


def pick(step, coefs):
    out = jnp.zeros(step.shape, F32)
    for m in range(1, HALO + 1):
        out = jnp.where(step == m, coefs[m - 1], out)
    return out.astype(BF16)


def band(coefs):
    shape = (LANES, LANES)
    return pick(jnp.abs(rows_of(shape) - lanes_of(shape)), coefs)


def side(coefs):
    shape = (LANES, LANES)
    c = rows_of(shape) & 7
    j = lanes_of(shape)
    return pick(jnp.where(c < HALO, LANES + c - j, j + 8 - c), coefs)


def chooser():
    shape = (LANES, LANES)
    c = lanes_of(shape) & 7
    return (rows_of(shape) == jnp.where(c < HALO, c, LANES - 8 + c)).astype(F32).astype(BF16)


def pack_columns(ref, out_ref):
    choose = chooser()
    choose_both = jnp.concatenate([choose, choose], axis=0)
    groups = ref.shape[1] // GROUP

    def step(i, carry):
        field, group = lax.div(i, groups), lax.rem(i, groups)
        cells = ref[field, pl.ds(group * GROUP, GROUP)].reshape(GROUP * SUB, LANES)
        first, second, third = split(cells)
        wide = dot(jnp.concatenate([first, second], axis=1), choose_both) + dot(third, choose)
        lane_group = lanes_of((SUB, LANES)) >> 3
        tile = wide[:SUB]
        for q in range(1, GROUP):
            tile = jnp.where(lane_group == q, wide[q * SUB : (q + 1) * SUB], tile)
        out_ref[field, group] = tile
        return carry

    lax.fori_loop(0, 2 * groups, step, 0, unroll=2)


def sides_y(ya, yb, odd, no_next, no_prev):
    after = jnp.where(no_next, 0.0, jnp.where(odd, yb, ya))
    before = jnp.where(no_prev, 0.0, jnp.where(odd, ya, yb))
    return jnp.where((lanes_of(ya.shape) & 7) < HALO, after, before)


def along_y(ref, ya_ref, yb_ref, place, out_ref):
    high, low, side_high, side_low = band(coef_high), band(coef_low), side(coef_high), side(coef_low)
    high, side_high = [jnp.concatenate([m, m], axis=0) for m in (high, side_high)]
    low = jnp.concatenate([low, side_low], axis=0)
    groups = ref.shape[1] // GROUP
    _, odd, _, _, no_next, no_prev = place

    def step(i, carry):
        field, group = lax.div(i, groups), lax.rem(i, groups)
        cells = ref[field, pl.ds(group * GROUP, GROUP)].reshape(GROUP * SUB, LANES)
        first, second, _ = split(cells)
        beside = sides_y(ya_ref[field, group], yb_ref[field, group], odd, no_next, no_prev)
        lane_group = lanes_of((SUB, LANES)) >> 3
        beside = jnp.concatenate([jnp.where(lane_group == q, beside, 0.0) for q in range(GROUP)], axis=0)
        beside_first, beside_second, _ = split(beside)
        total = dot(jnp.concatenate([first, second], axis=1), high)
        total = total + dot(jnp.concatenate([beside_first, beside_second], axis=1), side_high)
        total = total + dot(jnp.concatenate([first, beside_first], axis=1), low)
        out_ref[field, pl.ds(group * GROUP, GROUP)] = total.reshape(GROUP, SUB, LANES)
        return carry

    lax.fori_loop(0, 2 * groups, step, 0, unroll=2)


def where_am_i(counts):
    at_x, at_y = lax.axis_index("gx"), lax.axis_index("gy")
    return (
        lax.rem(at_x, 2) == 1, lax.rem(at_y, 2) == 1,
        at_x == counts[0] - 1, at_x == 0, at_y == counts[1] - 1, at_y == 0,
    )


def head_rows(first, second):
    return jnp.where(rows_of(first.shape) < HALO, first, pltpu.roll(second, HALO, 0))


def tail_rows(first, second):
    return jnp.where(rows_of(first.shape) < HALO, pltpu.roll(first, HALO, 0), second)


def sides_x(xa, xb, place):
    odd, _, no_next, no_prev, _, _ = place
    after = jnp.where(no_next, 0.0, jnp.where(odd, xb, xa))
    before = jnp.where(no_prev, 0.0, jnp.where(odd, xa, xb))
    low = rows_of(after.shape) < HALO
    return jnp.where(low, after, pltpu.roll(before, HALO, 0)), jnp.where(low, pltpu.roll(after, HALO, 0), before)


def shifted_pair(cells, beside, step):
    row = rows_of(cells.shape)
    up = pltpu.roll(jnp.where(row < step, beside, cells), SUB - step, 0)
    down = pltpu.roll(jnp.where(row >= SUB - step, beside, cells), step, 0)
    return up + down


def laplace(ref, field, depth, static_depth, beside_x, part_y):
    deep = ref.shape[1]
    cells = ref[field, depth]
    total = 3.0 * coef_zero * cells + part_y
    for step in range(1, HALO + 1):
        near = shifted_pair(cells, beside_x, step)
        if static_depth is None or static_depth + step < deep:
            near = near + ref[field, depth + step]
        if static_depth is None or static_depth >= step:
            near = near + ref[field, depth - step]
        total = total + coef_rest[step - 1] * near
    return cells, total


def over_depth(deep, body, after_part=None):
    parts = 4
    size = deep // parts
    for part in range(parts):
        start, stop = part * size, (part + 1) * size
        if part == 0:
            for depth in range(HALO):
                body(depth, depth)
            start = HALO
        if part == parts - 1:
            stop = deep - HALO

        def inner(depth, carry):
            body(depth, None)
            return carry

        lax.fori_loop(start, stop, inner, 0, unroll=4)
        if part == parts - 1:
            for depth in range(deep - HALO, deep):
                body(depth, depth)
        if after_part is not None:
            after_part(part, part * size, size)


def pack_xb_kernel(counts, now_ref, xb_ref):
    odd = where_am_i(counts)[0]

    def body(depth, carry):
        first, second = now_ref[0, depth], now_ref[1, depth]
        xb_ref[depth] = jnp.where(odd, tail_rows(first, second), head_rows(first, second))
        return carry

    lax.fori_loop(0, now_ref.shape[1], body, 0, unroll=8)


def pack_rest_kernel(counts, now_ref, xa_ref, y_ref):
    odd = where_am_i(counts)[0]
    pack_columns(now_ref, y_ref)

    def body(depth, carry):
        first, second = now_ref[0, depth], now_ref[1, depth]
        xa_ref[depth] = jnp.where(odd, head_rows(first, second), tail_rows(first, second))
        return carry

    lax.fori_loop(0, now_ref.shape[1], body, 0, unroll=8)


def residual_kernel(tiles_y, cells_x, cells_y, radius_sq, signs_ref, sx_ref, sy_ref, records_ref, cell_ref, out_ref):
    shots, rows, _ = records_ref.shape
    chunk = min(rows, 64)
    per = 2 * REC_DEV // LANES
    twice = (rows_of((chunk, chunk // 2)) >> 1 == lanes_of((chunk, chunk // 2))).astype(F32).astype(BF16)

    def chunk_step(c, carry):
        cell = cell_ref[pl.ds(pl.multiple_of(c * (chunk // 2), chunk // 2), chunk // 2), :]
        row, column = lax.shift_right_logical(cell, cells_y.bit_length() - 1), cell & (cells_y - 1)
        row, column = [dot(twice, v.astype(F32).astype(BF16)) for v in (row, column)]
        tile = c * (chunk // per) + rows_of((chunk, LANES)) // per
        tile_x, tile_y = tile // tiles_y, tile % tiles_y
        pos_x = (tile_x * cells_x).astype(F32) + row
        pos_y = (tile_y * cells_y).astype(F32) + column
        sums = [jnp.zeros((chunk, LANES), F32) for _ in range(2)]
        start = pl.multiple_of(c * chunk, chunk)
        for shot in range(shots):
            dx = pos_x - sx_ref[shot].astype(F32)
            dy = pos_y - sy_ref[shot].astype(F32)
            dist = dx * dx + dy * dy
            taped = records_ref[shot, pl.ds(start, chunk), :].astype(F32) * (dist / (dist + radius_sq))
            for code in range(2):
                sums[code] = sums[code] + signs_ref[code, shot].astype(F32) * taped
        for t in range(chunk // per):
            both = [s[t * per : (t + 1) * per] for s in sums]
            out_ref[c * (chunk // per) + t] = jnp.concatenate(both, axis=0)
        return carry

    lax.fori_loop(0, rows // chunk, chunk_step, 0)


def inject_layers(res, cells, cells_x, cells_y):
    out = None
    for half in range(REC_DEV // LANES):
        row = lax.shift_right_logical(cells[half], cells_y.bit_length() - 1)
        column = cells[half] & (cells_y - 1)
        in_row = rows_of((cells_x, LANES)) == row
        spread = jnp.concatenate(
            [
                jnp.where(in_row, res[code * 4 + half * 2 + sample][None, :], 0.0)
                for code in range(2)
                for sample in range(2)
            ],
            axis=0,
        )
        hot = (rows_of((cells_y, LANES)) == column).astype(F32).astype(BF16)
        parts = jnp.concatenate(split(spread), axis=0)
        got = lax.dot_general(parts, hot, (((1,), (1,)), ((), ())), preferred_element_type=F32)
        out = got if out is None else out + got
    count = 4 * cells_x
    return out[:count] + out[count : 2 * count] + out[2 * count :]


def middle_kernel(
    counts, now_ref, old_ref, courant_ref, xa_ref, xb_ref, ya_ref, yb_ref, res_ref, cell_ref,
    mid_ref, layer_ref, xa_out, xb_out, y_out, part_y_ref,
):
    place = where_am_i(counts)
    deep, cells_x, cells_y = now_ref.shape[1:]
    along_y(now_ref, ya_ref, yb_ref, place, part_y_ref)
    res = res_ref[0]
    for t in range(1, res_ref.shape[0]):
        res = res + res_ref[t]
    halves = REC_DEV // LANES
    first_row = (lax.axis_index("gx") * counts[1] + lax.axis_index("gy")) * halves
    cells = [cell_ref[pl.ds(first_row + half, 1), :] for half in range(halves)]
    layers = inject_layers(res, cells, cells_x, cells_y)
    for q in range(4):
        layer_ref[q] = layers[q * cells_x : (q + 1) * cells_x]

    def body(depth, static_depth):
        sides = sides_x(xa_ref[depth], xb_ref[depth], place)
        fields = []
        for field in range(2):
            cells, total = laplace(now_ref, field, depth, static_depth, sides[field], part_y_ref[field, depth])
            fresh = 2.0 * cells - old_ref[field, depth] + courant_ref[depth] * total
            if static_depth == RDEPTH:
                fresh = fresh + layer_ref[2 * field]
            mid_ref[field, depth] = fresh
            fields.append(fresh)
        head, tail = head_rows(*fields), tail_rows(*fields)
        xa_out[depth] = jnp.where(place[0], head, tail)
        xb_out[depth] = jnp.where(place[0], tail, head)

    over_depth(deep, body)
    pack_columns(mid_ref, y_out)


def after_kernel(
    counts, mid_ref, now_ref, courant_ref, xa_ref, xb_ref, ya_ref, yb_ref, layer_ref,
    out_ref, part_y_ref, held_ref, sems,
):
    place = where_am_i(counts)
    deep = now_ref.shape[1]
    along_y(mid_ref, ya_ref, yb_ref, place, part_y_ref)

    def body(depth, static_depth):
        sides = sides_x(xa_ref[depth], xb_ref[depth], place)
        for field in range(2):
            cells, total = laplace(mid_ref, field, depth, static_depth, sides[field], part_y_ref[field, depth])
            fresh = 2.0 * cells - now_ref[field, depth] + courant_ref[depth] * total
            if static_depth == RDEPTH:
                fresh = fresh + layer_ref[2 * field + 1]
            held_ref[field, depth] = fresh

    copies = []

    def send_out(part, start, size):
        copy = pltpu.make_async_copy(
            held_ref.at[:, pl.ds(start, size)], out_ref.at[:, pl.ds(start, size)], sems.at[part]
        )
        copy.start()
        copies.append(copy)

    over_depth(deep, body, send_out)
    for copy in copies:
        copy.wait()


def paired(groups, count_x, count_y, partner):
    index = lambda g, x, y: (g * count_x + x) * count_y + y
    return [
        (index(g, x, y), index(*partner(g, x, y)))
        for g in range(groups)
        for x in range(count_x)
        for y in range(count_y)
    ]


def on_device(wave_now, wave_before, courant, records, signs, source_x, source_y, receiver_cell):
    _, deep, cells_x, cells_y = wave_now.shape
    groups, tiles_x, tiles_y = [lax.axis_size(axis) for axis in AXES]
    counts = (tiles_x, tiles_y)
    total_recv = receiver_cell.shape[0]
    tiles = total_recv // REC_DEV
    shots = records.shape[0]
    span = (cells_x * tiles_x + cells_y * tiles_y) // 4

    perms = functools.partial(paired, groups, tiles_x, tiles_y)
    swap_xa = perms(lambda g, x, y: (g, x ^ 1, y))
    swap_ya = perms(lambda g, x, y: (g, x, y ^ 1))
    swap_xb = perms(
        lambda g, x, y: ((g + groups // 2) % groups, x, y) if x in (0, tiles_x - 1) else (g, ((x + 1) ^ 1) - 1, y)
    )
    swap_yb = perms(lambda g, x, y: (g, x ^ 1, y) if y in (0, tiles_y - 1) else (g, x, ((y + 1) ^ 1) - 1))
    send = lambda value, pairs: lax.ppermute(value, AXES, pairs)

    face_x = pltpu.VMEM((deep, cells_x, cells_y), F32)
    face_y = pltpu.VMEM((2, deep // GROUP, cells_x, cells_y), F32)
    wave = wave_now.shape

    def kernel(body, outs, n_scalar, n_array, scratch=(), out_specs=None):
        name = body.__name__.removesuffix("_kernel")

        def call(*args):
            args = args[:n_scalar] + tuple(near_memory(a) for a in args[n_scalar:])
            return pl.pallas_call(
                functools.partial(body, counts),
                out_shape=outs,
                in_specs=[SM] * n_scalar + [VM] * n_array,
                out_specs=out_specs if out_specs is not None else jax.tree.map(lambda _: VM, outs),
                scratch_shapes=scratch,
                compiler_params=PARAMS,
                name=name,
            )(*args)

        return call

    xb = kernel(pack_xb_kernel, face_x, 0, 1)(wave_now)
    xb_in = send(xb, swap_xb)
    xa, y_face = kernel(pack_rest_kernel, (face_x, face_y), 0, 1)(wave_now)
    ya_in, yb_in, xa_in = send(y_face, swap_ya), send(y_face, swap_yb), send(xa, swap_xa)

    cell_rows = receiver_cell.reshape(total_recv // LANES, LANES)
    record_rows = records.reshape(shots, 2, total_recv // LANES, LANES).transpose(0, 2, 1, 3)
    record_rows = record_rows.reshape(shots, 2 * total_recv // LANES, LANES)
    partial_res = pl.pallas_call(
        functools.partial(residual_kernel, tiles_y, cells_x, cells_y, float(span * span)),
        out_shape=pltpu.VMEM((tiles, SUB, LANES), F32),
        in_specs=[SM, SM, SM, VM, VM],
        out_specs=VM,
        compiler_params=PARAMS,
        name="residual",
    )(signs, source_x, source_y, near_memory(record_rows), near_memory(cell_rows))
    res_in = lax.all_to_all(partial_res, ("gx", "gy"), 0, 0, tiled=True)

    part_y = pltpu.VMEM(wave, F32)
    wave_middle, layers, xa, xb, y_face = kernel(
        middle_kernel,
        (pltpu.VMEM(wave, F32), pltpu.VMEM((4, cells_x, cells_y), F32), face_x, face_x, face_y),
        0, 9, [part_y],
    )(wave_now, wave_before, courant, xa_in, xb_in, ya_in, yb_in, res_in, cell_rows)
    xb_in, ya_in, yb_in, xa_in = send(xb, swap_xb), send(y_face, swap_ya), send(y_face, swap_yb), send(xa, swap_xa)
    wave_after = kernel(
        after_kernel, jax.ShapeDtypeStruct(wave, F32), 0, 8,
        [part_y, part_y, pltpu.SemaphoreType.DMA((4,))],
        out_specs=pl.BlockSpec(memory_space=pl.ANY),
    )(wave_middle, wave_now, courant, xa_in, xb_in, ya_in, yb_in, layers)
    return (wave_after, wave_middle)


def solution(mesh):
    return jax.shard_map(
        on_device,
        mesh=mesh,
        in_specs=(
            P("group", None, "gx", "gy"),
            P("group", None, "gx", "gy"),
            P("group", "gx", "gy"),
            P(("group", "gx", "gy"), None, None),
            P("group", ("gx", "gy")),
            P(("group", "gx", "gy")),
            P(("group", "gx", "gy")),
            P("group"),
        ),
        out_specs=(P("group", None, "gx", "gy"), P("group", None, "gx", "gy")),
        check_vma=False,
    )
```

```python
import functools

import jax
import jax.numpy as jnp
import ml_dtypes
import numpy as np
from jax import lax
from jax.experimental import pallas as pl
from jax.experimental.pallas import tpu as pltpu
from jax.sharding import PartitionSpec as P

REC_DEV = 256
RDEPTH = 2
HALO = 4
LANES = 128
SUB = 8
GROUP = 16
AXES = ("group", "gx", "gy")
F32, BF16 = jnp.float32, jnp.bfloat16

coef_zero = -205.0 / 72.0
coef_rest = (8.0 / 5.0, -1.0 / 5.0, 8.0 / 315.0, -1.0 / 560.0)
coef_high = [float(np.float32(c).astype(ml_dtypes.bfloat16)) for c in coef_rest]
coef_low = [float(np.float32(c - h).astype(ml_dtypes.bfloat16)) for c, h in zip(coef_rest, coef_high)]

VM = pl.BlockSpec(memory_space=pltpu.VMEM)
SM = pl.BlockSpec(memory_space=pltpu.SMEM)
PARAMS = pltpu.CompilerParams(vmem_limit_bytes=16 * 1024 * 1024)


def near_memory(value):
    return pltpu.with_memory_space_constraint(value, pltpu.VMEM)


def rows_of(shape):
    return lax.broadcasted_iota(jnp.int32, shape, len(shape) - 2)


def lanes_of(shape):
    return lax.broadcasted_iota(jnp.int32, shape, len(shape) - 1)


def dot(left, right):
    return jnp.dot(left, right, preferred_element_type=F32)


def split(value):
    first = value.astype(BF16)
    rest = value - first.astype(F32)
    second = rest.astype(BF16)
    return first, second, (rest - second.astype(F32)).astype(BF16)


def pick(step, coefs):
    out = jnp.zeros(step.shape, F32)
    for m in range(1, HALO + 1):
        out = jnp.where(step == m, coefs[m - 1], out)
    return out.astype(BF16)


def band(coefs):
    shape = (LANES, LANES)
    return pick(jnp.abs(rows_of(shape) - lanes_of(shape)), coefs)


def side(coefs):
    shape = (LANES, LANES)
    c = rows_of(shape) & 7
    j = lanes_of(shape)
    return pick(jnp.where(c < HALO, j + HALO - c, LANES + c - HALO - j), coefs)


def pack_columns(ref, odd, ya_ref, yb_ref):
    lane_group = lanes_of((SUB, LANES)) >> 3
    low = (lanes_of((SUB, LANES)) & 7) < HALO
    pairs = ref.shape[1] // GROUP // 2

    def step(pair, carry):
        for field in range(2):
            both = []
            for group in range(2):
                tile = None
                for q in range(GROUP):
                    cells = ref[field, (pair * 2 + group) * GROUP + q]
                    turned = pltpu.roll(cells, (q * 2 * HALO + HALO) % LANES, 1)
                    tile = turned if tile is None else jnp.where(lane_group == q, turned, tile)
                both.append(tile)
            last = jnp.where(low, both[0], pltpu.roll(both[1], HALO, 1))
            first = jnp.where(low, pltpu.roll(both[0], LANES - HALO, 1), both[1])
            ya_ref[field * pairs + pair] = jnp.where(odd, first, last)
            yb_ref[field * pairs + pair] = jnp.where(odd, last, first)
        return carry

    lax.fori_loop(0, pairs, step, 0)


def sides_y(ya, yb, odd, no_next, no_prev):
    after = jnp.where(no_next, 0.0, jnp.where(odd, yb, ya))
    before = jnp.where(no_prev, 0.0, jnp.where(odd, ya, yb))
    low = (lanes_of(ya.shape) & 7) < HALO
    return (
        jnp.where(low, before, pltpu.roll(after, HALO, 1)),
        jnp.where(low, pltpu.roll(before, LANES - HALO, 1), after),
    )


def local_y(cells, high, low):
    first, second, _ = split(cells)
    return dot(jnp.concatenate([first, second, first], axis=1), jnp.concatenate([high, high, low], axis=0))


def halo_y(ya_ref, yb_ref, place, out_ref):
    high, low = side(coef_high), side(coef_low)
    weights = jnp.concatenate([high, high, low], axis=0)
    _, odd, _, _, no_next, no_prev = place
    groups = out_ref.shape[1] // GROUP
    lane_group = lanes_of((SUB, LANES)) >> 3
    for field in range(2):
        firsts, seconds = [], []
        for pair in range(groups // 2):
            at = field * (groups // 2) + pair
            for beside in sides_y(ya_ref[at], yb_ref[at], odd, no_next, no_prev):
                first = beside.astype(BF16).astype(F32)
                second = beside - first
                firsts += [jnp.where(lane_group == q, first, 0.0) for q in range(GROUP)]
                seconds += [jnp.where(lane_group == q, second, 0.0) for q in range(GROUP)]
        first, second = [jnp.concatenate(v, axis=0).astype(BF16) for v in (firsts, seconds)]
        total = dot(jnp.concatenate([first, second, first], axis=1), weights)
        out_ref[field] = total.reshape(groups * GROUP, SUB, LANES)


def where_am_i(counts):
    at_x, at_y = lax.axis_index("gx"), lax.axis_index("gy")
    return (
        lax.rem(at_x, 2) == 1, lax.rem(at_y, 2) == 1,
        at_x == counts[0] - 1, at_x == 0, at_y == counts[1] - 1, at_y == 0,
    )


def head_rows(first, second):
    return jnp.where(rows_of(first.shape) < HALO, first, pltpu.roll(second, HALO, 0))


def tail_rows(first, second):
    return jnp.where(rows_of(first.shape) < HALO, pltpu.roll(first, HALO, 0), second)


def sides_x(xa, xb, place):
    odd, _, no_next, no_prev, _, _ = place
    after = jnp.where(no_next, 0.0, jnp.where(odd, xb, xa))
    before = jnp.where(no_prev, 0.0, jnp.where(odd, xa, xb))
    low = rows_of(after.shape) < HALO
    return jnp.where(low, after, pltpu.roll(before, HALO, 0)), jnp.where(low, pltpu.roll(after, HALO, 0), before)


def turns(kept):
    row = rows_of((SUB, LANES))
    out = []
    for turn in range(1, SUB):
        coef = coef_rest[min(turn, SUB - turn) - 1]
        inside = row >= turn if turn < HALO else row < turn if turn > HALO else row >= 0
        out.append(jnp.where(inside if kept else jnp.logical_not(inside) | (turn == HALO), coef, 0.0))
    return out


def along_x(cells, coefs):
    total = coefs[0] * pltpu.roll(cells, 1, 0)
    for turn in range(2, SUB):
        total = total + coefs[turn - 1] * pltpu.roll(cells, turn, 0)
    return total


def local_step(now_ref, old_ref, courant_ref, out_ref):
    deep = now_ref.shape[1]
    high, low = band(coef_high), band(coef_low)
    for field in range(2):
        cells = now_ref[field].reshape(deep * SUB, LANES)
        out_ref[field] = local_y(cells, high, low).reshape(deep, SUB, LANES)
    coefs = turns(True)

    def body(depth, static_depth):
        for field in range(2):
            cells = now_ref[field, depth]
            total = 3.0 * coef_zero * cells + out_ref[field, depth] + along_x(cells, coefs)
            for step in range(1, HALO + 1):
                near = None
                if static_depth is None or static_depth + step < deep:
                    near = now_ref[field, depth + step]
                if static_depth is None or static_depth >= step:
                    before = now_ref[field, depth - step]
                    near = before if near is None else near + before
                total = total + coef_rest[step - 1] * near
            out_ref[field, depth] = 2.0 * cells - old_ref[field, depth] + courant_ref[depth] * total

    over_depth(deep, body)


def halo_step(depth, base_ref, courant_ref, xa_ref, xb_ref, part_y_ref, place, coefs):
    sides = sides_x(xa_ref[depth], xb_ref[depth], place)
    return [
        base_ref[field, depth] + courant_ref[depth] * (part_y_ref[field, depth] + along_x(sides[field], coefs))
        for field in range(2)
    ]


def over_depth(deep, body):
    def inner(depth, carry):
        body(depth, None)
        return carry

    for depth in range(HALO):
        body(depth, depth)
    lax.fori_loop(HALO, deep - HALO, inner, 0, unroll=4)
    for depth in range(deep - HALO, deep):
        body(depth, depth)


def residual(counts, cells_x, cells_y, radius_sq, signs_ref, sx_ref, sy_ref, records_ref, cell_ref, out_ref, first):
    shots, rows, _ = records_ref.shape
    chunk = min(rows, 64)
    per = 2 * REC_DEV // LANES
    twice = (rows_of((chunk, chunk // 2)) >> 1 == lanes_of((chunk, chunk // 2))).astype(F32).astype(BF16)

    def chunk_step(c, carry):
        cell = cell_ref[pl.ds(pl.multiple_of(c * (chunk // 2), chunk // 2), chunk // 2), :]
        row, column = lax.shift_right_logical(cell, cells_y.bit_length() - 1), cell & (cells_y - 1)
        row, column = [dot(twice, v.astype(F32).astype(BF16)) for v in (row, column)]
        tile = c * (chunk // per) + rows_of((chunk, LANES)) // per
        tile_x, tile_y = tile // counts[1], tile % counts[1]
        pos_x = (tile_x * cells_x).astype(F32) + row
        pos_y = (tile_y * cells_y).astype(F32) + column
        start = pl.multiple_of(c * chunk, chunk)

        def shot_step(shot, sums):
            dx = pos_x - sx_ref[shot].astype(F32)
            dy = pos_y - sy_ref[shot].astype(F32)
            dist = dx * dx + dy * dy
            whole = dist + radius_sq
            inverse = pl.reciprocal(whole, approx=True)
            inverse = inverse * (2.0 - whole * inverse)
            taped = records_ref[shot, pl.ds(start, chunk), :].astype(F32) * (dist * inverse)
            return tuple(s + signs_ref[code, shot].astype(F32) * taped for code, s in enumerate(sums))

        sums = lax.fori_loop(0, shots, shot_step, (jnp.zeros((chunk, LANES), F32),) * 2, unroll=2)
        for t in range(chunk // per):
            both = [s[t * per : (t + 1) * per] for s in sums]
            out_ref[first + c * (chunk // per) + t] = jnp.concatenate(both, axis=0)
        return carry

    lax.fori_loop(0, rows // chunk, chunk_step, 0)


def prepare_kernel(
    radius_sq, counts, signs_hbm, sx_hbm, sy_hbm, records_hbm, cell_hbm, now_hbm,
    now_ref, cell_ref, xb_ref, xa_ref, ya_ref, yb_ref, records_ref, signs_ref, sx_ref, sy_ref, sems,
):
    odd, odd_y = where_am_i(counts)[:2]
    deep, cells_x, cells_y = now_ref.shape[1:]
    shots = records_ref.shape[0]
    pieces = 4
    copies = []

    def bring(source, target):
        copy = pltpu.make_async_copy(source, target, sems.at[len(copies)])
        copy.start()
        copies.append(copy)

    for piece in range(pieces):
        depths = pl.ds(piece * (deep // pieces), deep // pieces)
        bring(now_hbm.at[:, depths], now_ref.at[:, depths])
    for source, target in ((cell_hbm, cell_ref), (signs_hbm, signs_ref), (sx_hbm, sx_ref), (sy_hbm, sy_ref)):
        bring(source, target)
    for piece in range(pieces):
        some = pl.ds(piece * (shots // pieces), shots // pieces)
        bring(records_hbm.at[some], records_ref.at[some])

    def body(depth, carry):
        first, second = now_ref[0, depth], now_ref[1, depth]
        head, tail = head_rows(first, second), tail_rows(first, second)
        xb_ref[depth] = jnp.where(odd, tail, head)
        xa_ref[depth] = jnp.where(odd, head, tail)
        return carry

    for piece in range(pieces):
        copies[piece].wait()
        lax.fori_loop(piece * (deep // pieces), (piece + 1) * (deep // pieces), body, 0, unroll=4)
    pack_columns(now_ref, odd_y, ya_ref, yb_ref)
    for copy in copies[pieces:]:
        copy.wait()
    residual(counts, cells_x, cells_y, radius_sq, signs_ref, sx_ref, sy_ref, records_ref, cell_ref, xa_ref, deep)


def needed_tiles(counts, x, y):
    return (
        (x, y),
        (jnp.minimum(x + 1, counts[0] - 1), y), (jnp.maximum(x - 1, 0), y),
        (x, jnp.minimum(y + 1, counts[1] - 1)), (x, jnp.maximum(y - 1, 0)),
    )


def inject(pieces, samples, cells_y):
    values, hots = [], []
    for res, cells, row_kept, column_kept in pieces:
        for half in range(REC_DEV // LANES):
            row = lax.shift_right_logical(cells[half], cells_y.bit_length() - 1)
            column = cells[half] & (cells_y - 1)
            in_row = (rows_of((SUB, LANES)) == row) & row_kept(rows_of((SUB, LANES)))
            values.append(jnp.concatenate(
                [
                    jnp.where(in_row, res[code * 4 + half * 2 + sample][None, :], 0.0)
                    for code in range(2)
                    for sample in range(samples)
                ],
                axis=0,
            ))
            at = rows_of((cells_y, LANES))
            hots.append(((at == column) & column_kept(at)).astype(F32).astype(BF16))
    values = jnp.concatenate(split(jnp.concatenate(values, axis=1)), axis=0)
    got = lax.dot_general(
        values, jnp.concatenate(hots, axis=1), (((1,), (1,)), ((), ())), preferred_element_type=F32
    )
    count = 2 * samples * SUB
    return got[:count] + got[count : 2 * count] + got[2 * count :]


def local_kernel(counts, now_ref, old_ref, courant_ref, out_ref):
    local_step(now_ref, old_ref, courant_ref, out_ref)


def packed_sizes(counts):
    return counts[0] * counts[1] // 2, counts[0] * counts[1] // 8


def pack_samples(first, second):
    even = rows_of((SUB, LANES)) % 2 == 0
    return (
        jnp.where(even, first, pltpu.roll(second, 1, 0)),
        jnp.where(even, pltpu.roll(first, SUB - 1, 0), second),
    )


def join_kernel(counts, face_ref, own_ref, other_ref, out_ref, keep_ref):
    faces, at = face_ref.shape[0], own_ref.shape[0] - counts[0] * counts[1]
    out_ref[:faces] = face_ref[...]
    total = lambda x, y: own_ref[at + x * counts[1] + y] + other_ref[at + x * counts[1] + y]
    here = faces
    for high in range(0, counts[0], 4):
        for x in range(high, high + 2):
            for y in range(counts[1]):
                out_ref[here] = pack_samples(total(x, y), total(x + 2, y))[0]
                here += 1
    odd_x, odd_y = [lax.rem(lax.axis_index(axis), 2) for axis in AXES[1:]]
    i = 0
    for high in range(0, counts[0], 4):
        for y in range(0, counts[1], 2):
            x = high + odd_x
            out_ref[here + i] = pack_samples(total(x, y + 1 - odd_y), total(x + 2, y + 1 - odd_y))[1]
            keep_ref[i] = pack_samples(total(x, y + odd_y), total(x + 2, y + odd_y))[1]
            i += 1


def sum_kernel(counts, own_ref, keep_ref, other_ref, before_ref, more_ref, out_ref):
    del before_ref, more_ref
    firsts, seconds = packed_sizes(counts)
    at, at_other = [ref.shape[0] - firsts - seconds for ref in (own_ref, other_ref)]
    out_ref[:firsts] = own_ref[pl.ds(at, firsts)] + other_ref[pl.ds(at_other, firsts)]
    at_keep = keep_ref.shape[0] - seconds
    out_ref[firsts:] = keep_ref[pl.ds(at_keep, seconds)] + other_ref[pl.ds(at_other + firsts, seconds)]


def needed_kernel(counts, own_ref, other_ref, face_ref, out_ref, keep_ref, face_out):
    del face_ref, face_out
    firsts, _ = packed_sizes(counts)
    at_x, at_y = lax.axis_index("gx"), lax.axis_index("gy")
    half = counts[1] // 2
    even = rows_of((SUB, LANES)) % 2 == 0
    total = lambda i: own_ref[i] + other_ref[i]

    def collect(target_ref, y_here):
        for i, (x, y) in enumerate(needed_tiles(counts, at_x, y_here)):
            second_of_pair = lax.rem(lax.div(x, 2), 2) == 1
            got = total((lax.div(x, 4) * 2 + lax.rem(x, 2)) * counts[1] + y)
            got = jnp.where(second_of_pair, pltpu.roll(got, SUB - 1, 0), got)
            if i == 0:
                more = total(firsts + lax.div(x, 4) * half + lax.div(y, 2))
                got = jnp.where(even, got, jnp.where(second_of_pair, more, pltpu.roll(more, 1, 0)))
            target_ref[i] = got

    collect(out_ref, lax.rem(at_y + half, counts[1]))
    collect(keep_ref, at_y)


def middle_kernel(
    counts, base_ref, courant_ref, xa_ref, xb_ref, ya_ref, yb_ref,
    mid_ref, xa_out, xb_out, ya_out, yb_out, part_y_ref,
):
    place = where_am_i(counts)
    deep = base_ref.shape[1]
    halo_y(ya_ref, yb_ref, place, part_y_ref)
    coefs = turns(False)

    def body(depth, carry):
        fields = halo_step(depth, base_ref, courant_ref, xa_ref, xb_ref, part_y_ref, place, coefs)
        for field in range(2):
            mid_ref[field, depth] = fields[field]
        head, tail = head_rows(*fields), tail_rows(*fields)
        xa_out[depth] = jnp.where(place[0], head, tail)
        xb_out[depth] = jnp.where(place[0], tail, head)
        return carry

    lax.fori_loop(0, deep, body, 0, unroll=4)
    pack_columns(mid_ref, place[1], ya_out, yb_out)


def inject_kernel(counts, keep_ref, res_ref, cell_ref, courant_ref, layer_ref):
    _, _, no_next_x, no_prev_x, no_next_y, no_prev_y = where_am_i(counts)
    _, cells_x, cells_y = courant_ref.shape
    tiles = needed_tiles(counts, lax.axis_index("gx"), lax.axis_index("gy"))
    halves = REC_DEV // LANES
    res = [keep_ref[i] + res_ref[i] for i in range(len(tiles))]
    for i, absent in enumerate((no_next_x, no_prev_x, no_next_y, no_prev_y)):
        res[i + 1] = jnp.where(absent, 0.0, res[i + 1])
    cells = [
        [cell_ref[pl.ds((x * counts[1] + y) * halves + half, 1), :] for half in range(halves)] for x, y in tiles
    ]
    every = lambda at: at >= 0
    own = inject([(res[0], cells[0], every, every)], 2, cells_y)
    beside_x = inject(
        [(res[1], cells[1], lambda at: at < HALO, every), (res[2], cells[2], lambda at: at >= SUB - HALO, every)],
        1, cells_y,
    )
    beside_y = inject(
        [(res[3], cells[3], every, lambda at: at < HALO), (res[4], cells[4], every, lambda at: at >= cells_y - HALO)],
        1, cells_y,
    )
    kept, beside = turns(True), turns(False)
    lane = lanes_of((cells_x, cells_y))
    for field in range(2):
        layer = own[2 * field * cells_x : (2 * field + 1) * cells_x]
        side_x, side_y = [v[field * cells_x : (field + 1) * cells_x] for v in (beside_x, beside_y)]
        total = 3.0 * coef_zero * layer + along_x(layer, kept) + along_x(side_x, beside)
        for step in range(1, HALO + 1):
            up = pltpu.roll(jnp.where(lane < step, side_y, layer), cells_y - step, 1)
            down = pltpu.roll(jnp.where(lane >= cells_y - step, side_y, layer), step, 1)
            total = total + coef_rest[step - 1] * (up + down)
        layer_ref[field] = layer
        second = own[(2 * field + 1) * cells_x : (2 * field + 2) * cells_x]
        layer_ref[2 + field] = 2.0 * layer + courant_ref[RDEPTH] * total + second


def after_kernel(
    counts, base_ref, mid_ref, courant_ref, xa_ref, xb_ref, ya_ref, yb_ref, layer_ref,
    out_ref, mid_out, part_y_ref, held_ref, plane_ref, sems,
):
    place = where_am_i(counts)
    deep = base_ref.shape[1]
    beside = turns(False)
    copies = []

    def send_out(source, target):
        copy = pltpu.make_async_copy(source, target, sems.at[len(copies)])
        copy.start()
        copies.append(copy)

    send_out(mid_ref.at[:, pl.ds(0, RDEPTH)], mid_out.at[:, pl.ds(0, RDEPTH)])
    rest = pl.ds(RDEPTH + 1, deep - RDEPTH - 1)
    send_out(mid_ref.at[:, rest], mid_out.at[:, rest])
    for field in range(2):
        plane_ref[field, 0] = mid_ref[field, RDEPTH] + layer_ref[field]
    plane = pl.ds(RDEPTH, 1)
    send_out(plane_ref, mid_out.at[:, plane])

    halo_y(ya_ref, yb_ref, place, part_y_ref)
    size = deep // 4
    for part in range(4):
        def body(depth, carry):
            fields = halo_step(depth, base_ref, courant_ref, xa_ref, xb_ref, part_y_ref, place, beside)
            for field in range(2):
                held_ref[field, depth] = fields[field]
            return carry

        lax.fori_loop(part * size, (part + 1) * size, body, 0, unroll=4)
        if part == 0:
            for field in range(2):
                held_ref[field, RDEPTH] = held_ref[field, RDEPTH] + layer_ref[2 + field]
                for step in range(1, HALO + 1):
                    change = coef_rest[step - 1] * layer_ref[field]
                    for depth in (RDEPTH - step, RDEPTH + step):
                        if depth >= 0:
                            held_ref[field, depth] = held_ref[field, depth] + courant_ref[depth] * change
        depths = pl.ds(part * size, size)
        send_out(held_ref.at[:, depths], out_ref.at[:, depths])
    for copy in copies:
        copy.wait()


def paired(groups, count_x, count_y, partner):
    index = lambda g, x, y: (g * count_x + x) * count_y + y
    return [
        (index(g, x, y), index(*partner(g, x, y)))
        for g in range(groups)
        for x in range(count_x)
        for y in range(count_y)
    ]


def on_device(wave_now, wave_before, courant, records, signs, source_x, source_y, receiver_cell):
    _, deep, cells_x, cells_y = wave_now.shape
    groups, tiles_x, tiles_y = [lax.axis_size(axis) for axis in AXES]
    counts = (tiles_x, tiles_y)
    total_recv = receiver_cell.shape[0]
    tiles = total_recv // REC_DEV
    shots = records.shape[0]
    span = (cells_x * tiles_x + cells_y * tiles_y) // 4

    perms = functools.partial(paired, groups, tiles_x, tiles_y)
    swap_xa = perms(lambda g, x, y: (g, x ^ 1, y))
    swap_ya = perms(lambda g, x, y: (g, x, y ^ 1))
    swap_xb = perms(
        lambda g, x, y: ((g + groups // 2) % groups, x, y) if x in (0, tiles_x - 1) else (g, ((x + 1) ^ 1) - 1, y)
    )
    swap_yb = perms(lambda g, x, y: (g, x ^ 1, y) if y in (0, tiles_y - 1) else (g, x, ((y + 1) ^ 1) - 1))
    swap_along = {
        "gx": lambda step: perms(lambda g, x, y: (g, x ^ step, y)),
        "gy": lambda step: perms(lambda g, x, y: (g, x, y ^ step)),
    }
    steps = [("gx", 1 << i) for i in range(1, (tiles_x - 1).bit_length())]
    steps += [("gy", 1 << i) for i in range(1, (tiles_y - 1).bit_length() - 1)]
    send = lambda value, pairs: lax.ppermute(value, AXES, pairs)

    face_x = pltpu.VMEM((deep, cells_x, cells_y), F32)
    faces = deep // GROUP
    face_y = pltpu.VMEM((faces, cells_x, cells_y), F32)
    tiles_of = lambda count: pltpu.VMEM((count, SUB, LANES), F32)
    wave = wave_now.shape

    def kernel(body, outs, n_scalar, n_array, scratch=(), out_specs=None, aliases={}):
        name = body.__name__.removesuffix("_kernel")

        def call(*args):
            args = args[:n_scalar] + tuple(near_memory(a) for a in args[n_scalar:])
            return pl.pallas_call(
                functools.partial(body, counts),
                out_shape=outs,
                in_specs=[SM] * n_scalar + [VM] * n_array,
                out_specs=out_specs if out_specs is not None else jax.tree.map(lambda _: VM, outs),
                scratch_shapes=scratch,
                input_output_aliases=aliases,
                compiler_params=PARAMS,
                name=name,
            )(*args)

        return call

    wave_v = pltpu.VMEM(wave, F32)
    cell_rows = receiver_cell.reshape(total_recv // LANES, LANES)
    record_rows = records.reshape(shots, 2, total_recv // LANES, LANES).transpose(0, 2, 1, 3)
    record_rows = record_rows.reshape(shots, 2 * total_recv // LANES, LANES)
    far = lambda value: pltpu.with_memory_space_constraint(value, pltpu.HBM)
    now, cells, xb, xa, ya, yb = pl.pallas_call(
        functools.partial(prepare_kernel, float(span * span), counts),
        out_shape=(wave_v, pltpu.VMEM(cell_rows.shape, jnp.int32), face_x, tiles_of(deep + tiles), face_y, face_y),
        in_specs=[pl.BlockSpec(memory_space=pltpu.HBM)] * 6,
        out_specs=(VM,) * 6,
        scratch_shapes=[
            pltpu.VMEM(record_rows.shape, BF16),
            pltpu.SMEM(signs.shape, jnp.int32), pltpu.SMEM((shots,), jnp.int32), pltpu.SMEM((shots,), jnp.int32),
            pltpu.SemaphoreType.DMA((12,)),
        ],
        compiler_params=PARAMS,
        name="prepare",
    )(*(far(a) for a in (signs, source_x, source_y, record_rows, cell_rows, wave_now)))
    xb_in, xa_in = send(xb, swap_xb), send(xa, swap_xa)
    left = sum(packed_sizes(counts))
    partial_res, keep = kernel(join_kernel, (tiles_of(faces + left), tiles_of(packed_sizes(counts)[1])), 0, 3)(
        ya, xa, xa_in
    )
    ya_in, yb_in = send(partial_res, swap_ya), send(yb, swap_yb)
    other = ya_in
    base = kernel(local_kernel, wave_v, 0, 3)(now, wave_before, courant)
    for axis, step in steps:
        partial_res = kernel(sum_kernel, tiles_of(left), 0, 5)(partial_res, keep, other, base, yb_in)
        keep = partial_res
        other = send(partial_res, swap_along[axis](step))
    wave_middle, xa, xb, ya, yb = kernel(middle_kernel, (wave_v, face_x, face_x, face_y, face_y), 0, 6, [wave_v])(
        base, courant, xa_in, xb_in, ya_in, yb_in
    )
    wanted, keep, xb = kernel(needed_kernel, (tiles_of(5), tiles_of(5), face_x), 0, 3, aliases={2: 2})(
        partial_res, other, xb
    )
    xb_in, xa_in = send(xb, swap_xb), send(xa, swap_xa)
    res_in = send(wanted, swap_along["gy"](tiles_y // 2))
    ya_in, yb_in = send(ya, swap_ya), send(yb, swap_yb)
    base = kernel(local_kernel, wave_v, 0, 3)(wave_middle, now, courant)
    plane = (2, 1, cells_x, cells_y)
    layers = kernel(inject_kernel, tiles_of(4), 0, 4)(keep, res_in, cells, courant)
    wave_after, wave_middle = kernel(
        after_kernel, (jax.ShapeDtypeStruct(wave, F32),) * 2, 0, 8,
        [wave_v, wave_v, pltpu.VMEM(plane, F32), pltpu.SemaphoreType.DMA((7,))],
        out_specs=(pl.BlockSpec(memory_space=pl.ANY),) * 2,
    )(base, wave_middle, courant, xa_in, xb_in, ya_in, yb_in, layers)
    return (wave_after, wave_middle)


def solution(mesh):
    return jax.shard_map(
        on_device,
        mesh=mesh,
        in_specs=(
            P("group", None, "gx", "gy"),
            P("group", None, "gx", "gy"),
            P("group", "gx", "gy"),
            P(("group", "gx", "gy"), None, None),
            P("group", ("gx", "gy")),
            P(("group", "gx", "gy")),
            P(("group", "gx", "gy")),
            P("group"),
        ),
        out_specs=(P("group", None, "gx", "gy"), P("group", None, "gx", "gy")),
        check_vma=False,
    )
```

```python
import functools

import jax
import jax.numpy as jnp
import ml_dtypes
import numpy as np
from jax import lax
from jax.experimental import pallas as pl
from jax.experimental.pallas import tpu as pltpu
from jax.sharding import PartitionSpec as P

REC_DEV = 256
RDEPTH = 2
HALO = 4
LANES = 128
SUB = 8
GROUP = 16
AXES = ("group", "gx", "gy")
F32, BF16 = jnp.float32, jnp.bfloat16

coef_zero = -205.0 / 72.0
coef_rest = (8.0 / 5.0, -1.0 / 5.0, 8.0 / 315.0, -1.0 / 560.0)
coef_high = [float(np.float32(c).astype(ml_dtypes.bfloat16)) for c in coef_rest]
coef_low = [float(np.float32(c - h).astype(ml_dtypes.bfloat16)) for c, h in zip(coef_rest, coef_high)]

VM = pl.BlockSpec(memory_space=pltpu.VMEM)
SM = pl.BlockSpec(memory_space=pltpu.SMEM)
PARAMS = pltpu.CompilerParams(vmem_limit_bytes=16 * 1024 * 1024)


def near_memory(value):
    return pltpu.with_memory_space_constraint(value, pltpu.VMEM)


def rows_of(shape):
    return lax.broadcasted_iota(jnp.int32, shape, len(shape) - 2)


def lanes_of(shape):
    return lax.broadcasted_iota(jnp.int32, shape, len(shape) - 1)


def dot(left, right):
    return jnp.dot(left, right, preferred_element_type=F32)


def split(value):
    first = value.astype(BF16)
    rest = value - first.astype(F32)
    second = rest.astype(BF16)
    return first, second, (rest - second.astype(F32)).astype(BF16)


def pick(step, coefs):
    out = jnp.zeros(step.shape, F32)
    for m in range(1, HALO + 1):
        out = jnp.where(step == m, coefs[m - 1], out)
    return out.astype(BF16)


def band(coefs):
    shape = (LANES, LANES)
    return pick(jnp.abs(rows_of(shape) - lanes_of(shape)), coefs)


def side(coefs):
    shape = (LANES, LANES)
    c = rows_of(shape) & 7
    j = lanes_of(shape)
    return pick(jnp.where(c < HALO, j + HALO - c, LANES + c - HALO - j), coefs)


def pack_columns(ref, odd, ya_ref, yb_ref):
    lane_group = lanes_of((SUB, LANES)) >> 3
    low = (lanes_of((SUB, LANES)) & 7) < HALO
    pairs = ref.shape[1] // GROUP // 2

    def step(pair, carry):
        for field in range(2):
            both = []
            for group in range(2):
                tile = None
                for q in range(GROUP):
                    cells = ref[field, (pair * 2 + group) * GROUP + q]
                    turned = pltpu.roll(cells, (q * 2 * HALO + HALO) % LANES, 1)
                    tile = turned if tile is None else jnp.where(lane_group == q, turned, tile)
                both.append(tile)
            last = jnp.where(low, both[0], pltpu.roll(both[1], HALO, 1))
            first = jnp.where(low, pltpu.roll(both[0], LANES - HALO, 1), both[1])
            ya_ref[field * pairs + pair] = jnp.where(odd, first, last)
            yb_ref[field * pairs + pair] = jnp.where(odd, last, first)
        return carry

    lax.fori_loop(0, pairs, step, 0)


def sides_y(ya, yb, odd, no_next, no_prev):
    after = jnp.where(no_next, 0.0, jnp.where(odd, yb, ya))
    before = jnp.where(no_prev, 0.0, jnp.where(odd, ya, yb))
    low = (lanes_of(ya.shape) & 7) < HALO
    return (
        jnp.where(low, before, pltpu.roll(after, HALO, 1)),
        jnp.where(low, pltpu.roll(before, LANES - HALO, 1), after),
    )


def local_y(cells, high, low):
    first, second, _ = split(cells)
    return dot(jnp.concatenate([first, second, first], axis=1), jnp.concatenate([high, high, low], axis=0))


def halo_y(ya_ref, yb_ref, place, out_ref):
    high, low = side(coef_high), side(coef_low)
    weights = jnp.concatenate([high, high, low], axis=0)
    _, odd, _, _, no_next, no_prev = place
    groups = out_ref.shape[1] // GROUP
    lane_group = lanes_of((SUB, LANES)) >> 3
    for field in range(2):
        firsts, seconds = [], []
        for pair in range(groups // 2):
            at = field * (groups // 2) + pair
            for beside in sides_y(ya_ref[at], yb_ref[at], odd, no_next, no_prev):
                first = beside.astype(BF16).astype(F32)
                second = beside - first
                firsts += [jnp.where(lane_group == q, first, 0.0) for q in range(GROUP)]
                seconds += [jnp.where(lane_group == q, second, 0.0) for q in range(GROUP)]
        first, second = [jnp.concatenate(v, axis=0).astype(BF16) for v in (firsts, seconds)]
        total = dot(jnp.concatenate([first, second, first], axis=1), weights)
        out_ref[field] = total.reshape(groups * GROUP, SUB, LANES)


def where_am_i(counts):
    at_x, at_y = lax.axis_index("gx"), lax.axis_index("gy")
    return (
        lax.rem(at_x, 2) == 1, lax.rem(at_y, 2) == 1,
        at_x == counts[0] - 1, at_x == 0, at_y == counts[1] - 1, at_y == 0,
    )


def head_rows(first, second):
    return jnp.where(rows_of(first.shape) < HALO, first, pltpu.roll(second, HALO, 0))


def tail_rows(first, second):
    return jnp.where(rows_of(first.shape) < HALO, pltpu.roll(first, HALO, 0), second)


def sides_x(xa, xb, place):
    odd, _, no_next, no_prev, _, _ = place
    after = jnp.where(no_next, 0.0, jnp.where(odd, xb, xa))
    before = jnp.where(no_prev, 0.0, jnp.where(odd, xa, xb))
    low = rows_of(after.shape) < HALO
    return jnp.where(low, after, pltpu.roll(before, HALO, 0)), jnp.where(low, pltpu.roll(after, HALO, 0), before)


def turns(kept):
    row = rows_of((SUB, LANES))
    out = []
    for turn in range(1, SUB):
        coef = coef_rest[min(turn, SUB - turn) - 1]
        inside = row >= turn if turn < HALO else row < turn if turn > HALO else row >= 0
        out.append(jnp.where(inside if kept else jnp.logical_not(inside) | (turn == HALO), coef, 0.0))
    return out


def along_x(cells, coefs):
    total = coefs[0] * pltpu.roll(cells, 1, 0)
    for turn in range(2, SUB):
        total = total + coefs[turn - 1] * pltpu.roll(cells, turn, 0)
    return total


def local_step(now_ref, old_ref, courant_ref, out_ref):
    deep = now_ref.shape[1]
    high, low = band(coef_high), band(coef_low)
    for field in range(2):
        cells = now_ref[field].reshape(deep * SUB, LANES)
        out_ref[field] = local_y(cells, high, low).reshape(deep, SUB, LANES)
    coefs = turns(True)

    def body(depth, static_depth):
        for field in range(2):
            cells = now_ref[field, depth]
            total = 3.0 * coef_zero * cells + out_ref[field, depth] + along_x(cells, coefs)
            for step in range(1, HALO + 1):
                near = None
                if static_depth is None or static_depth + step < deep:
                    near = now_ref[field, depth + step]
                if static_depth is None or static_depth >= step:
                    before = now_ref[field, depth - step]
                    near = before if near is None else near + before
                total = total + coef_rest[step - 1] * near
            out_ref[field, depth] = 2.0 * cells - old_ref[field, depth] + courant_ref[depth] * total

    over_depth(deep, body)


def halo_step(depth, base_ref, courant_ref, xa_ref, xb_ref, part_y_ref, place, coefs):
    sides = sides_x(xa_ref[depth], xb_ref[depth], place)
    return [
        base_ref[field, depth] + courant_ref[depth] * (part_y_ref[field, depth] + along_x(sides[field], coefs))
        for field in range(2)
    ]


def over_depth(deep, body):
    def inner(depth, carry):
        body(depth, None)
        return carry

    for depth in range(HALO):
        body(depth, depth)
    lax.fori_loop(HALO, deep - HALO, inner, 0, unroll=4)
    for depth in range(deep - HALO, deep):
        body(depth, depth)


def residual(counts, cells_x, cells_y, radius_sq, signs_ref, sx_ref, sy_ref, records_ref, cell_ref, out_ref):
    shots, rows, _ = records_ref.shape
    chunk = min(rows, 64)
    per = 2 * REC_DEV // LANES
    twice = (rows_of((chunk, chunk // 2)) >> 1 == lanes_of((chunk, chunk // 2))).astype(F32).astype(BF16)

    def chunk_step(c, carry):
        cell = cell_ref[pl.ds(pl.multiple_of(c * (chunk // 2), chunk // 2), chunk // 2), :]
        row, column = lax.shift_right_logical(cell, cells_y.bit_length() - 1), cell & (cells_y - 1)
        row, column = [dot(twice, v.astype(F32).astype(BF16)) for v in (row, column)]
        tile = c * (chunk // per) + rows_of((chunk, LANES)) // per
        tile_x, tile_y = tile // counts[1], tile % counts[1]
        pos_x = (tile_x * cells_x).astype(F32) + row
        pos_y = (tile_y * cells_y).astype(F32) + column
        start = pl.multiple_of(c * chunk, chunk)

        def shot_step(shot, sums):
            dx = pos_x - sx_ref[shot].astype(F32)
            dy = pos_y - sy_ref[shot].astype(F32)
            dist = dx * dx + dy * dy
            whole = dist + radius_sq
            inverse = pl.reciprocal(whole, approx=True)
            inverse = inverse * (2.0 - whole * inverse)
            taped = records_ref[shot, pl.ds(start, chunk), :].astype(F32) * (dist * inverse)
            return tuple(s + signs_ref[code, shot].astype(F32) * taped for code, s in enumerate(sums))

        sums = lax.fori_loop(0, shots, shot_step, (jnp.zeros((chunk, LANES), F32),) * 2, unroll=2)
        for t in range(chunk // per):
            both = [s[t * per : (t + 1) * per] for s in sums]
            out_ref[c * (chunk // per) + t] = jnp.concatenate(both, axis=0)
        return carry

    lax.fori_loop(0, rows // chunk, chunk_step, 0)


def bring_kernel(
    radius_sq, counts, signs_hbm, sx_hbm, sy_hbm, records_hbm, cell_hbm, now_hbm, old_hbm, courant_hbm,
    now_ref, old_ref, courant_ref, cell_ref, res_ref, xa_ref, xb_ref, records_ref, signs_ref, sx_ref, sy_ref, sems,
):
    copies = []

    def bring(source, target):
        copy = pltpu.make_async_copy(source, target, sems.at[len(copies)])
        copy.start()
        copies.append(copy)

    for source, target in (
        (cell_hbm, cell_ref), (signs_hbm, signs_ref), (sx_hbm, sx_ref), (sy_hbm, sy_ref), (records_hbm, records_ref),
        (now_hbm, now_ref), (old_hbm, old_ref), (courant_hbm, courant_ref),
    ):
        bring(source, target)
    for copy in copies[:5]:
        copy.wait()
    _, deep, cells_x, cells_y = now_ref.shape
    residual(counts, cells_x, cells_y, radius_sq, signs_ref, sx_ref, sy_ref, records_ref, cell_ref, res_ref)
    copies[5].wait()
    odd = where_am_i(counts)[0]

    def body(depth, carry):
        first, second = now_ref[0, depth], now_ref[1, depth]
        head, tail = head_rows(first, second), tail_rows(first, second)
        xb_ref[depth] = jnp.where(odd, tail, head)
        xa_ref[depth] = jnp.where(odd, head, tail)
        return carry

    lax.fori_loop(0, deep, body, 0, unroll=4)
    for copy in copies[6:]:
        copy.wait()


def pack_kernel(counts, now_ref, ya_ref, yb_ref):
    pack_columns(now_ref, where_am_i(counts)[1], ya_ref, yb_ref)


def needed_tiles(counts, x, y):
    return (
        (x, y),
        (jnp.minimum(x + 1, counts[0] - 1), y), (jnp.maximum(x - 1, 0), y),
        (x, jnp.minimum(y + 1, counts[1] - 1)), (x, jnp.maximum(y - 1, 0)),
    )


def inject(pieces, samples, cells_y):
    values, hots = [], []
    for res, cells, row_kept, column_kept in pieces:
        for half in range(REC_DEV // LANES):
            row = lax.shift_right_logical(cells[half], cells_y.bit_length() - 1)
            column = cells[half] & (cells_y - 1)
            in_row = (rows_of((SUB, LANES)) == row) & row_kept(rows_of((SUB, LANES)))
            values.append(jnp.concatenate(
                [
                    jnp.where(in_row, res[code * 4 + half * 2 + sample][None, :], 0.0)
                    for code in range(2)
                    for sample in range(samples)
                ],
                axis=0,
            ))
            at = rows_of((cells_y, LANES))
            hots.append(((at == column) & column_kept(at)).astype(F32).astype(BF16))
    values = jnp.concatenate(split(jnp.concatenate(values, axis=1)), axis=0)
    got = lax.dot_general(
        values, jnp.concatenate(hots, axis=1), (((1,), (1,)), ((), ())), preferred_element_type=F32
    )
    count = 2 * samples * SUB
    return got[:count] + got[count : 2 * count] + got[2 * count :]


def second_local_kernel(counts, now_ref, old_ref, courant_ref, before_ref, out_ref):
    del before_ref
    local_step(now_ref, old_ref, courant_ref, out_ref)


def local_kernel(counts, now_ref, old_ref, courant_ref, out_ref):
    local_step(now_ref, old_ref, courant_ref, out_ref)


def packed_sizes(counts):
    return counts[0] * counts[1] // 2, counts[0] * counts[1] // 8


def pack_samples(first, second):
    even = rows_of((SUB, LANES)) % 2 == 0
    return (
        jnp.where(even, first, pltpu.roll(second, 1, 0)),
        jnp.where(even, pltpu.roll(first, SUB - 1, 0), second),
    )


def join_kernel(counts, face_ref, own_ref, other_ref, xa_ref, out_ref, keep_ref, xa_out):
    del xa_ref, xa_out
    faces, at = face_ref.shape[0], own_ref.shape[0] - counts[0] * counts[1]
    out_ref[:faces] = face_ref[...]
    total = lambda x, y: own_ref[at + x * counts[1] + y] + other_ref[at + x * counts[1] + y]
    here = faces
    for high in range(0, counts[0], 4):
        for x in range(high, high + 2):
            for y in range(counts[1]):
                out_ref[here] = pack_samples(total(x, y), total(x + 2, y))[0]
                here += 1
    odd_x, odd_y = [lax.rem(lax.axis_index(axis), 2) for axis in AXES[1:]]
    i = 0
    for high in range(0, counts[0], 4):
        for y in range(0, counts[1], 2):
            x = high + odd_x
            out_ref[here + i] = pack_samples(total(x, y + 1 - odd_y), total(x + 2, y + 1 - odd_y))[1]
            keep_ref[i] = pack_samples(total(x, y + odd_y), total(x + 2, y + odd_y))[1]
            i += 1


def sum_kernel(counts, own_ref, keep_ref, other_ref, before_ref, more_ref, out_ref):
    del before_ref, more_ref
    firsts, seconds = packed_sizes(counts)
    at, at_other = [ref.shape[0] - firsts - seconds for ref in (own_ref, other_ref)]
    out_ref[:firsts] = own_ref[pl.ds(at, firsts)] + other_ref[pl.ds(at_other, firsts)]
    at_keep = keep_ref.shape[0] - seconds
    out_ref[firsts:] = keep_ref[pl.ds(at_keep, seconds)] + other_ref[pl.ds(at_other + firsts, seconds)]


def needed_kernel(counts, own_ref, other_ref, before_ref, ya_ref, yb_ref, out_ref, keep_ref, *handed_on):
    del before_ref, ya_ref, yb_ref, handed_on
    firsts, _ = packed_sizes(counts)
    at_x, at_y = lax.axis_index("gx"), lax.axis_index("gy")
    half = counts[1] // 2
    even = rows_of((SUB, LANES)) % 2 == 0
    total = lambda i: own_ref[i] + other_ref[i]

    def collect(target_ref, y_here):
        for i, (x, y) in enumerate(needed_tiles(counts, at_x, y_here)):
            second_of_pair = lax.rem(lax.div(x, 2), 2) == 1
            got = total((lax.div(x, 4) * 2 + lax.rem(x, 2)) * counts[1] + y)
            got = jnp.where(second_of_pair, pltpu.roll(got, SUB - 1, 0), got)
            if i == 0:
                more = total(firsts + lax.div(x, 4) * half + lax.div(y, 2))
                got = jnp.where(even, got, jnp.where(second_of_pair, more, pltpu.roll(more, 1, 0)))
            target_ref[i] = got

    collect(out_ref, lax.rem(at_y + half, counts[1]))
    collect(keep_ref, at_y)


def middle_kernel(
    counts, base_ref, courant_ref, xa_ref, xb_ref, ya_ref, yb_ref,
    mid_ref, xa_out, xb_out, ya_out, yb_out, part_y_ref,
):
    place = where_am_i(counts)
    deep = base_ref.shape[1]
    halo_y(ya_ref, yb_ref, place, part_y_ref)
    coefs = turns(False)

    def body(depth, carry):
        fields = halo_step(depth, base_ref, courant_ref, xa_ref, xb_ref, part_y_ref, place, coefs)
        for field in range(2):
            mid_ref[field, depth] = fields[field]
        head, tail = head_rows(*fields), tail_rows(*fields)
        xa_out[depth] = jnp.where(place[0], head, tail)
        xb_out[depth] = jnp.where(place[0], tail, head)
        return carry

    lax.fori_loop(0, deep, body, 0, unroll=4)
    pack_columns(mid_ref, place[1], ya_out, yb_out)


def inject_kernel(counts, keep_ref, res_ref, cell_ref, courant_ref, layer_ref):
    _, _, no_next_x, no_prev_x, no_next_y, no_prev_y = where_am_i(counts)
    _, cells_x, cells_y = courant_ref.shape
    tiles = needed_tiles(counts, lax.axis_index("gx"), lax.axis_index("gy"))
    halves = REC_DEV // LANES
    res = [keep_ref[i] + res_ref[i] for i in range(len(tiles))]
    for i, absent in enumerate((no_next_x, no_prev_x, no_next_y, no_prev_y)):
        res[i + 1] = jnp.where(absent, 0.0, res[i + 1])
    cells = [
        [cell_ref[pl.ds((x * counts[1] + y) * halves + half, 1), :] for half in range(halves)] for x, y in tiles
    ]
    every = lambda at: at >= 0
    own = inject([(res[0], cells[0], every, every)], 2, cells_y)
    beside_x = inject(
        [(res[1], cells[1], lambda at: at < HALO, every), (res[2], cells[2], lambda at: at >= SUB - HALO, every)],
        1, cells_y,
    )
    beside_y = inject(
        [(res[3], cells[3], every, lambda at: at < HALO), (res[4], cells[4], every, lambda at: at >= cells_y - HALO)],
        1, cells_y,
    )
    kept, beside = turns(True), turns(False)
    lane = lanes_of((cells_x, cells_y))
    for field in range(2):
        layer = own[2 * field * cells_x : (2 * field + 1) * cells_x]
        side_x, side_y = [v[field * cells_x : (field + 1) * cells_x] for v in (beside_x, beside_y)]
        total = 3.0 * coef_zero * layer + along_x(layer, kept) + along_x(side_x, beside)
        for step in range(1, HALO + 1):
            up = pltpu.roll(jnp.where(lane < step, side_y, layer), cells_y - step, 1)
            down = pltpu.roll(jnp.where(lane >= cells_y - step, side_y, layer), step, 1)
            total = total + coef_rest[step - 1] * (up + down)
        layer_ref[field] = layer
        second = own[(2 * field + 1) * cells_x : (2 * field + 2) * cells_x]
        layer_ref[2 + field] = 2.0 * layer + courant_ref[RDEPTH] * total + second


def after_kernel(
    counts, base_ref, mid_ref, courant_ref, xa_ref, xb_ref, ya_ref, yb_ref, layer_ref,
    out_ref, mid_out, part_y_ref, held_ref, plane_ref, sems,
):
    place = where_am_i(counts)
    deep = base_ref.shape[1]
    beside = turns(False)
    copies = []

    def send_out(source, target):
        copy = pltpu.make_async_copy(source, target, sems.at[len(copies)])
        copy.start()
        copies.append(copy)

    send_out(mid_ref.at[:, pl.ds(0, RDEPTH)], mid_out.at[:, pl.ds(0, RDEPTH)])
    rest = pl.ds(RDEPTH + 1, deep - RDEPTH - 1)
    send_out(mid_ref.at[:, rest], mid_out.at[:, rest])
    for field in range(2):
        plane_ref[field, 0] = mid_ref[field, RDEPTH] + layer_ref[field]
    plane = pl.ds(RDEPTH, 1)
    send_out(plane_ref, mid_out.at[:, plane])

    halo_y(ya_ref, yb_ref, place, part_y_ref)
    size = deep // 4
    for part in range(4):
        def body(depth, carry):
            fields = halo_step(depth, base_ref, courant_ref, xa_ref, xb_ref, part_y_ref, place, beside)
            for field in range(2):
                held_ref[field, depth] = fields[field]
            return carry

        lax.fori_loop(part * size, (part + 1) * size, body, 0, unroll=4)
        if part == 0:
            for field in range(2):
                held_ref[field, RDEPTH] = held_ref[field, RDEPTH] + layer_ref[2 + field]
                for step in range(1, HALO + 1):
                    change = coef_rest[step - 1] * layer_ref[field]
                    for depth in (RDEPTH - step, RDEPTH + step):
                        if depth >= 0:
                            held_ref[field, depth] = held_ref[field, depth] + courant_ref[depth] * change
        depths = pl.ds(part * size, size)
        send_out(held_ref.at[:, depths], out_ref.at[:, depths])
    for copy in copies:
        copy.wait()


def paired(groups, count_x, count_y, partner):
    index = lambda g, x, y: (g * count_x + x) * count_y + y
    return [
        (index(g, x, y), index(*partner(g, x, y)))
        for g in range(groups)
        for x in range(count_x)
        for y in range(count_y)
    ]


def on_device(wave_now, wave_before, courant, records, signs, source_x, source_y, receiver_cell):
    _, deep, cells_x, cells_y = wave_now.shape
    groups, tiles_x, tiles_y = [lax.axis_size(axis) for axis in AXES]
    counts = (tiles_x, tiles_y)
    total_recv = receiver_cell.shape[0]
    tiles = total_recv // REC_DEV
    shots = records.shape[0]
    span = (cells_x * tiles_x + cells_y * tiles_y) // 4

    perms = functools.partial(paired, groups, tiles_x, tiles_y)
    swap_xa = perms(lambda g, x, y: (g, x ^ 1, y))
    swap_ya = perms(lambda g, x, y: (g, x, y ^ 1))
    swap_xb = perms(
        lambda g, x, y: ((g + groups // 2) % groups, x, y) if x in (0, tiles_x - 1) else (g, ((x + 1) ^ 1) - 1, y)
    )
    swap_yb = perms(lambda g, x, y: (g, x ^ 1, y) if y in (0, tiles_y - 1) else (g, x, ((y + 1) ^ 1) - 1))
    swap_along = {
        "gx": lambda step: perms(lambda g, x, y: (g, x ^ step, y)),
        "gy": lambda step: perms(lambda g, x, y: (g, x, y ^ step)),
    }
    steps = [("gx", 1 << i) for i in range(1, (tiles_x - 1).bit_length())]
    steps += [("gy", 1 << i) for i in range(1, (tiles_y - 1).bit_length() - 1)]
    send = lambda value, pairs: lax.ppermute(value, AXES, pairs)

    face_x = pltpu.VMEM((deep, cells_x, cells_y), F32)
    faces = deep // GROUP
    face_y = pltpu.VMEM((faces, cells_x, cells_y), F32)
    tiles_of = lambda count: pltpu.VMEM((count, SUB, LANES), F32)
    wave = wave_now.shape

    def kernel(body, outs, n_scalar, n_array, scratch=(), out_specs=None, aliases={}, cost=None):
        name = body.__name__.removesuffix("_kernel")

        def call(*args):
            args = args[:n_scalar] + tuple(near_memory(a) for a in args[n_scalar:])
            return pl.pallas_call(
                functools.partial(body, counts),
                out_shape=outs,
                in_specs=[SM] * n_scalar + [VM] * n_array,
                out_specs=out_specs if out_specs is not None else jax.tree.map(lambda _: VM, outs),
                scratch_shapes=scratch,
                input_output_aliases=aliases,
                cost_estimate=cost,
                compiler_params=PARAMS,
                name=name,
            )(*args)

        return call

    wave_v = pltpu.VMEM(wave, F32)
    cell_rows = receiver_cell.reshape(total_recv // LANES, LANES)
    record_rows = records.reshape(shots, 2, total_recv // LANES, LANES).transpose(0, 2, 1, 3)
    record_rows = record_rows.reshape(shots, 2 * total_recv // LANES, LANES)
    far = lambda value: pltpu.with_memory_space_constraint(value, pltpu.HBM)
    left = sum(packed_sizes(counts))
    pad = left + 2
    now, old, speed, cells, partial_res, xa, xb = pl.pallas_call(
        functools.partial(bring_kernel, float(span * span), counts),
        out_shape=(
            wave_v, wave_v, pltpu.VMEM(courant.shape, F32), pltpu.VMEM(cell_rows.shape, jnp.int32), tiles_of(tiles),
            face_x, face_x,
        ),
        in_specs=[pl.BlockSpec(memory_space=pltpu.HBM)] * 8,
        out_specs=(VM,) * 7,
        scratch_shapes=[
            pltpu.VMEM(record_rows.shape, BF16),
            pltpu.SMEM(signs.shape, jnp.int32), pltpu.SMEM((shots,), jnp.int32), pltpu.SMEM((shots,), jnp.int32),
            pltpu.SemaphoreType.DMA((8,)),
        ],
        compiler_params=PARAMS,
        name="bring",
    )(*(far(a) for a in (signs, source_x, source_y, record_rows, cell_rows, wave_now, wave_before, courant)))
    xb_in, other = send(xb, swap_xb), send(partial_res, swap_xa)
    ya, yb = kernel(pack_kernel, (face_y, tiles_of(faces + pad)), 0, 1)(now)
    yb_in = send(yb, swap_yb)
    partial_res, keep, xa = kernel(
        join_kernel, (tiles_of(faces + left), tiles_of(packed_sizes(counts)[1]), face_x), 0, 4, aliases={3: 2},
    )(ya, partial_res, other, xa)
    ya_in, xa_in = send(partial_res, swap_ya), send(xa, swap_xa)
    other = ya_in
    base = kernel(local_kernel, wave_v, 0, 3)(now, old, speed)
    for axis, step in steps:
        partial_res = kernel(sum_kernel, tiles_of(left), 0, 5)(partial_res, keep, other, base, yb_in)
        keep = partial_res
        other = send(partial_res, swap_along[axis](step))
    wave_middle, xa, xb, ya, yb = kernel(middle_kernel, (wave_v, face_x, face_x, face_y, face_y), 0, 6, [wave_v])(
        base, speed, xa_in, xb_in, ya_in, yb_in
    )
    wanted, keep, ya, yb = kernel(
        needed_kernel, (tiles_of(5), tiles_of(5), face_y, face_y), 0, 5, aliases={3: 2, 4: 3}, cost=pl.CostEstimate(flops=30*10**8, bytes_accessed=0, transcendentals=0)
    )(partial_res, other, wave_middle, ya, yb)
    xb_in, xa_in = send(xb, swap_xb), send(xa, swap_xa)
    res_in = send(wanted, swap_along["gy"](tiles_y // 2))
    ya_in, yb_in = send(ya, swap_ya), send(yb, swap_yb)
    base = kernel(second_local_kernel, wave_v, 0, 4, cost=pl.CostEstimate(flops=0*10**8, bytes_accessed=0, transcendentals=0))(wave_middle, now, speed, keep)
    plane = (2, 1, cells_x, cells_y)
    layers = kernel(inject_kernel, tiles_of(4), 0, 4)(keep, res_in, cells, speed)
    wave_after, wave_middle = kernel(
        after_kernel, (jax.ShapeDtypeStruct(wave, F32),) * 2, 0, 8,
        [wave_v, wave_v, pltpu.VMEM(plane, F32), pltpu.SemaphoreType.DMA((7,))],
        out_specs=(pl.BlockSpec(memory_space=pl.ANY),) * 2,
    )(base, wave_middle, speed, xa_in, xb_in, ya_in, yb_in, layers)
    return (wave_after, wave_middle)


def solution(mesh):
    return jax.shard_map(
        on_device,
        mesh=mesh,
        in_specs=(
            P("group", None, "gx", "gy"),
            P("group", None, "gx", "gy"),
            P("group", "gx", "gy"),
            P(("group", "gx", "gy"), None, None),
            P("group", ("gx", "gy")),
            P(("group", "gx", "gy")),
            P(("group", "gx", "gy")),
            P("group"),
        ),
        out_specs=(P("group", None, "gx", "gy"), P("group", None, "gx", "gy")),
        check_vma=False,
    )
```

```python
import functools

import jax
import jax.numpy as jnp
import ml_dtypes
import numpy as np
from jax import lax
from jax.experimental import pallas as pl
from jax.experimental.pallas import tpu as pltpu
from jax.sharding import PartitionSpec as P

REC_DEV = 256
RDEPTH = 2
HALO = 4
LANES = 128
SUB = 8
GROUP = 16
AXES = ("group", "gx", "gy")
F32, BF16 = jnp.float32, jnp.bfloat16

coef_zero = -205.0 / 72.0
coef_rest = (8.0 / 5.0, -1.0 / 5.0, 8.0 / 315.0, -1.0 / 560.0)
coef_high = [float(np.float32(c).astype(ml_dtypes.bfloat16)) for c in coef_rest]
coef_low = [float(np.float32(c - h).astype(ml_dtypes.bfloat16)) for c, h in zip(coef_rest, coef_high)]

VM = pl.BlockSpec(memory_space=pltpu.VMEM)
SM = pl.BlockSpec(memory_space=pltpu.SMEM)
PARAMS = pltpu.CompilerParams(vmem_limit_bytes=16 * 1024 * 1024)


def near_memory(value):
    return pltpu.with_memory_space_constraint(value, pltpu.VMEM)


def rows_of(shape):
    return lax.broadcasted_iota(jnp.int32, shape, len(shape) - 2)


def lanes_of(shape):
    return lax.broadcasted_iota(jnp.int32, shape, len(shape) - 1)


def dot(left, right):
    return jnp.dot(left, right, preferred_element_type=F32)


def split(value):
    first = value.astype(BF16)
    rest = value - first.astype(F32)
    second = rest.astype(BF16)
    return first, second, (rest - second.astype(F32)).astype(BF16)


def pick(step, coefs):
    out = jnp.zeros(step.shape, F32)
    for m in range(1, HALO + 1):
        out = jnp.where(step == m, coefs[m - 1], out)
    return out.astype(BF16)


def band(coefs):
    shape = (LANES, LANES)
    return pick(jnp.abs(rows_of(shape) - lanes_of(shape)), coefs)


def side():
    shape = (LANES, LANES)
    c = rows_of(shape) & 7
    j = lanes_of(shape)
    step = jnp.where(c < HALO, j + HALO - c, LANES + c - HALO - j)
    return jnp.where(rows_of(shape) < LANES // 2, pick(step, coef_high).astype(F32), pick(step, coef_low).astype(F32)).astype(BF16)


def pack_columns(ref, odd, ya_ref, yb_ref):
    lane_group = lanes_of((SUB, LANES)) >> 3
    low = (lanes_of((SUB, LANES)) & 7) < HALO
    pairs = ref.shape[1] // GROUP // 2

    def step(pair, carry):
        for field in range(2):
            both = []
            for group in range(2):
                tile = None
                for q in range(GROUP):
                    cells = ref[field, (pair * 2 + group) * GROUP + q]
                    turned = pltpu.roll(cells, (q * 2 * HALO + HALO) % LANES, 1)
                    tile = turned if tile is None else jnp.where(lane_group == q, turned, tile)
                both.append(tile)
            last = jnp.where(low, both[0], pltpu.roll(both[1], HALO, 1))
            first = jnp.where(low, pltpu.roll(both[0], LANES - HALO, 1), both[1])
            ya_ref[field * pairs + pair] = jnp.where(odd, first, last)
            yb_ref[field * pairs + pair] = jnp.where(odd, last, first)
        return carry

    lax.fori_loop(0, pairs, step, 0)


def sides_y(ya, yb, odd, no_next, no_prev):
    after = jnp.where(no_next, 0.0, jnp.where(odd, yb, ya))
    before = jnp.where(no_prev, 0.0, jnp.where(odd, ya, yb))
    low = (lanes_of(ya.shape) & 7) < HALO
    return (
        jnp.where(low, before, pltpu.roll(after, HALO, 1)),
        jnp.where(low, pltpu.roll(before, LANES - HALO, 1), after),
    )


def local_y(cells, high, low):
    first, second, _ = split(cells)
    return dot(jnp.concatenate([first, second, first], axis=1), jnp.concatenate([high, high, low], axis=0))


def halo_y(ya_ref, yb_ref, place, out_ref):
    weights = side()
    _, odd, _, _, no_next, no_prev = place
    groups = out_ref.shape[1] // GROUP
    lane_group = lanes_of((SUB, LANES)) >> 3
    half, quarter = GROUP // 2, GROUP // 4
    for field in range(2):
        rows = []
        for pair in range(groups // 2):
            at = field * (groups // 2) + pair
            for beside in sides_y(ya_ref[at], yb_ref[at], odd, no_next, no_prev):
                first = beside.astype(BF16).astype(F32)
                second = (beside - first).astype(BF16).astype(F32)
                turned = pltpu.roll(first, LANES // 2, 1)
                seconds = [pltpu.roll(second, turn, 1) for turn in (LANES // 4, LANES - LANES // 4)]
                for q in range(GROUP):
                    other = (q + half) % GROUP
                    at_second = (q % half + quarter) % half
                    tile = jnp.where(lane_group == q, first, 0.0)
                    tile = jnp.where(lane_group == other, turned, tile)
                    turn = 0 if (at_second - q) % GROUP == quarter else 1
                    rows.append(jnp.where(lane_group == at_second, seconds[turn], tile))
        total = dot(jnp.concatenate(rows, axis=0).astype(BF16), weights)
        out_ref[field] = total.reshape(groups * GROUP, SUB, LANES)


def where_am_i(counts):
    at_x, at_y = lax.axis_index("gx"), lax.axis_index("gy")
    return (
        lax.rem(at_x, 2) == 1, lax.rem(at_y, 2) == 1,
        at_x == counts[0] - 1, at_x == 0, at_y == counts[1] - 1, at_y == 0,
    )


def head_rows(first, second):
    return jnp.where(rows_of(first.shape) < HALO, first, pltpu.roll(second, HALO, 0))


def tail_rows(first, second):
    return jnp.where(rows_of(first.shape) < HALO, pltpu.roll(first, HALO, 0), second)


def face_turns(place):
    _, _, no_next, no_prev, _, _ = place
    row = rows_of((SUB, LANES)) % HALO
    after = [jnp.where((row >= d) & jnp.logical_not(no_next), coef_rest[HALO - 1 - d], 0.0) for d in range(HALO)]
    before = [jnp.where((row + d < HALO) & jnp.logical_not(no_prev), coef_rest[HALO - 1 - d], 0.0) for d in range(HALO)]
    return after, before


def from_faces(xa, xb, odd, coefs):
    after, before = jnp.where(odd, xb, xa), jnp.where(odd, xa, xb)
    after_sum, before_sum = coefs[0][0] * after, coefs[1][0] * before
    for d in range(1, HALO):
        after_sum = after_sum + coefs[0][d] * pltpu.roll(after, d, 0)
        before_sum = before_sum + coefs[1][d] * pltpu.roll(before, SUB - d, 0)
    low = rows_of(after.shape) < HALO
    return (
        jnp.where(low, before_sum, pltpu.roll(after_sum, HALO, 0)),
        jnp.where(low, pltpu.roll(before_sum, HALO, 0), after_sum),
    )


def turns(kept):
    row = rows_of((SUB, LANES))
    out = []
    for turn in range(1, SUB):
        coef = coef_rest[min(turn, SUB - turn) - 1]
        inside = row >= turn if turn < HALO else row < turn if turn > HALO else row >= 0
        out.append(jnp.where(inside if kept else jnp.logical_not(inside) | (turn == HALO), coef, 0.0))
    return out


def along_x(cells, coefs):
    total = coefs[0] * pltpu.roll(cells, 1, 0)
    for turn in range(2, SUB):
        total = total + coefs[turn - 1] * pltpu.roll(cells, turn, 0)
    return total


def local_step(now_ref, old_ref, courant_ref, out_ref):
    deep = now_ref.shape[1]
    high, low = band(coef_high), band(coef_low)
    for field in range(2):
        cells = now_ref[field].reshape(deep * SUB, LANES)
        out_ref[field] = local_y(cells, high, low).reshape(deep, SUB, LANES)
    coefs = turns(True)

    def body(depth, static_depth):
        for field in range(2):
            cells = now_ref[field, depth]
            total = 3.0 * coef_zero * cells + out_ref[field, depth] + along_x(cells, coefs)
            for step in range(1, HALO + 1):
                near = None
                if static_depth is None or static_depth + step < deep:
                    near = now_ref[field, depth + step]
                if static_depth is None or static_depth >= step:
                    before = now_ref[field, depth - step]
                    near = before if near is None else near + before
                total = total + coef_rest[step - 1] * near
            out_ref[field, depth] = 2.0 * cells - old_ref[field, depth] + courant_ref[depth] * total

    over_depth(deep, body)


def halo_step(depth, base_ref, courant_ref, xa_ref, xb_ref, part_y_ref, odd, coefs):
    sides = from_faces(xa_ref[depth], xb_ref[depth], odd, coefs)
    return [
        base_ref[field, depth] + courant_ref[depth] * (part_y_ref[field, depth] + sides[field]) for field in range(2)
    ]


def over_depth(deep, body):
    def inner(depth, carry):
        body(depth, None)
        return carry

    for depth in range(HALO):
        body(depth, depth)
    lax.fori_loop(HALO, deep - HALO, inner, 0, unroll=8)
    for depth in range(deep - HALO, deep):
        body(depth, depth)


def residual(counts, cells_x, cells_y, radius_sq, signs_ref, sx_ref, sy_ref, records_ref, cell_ref, out_ref):
    shots, rows, _ = records_ref.shape
    chunk = min(rows, 64)
    per = 2 * REC_DEV // LANES
    twice = (rows_of((chunk, chunk // 2)) >> 1 == lanes_of((chunk, chunk // 2))).astype(F32).astype(BF16)

    def chunk_step(c, carry):
        cell = cell_ref[pl.ds(pl.multiple_of(c * (chunk // 2), chunk // 2), chunk // 2), :]
        row, column = lax.shift_right_logical(cell, cells_y.bit_length() - 1), cell & (cells_y - 1)
        row, column = [dot(twice, v.astype(F32).astype(BF16)) for v in (row, column)]
        tile = c * (chunk // per) + rows_of((chunk, LANES)) // per
        tile_x, tile_y = tile // counts[1], tile % counts[1]
        pos_x = (tile_x * cells_x).astype(F32) + row
        pos_y = (tile_y * cells_y).astype(F32) + column
        start = pl.multiple_of(c * chunk, chunk)

        def shot_step(shot, sums):
            dx = pos_x - sx_ref[shot].astype(F32)
            dy = pos_y - sy_ref[shot].astype(F32)
            dist = dx * dx + dy * dy
            whole = dist + radius_sq
            inverse = pl.reciprocal(whole, approx=True)
            inverse = inverse * (2.0 - whole * inverse)
            taped = records_ref[shot, pl.ds(start, chunk), :].astype(F32) * (dist * inverse)
            return tuple(s + signs_ref[code, shot].astype(F32) * taped for code, s in enumerate(sums))

        sums = lax.fori_loop(0, shots, shot_step, (jnp.zeros((chunk, LANES), F32),) * 2, unroll=2)
        for t in range(chunk // per):
            both = [s[t * per : (t + 1) * per] for s in sums]
            out_ref[c * (chunk // per) + t] = jnp.concatenate(both, axis=0)
        return carry

    lax.fori_loop(0, rows // chunk, chunk_step, 0)


def bring_kernel(
    radius_sq, counts, signs_hbm, sx_hbm, sy_hbm, records_hbm, cell_hbm, now_hbm, old_hbm, courant_hbm,
    now_ref, old_ref, courant_ref, cell_ref, res_ref, xa_ref, xb_ref, records_ref, signs_ref, sx_ref, sy_ref, sems,
):
    copies = []

    def bring(source, target):
        copy = pltpu.make_async_copy(source, target, sems.at[len(copies)])
        copy.start()
        copies.append(copy)

    for source, target in (
        (cell_hbm, cell_ref), (signs_hbm, signs_ref), (sx_hbm, sx_ref), (sy_hbm, sy_ref), (records_hbm, records_ref),
        (now_hbm, now_ref), (old_hbm, old_ref), (courant_hbm, courant_ref),
    ):
        bring(source, target)
    for copy in copies[:5]:
        copy.wait()
    _, deep, cells_x, cells_y = now_ref.shape
    residual(counts, cells_x, cells_y, radius_sq, signs_ref, sx_ref, sy_ref, records_ref, cell_ref, res_ref)
    copies[5].wait()
    odd = where_am_i(counts)[0]

    def body(depth, carry):
        first, second = now_ref[0, depth], now_ref[1, depth]
        head, tail = head_rows(first, second), tail_rows(first, second)
        xb_ref[depth] = jnp.where(odd, tail, head)
        xa_ref[depth] = jnp.where(odd, head, tail)
        return carry

    lax.fori_loop(0, deep, body, 0, unroll=8)
    for copy in copies[6:]:
        copy.wait()


def pack_kernel(counts, now_ref, ya_ref, yb_ref):
    pack_columns(now_ref, where_am_i(counts)[1], ya_ref, yb_ref)


def needed_tiles(counts, x, y):
    return (
        (x, y),
        (jnp.minimum(x + 1, counts[0] - 1), y), (jnp.maximum(x - 1, 0), y),
        (x, jnp.minimum(y + 1, counts[1] - 1)), (x, jnp.maximum(y - 1, 0)),
    )


def inject(pieces, samples, cells_y):
    values, hots = [], []
    for res, cells, row_kept, column_kept in pieces:
        for half in range(REC_DEV // LANES):
            row = lax.shift_right_logical(cells[half], cells_y.bit_length() - 1)
            column = cells[half] & (cells_y - 1)
            in_row = (rows_of((SUB, LANES)) == row) & row_kept(rows_of((SUB, LANES)))
            values.append(jnp.concatenate(
                [
                    jnp.where(in_row, res[code * 4 + half * 2 + sample][None, :], 0.0)
                    for code in range(2)
                    for sample in range(samples)
                ],
                axis=0,
            ))
            at = rows_of((cells_y, LANES))
            hots.append(((at == column) & column_kept(at)).astype(F32).astype(BF16))
    values = jnp.concatenate(split(jnp.concatenate(values, axis=1)), axis=0)
    got = lax.dot_general(
        values, jnp.concatenate(hots, axis=1), (((1,), (1,)), ((), ())), preferred_element_type=F32
    )
    count = 2 * samples * SUB
    return got[:count] + got[count : 2 * count] + got[2 * count :]


def second_local_kernel(counts, now_ref, old_ref, courant_ref, before_ref, out_ref):
    del before_ref
    local_step(now_ref, old_ref, courant_ref, out_ref)


def local_kernel(counts, now_ref, old_ref, courant_ref, out_ref):
    local_step(now_ref, old_ref, courant_ref, out_ref)


def packed_sizes(counts):
    return counts[0] * counts[1] // 2, counts[0] * counts[1] // 8


def pack_samples(first, second):
    even = rows_of((SUB, LANES)) % 2 == 0
    return (
        jnp.where(even, first, pltpu.roll(second, 1, 0)),
        jnp.where(even, pltpu.roll(first, SUB - 1, 0), second),
    )


def join_kernel(counts, face_ref, own_ref, other_ref, xa_ref, out_ref, keep_ref, xa_out):
    del xa_ref, xa_out
    faces, at = face_ref.shape[0], own_ref.shape[0] - counts[0] * counts[1]
    out_ref[:faces] = face_ref[...]
    total = lambda x, y: own_ref[at + x * counts[1] + y] + other_ref[at + x * counts[1] + y]
    here = faces
    for high in range(0, counts[0], 4):
        for x in range(high, high + 2):
            for y in range(counts[1]):
                out_ref[here] = pack_samples(total(x, y), total(x + 2, y))[0]
                here += 1
    odd_x, odd_y = [lax.rem(lax.axis_index(axis), 2) for axis in AXES[1:]]
    i = 0
    for high in range(0, counts[0], 4):
        for y in range(0, counts[1], 2):
            x = high + odd_x
            out_ref[here + i] = pack_samples(total(x, y + 1 - odd_y), total(x + 2, y + 1 - odd_y))[1]
            keep_ref[i] = pack_samples(total(x, y + odd_y), total(x + 2, y + odd_y))[1]
            i += 1


def sum_kernel(counts, own_ref, keep_ref, other_ref, before_ref, more_ref, out_ref):
    del before_ref, more_ref
    firsts, seconds = packed_sizes(counts)
    at, at_other = [ref.shape[0] - firsts - seconds for ref in (own_ref, other_ref)]
    out_ref[:firsts] = own_ref[pl.ds(at, firsts)] + other_ref[pl.ds(at_other, firsts)]
    at_keep = keep_ref.shape[0] - seconds
    out_ref[firsts:] = keep_ref[pl.ds(at_keep, seconds)] + other_ref[pl.ds(at_other + firsts, seconds)]


def needed_kernel(counts, own_ref, other_ref, before_ref, ya_ref, yb_ref, out_ref, keep_ref, *handed_on):
    del before_ref, ya_ref, yb_ref, handed_on
    firsts, _ = packed_sizes(counts)
    at_x, at_y = lax.axis_index("gx"), lax.axis_index("gy")
    half = counts[1] // 2
    even = rows_of((SUB, LANES)) % 2 == 0
    total = lambda i: own_ref[i] + other_ref[i]

    def collect(target_ref, y_here):
        for i, (x, y) in enumerate(needed_tiles(counts, at_x, y_here)):
            second_of_pair = lax.rem(lax.div(x, 2), 2) == 1
            got = total((lax.div(x, 4) * 2 + lax.rem(x, 2)) * counts[1] + y)
            got = jnp.where(second_of_pair, pltpu.roll(got, SUB - 1, 0), got)
            if i == 0:
                more = total(firsts + lax.div(x, 4) * half + lax.div(y, 2))
                got = jnp.where(even, got, jnp.where(second_of_pair, more, pltpu.roll(more, 1, 0)))
            target_ref[i] = got

    collect(out_ref, lax.rem(at_y + half, counts[1]))
    collect(keep_ref, at_y)


def middle_kernel(
    counts, base_ref, courant_ref, xa_ref, xb_ref, ya_ref, yb_ref,
    mid_ref, xa_out, xb_out, ya_out, yb_out, part_y_ref,
):
    place = where_am_i(counts)
    deep = base_ref.shape[1]
    halo_y(ya_ref, yb_ref, place, part_y_ref)
    coefs = face_turns(place)

    def body(depth, carry):
        fields = halo_step(depth, base_ref, courant_ref, xa_ref, xb_ref, part_y_ref, place[0], coefs)
        for field in range(2):
            mid_ref[field, depth] = fields[field]
        head, tail = head_rows(*fields), tail_rows(*fields)
        xa_out[depth] = jnp.where(place[0], head, tail)
        xb_out[depth] = jnp.where(place[0], tail, head)
        return carry

    lax.fori_loop(0, deep, body, 0, unroll=8)
    pack_columns(mid_ref, place[1], ya_out, yb_out)


def inject_kernel(counts, keep_ref, res_ref, cell_ref, courant_ref, layer_ref):
    _, _, no_next_x, no_prev_x, no_next_y, no_prev_y = where_am_i(counts)
    _, cells_x, cells_y = courant_ref.shape
    tiles = needed_tiles(counts, lax.axis_index("gx"), lax.axis_index("gy"))
    halves = REC_DEV // LANES
    res = [keep_ref[i] + res_ref[i] for i in range(len(tiles))]
    for i, absent in enumerate((no_next_x, no_prev_x, no_next_y, no_prev_y)):
        res[i + 1] = jnp.where(absent, 0.0, res[i + 1])
    cells = [
        [cell_ref[pl.ds((x * counts[1] + y) * halves + half, 1), :] for half in range(halves)] for x, y in tiles
    ]
    every = lambda at: at >= 0
    own = inject([(res[0], cells[0], every, every)], 2, cells_y)
    beside_x = inject(
        [(res[1], cells[1], lambda at: at < HALO, every), (res[2], cells[2], lambda at: at >= SUB - HALO, every)],
        1, cells_y,
    )
    beside_y = inject(
        [(res[3], cells[3], every, lambda at: at < HALO), (res[4], cells[4], every, lambda at: at >= cells_y - HALO)],
        1, cells_y,
    )
    kept, beside = turns(True), turns(False)
    lane = lanes_of((cells_x, cells_y))
    for field in range(2):
        layer = own[2 * field * cells_x : (2 * field + 1) * cells_x]
        side_x, side_y = [v[field * cells_x : (field + 1) * cells_x] for v in (beside_x, beside_y)]
        total = 3.0 * coef_zero * layer + along_x(layer, kept) + along_x(side_x, beside)
        for step in range(1, HALO + 1):
            up = pltpu.roll(jnp.where(lane < step, side_y, layer), cells_y - step, 1)
            down = pltpu.roll(jnp.where(lane >= cells_y - step, side_y, layer), step, 1)
            total = total + coef_rest[step - 1] * (up + down)
        layer_ref[field] = layer
        second = own[(2 * field + 1) * cells_x : (2 * field + 2) * cells_x]
        layer_ref[2 + field] = 2.0 * layer + courant_ref[RDEPTH] * total + second


def after_kernel(
    counts, base_ref, mid_ref, courant_ref, xa_ref, xb_ref, ya_ref, yb_ref, layer_ref,
    out_ref, mid_out, part_y_ref, held_ref, plane_ref, sems,
):
    place = where_am_i(counts)
    deep = base_ref.shape[1]
    coefs = face_turns(place)
    copies = []

    def send_out(source, target):
        copy = pltpu.make_async_copy(source, target, sems.at[len(copies)])
        copy.start()
        copies.append(copy)

    send_out(mid_ref.at[:, pl.ds(0, RDEPTH)], mid_out.at[:, pl.ds(0, RDEPTH)])
    rest = pl.ds(RDEPTH + 1, deep - RDEPTH - 1)
    send_out(mid_ref.at[:, rest], mid_out.at[:, rest])
    for field in range(2):
        plane_ref[field, 0] = mid_ref[field, RDEPTH] + layer_ref[field]
    plane = pl.ds(RDEPTH, 1)
    send_out(plane_ref, mid_out.at[:, plane])

    halo_y(ya_ref, yb_ref, place, part_y_ref)
    size = deep // 8
    for part in range(8):
        def body(depth, carry):
            fields = halo_step(depth, base_ref, courant_ref, xa_ref, xb_ref, part_y_ref, place[0], coefs)
            for field in range(2):
                held_ref[field, depth] = fields[field]
            return carry

        lax.fori_loop(part * size, (part + 1) * size, body, 0, unroll=8)
        if part == 0:
            for field in range(2):
                held_ref[field, RDEPTH] = held_ref[field, RDEPTH] + layer_ref[2 + field]
                for step in range(1, HALO + 1):
                    change = coef_rest[step - 1] * layer_ref[field]
                    for depth in (RDEPTH - step, RDEPTH + step):
                        if depth >= 0:
                            held_ref[field, depth] = held_ref[field, depth] + courant_ref[depth] * change
        depths = pl.ds(part * size, size)
        send_out(held_ref.at[:, depths], out_ref.at[:, depths])
    for copy in copies:
        copy.wait()


def paired(groups, count_x, count_y, partner):
    index = lambda g, x, y: (g * count_x + x) * count_y + y
    return [
        (index(g, x, y), index(*partner(g, x, y)))
        for g in range(groups)
        for x in range(count_x)
        for y in range(count_y)
    ]


def on_device(wave_now, wave_before, courant, records, signs, source_x, source_y, receiver_cell):
    _, deep, cells_x, cells_y = wave_now.shape
    groups, tiles_x, tiles_y = [lax.axis_size(axis) for axis in AXES]
    counts = (tiles_x, tiles_y)
    total_recv = receiver_cell.shape[0]
    tiles = total_recv // REC_DEV
    shots = records.shape[0]
    span = (cells_x * tiles_x + cells_y * tiles_y) // 4

    perms = functools.partial(paired, groups, tiles_x, tiles_y)
    swap_xa = perms(lambda g, x, y: (g, x ^ 1, y))
    swap_ya = perms(lambda g, x, y: (g, x, y ^ 1))
    swap_xb = perms(
        lambda g, x, y: ((g + groups // 2) % groups, x, y) if x in (0, tiles_x - 1) else (g, ((x + 1) ^ 1) - 1, y)
    )
    swap_yb = perms(lambda g, x, y: (g, x ^ 1, y) if y in (0, tiles_y - 1) else (g, x, ((y + 1) ^ 1) - 1))
    swap_along = {
        "gx": lambda step: perms(lambda g, x, y: (g, x ^ step, y)),
        "gy": lambda step: perms(lambda g, x, y: (g, x, y ^ step)),
    }
    steps = [("gx", 1 << i) for i in range(1, (tiles_x - 1).bit_length())]
    steps += [("gy", 1 << i) for i in range(1, (tiles_y - 1).bit_length() - 1)]
    send = lambda value, pairs: lax.ppermute(value, AXES, pairs)

    face_x = pltpu.VMEM((deep, cells_x, cells_y), F32)
    faces = deep // GROUP
    face_y = pltpu.VMEM((faces, cells_x, cells_y), F32)
    tiles_of = lambda count: pltpu.VMEM((count, SUB, LANES), F32)
    wave = wave_now.shape

    def kernel(body, outs, n_scalar, n_array, scratch=(), out_specs=None, aliases={}, cost=None):
        name = body.__name__.removesuffix("_kernel")

        def call(*args):
            args = args[:n_scalar] + tuple(near_memory(a) for a in args[n_scalar:])
            return pl.pallas_call(
                functools.partial(body, counts),
                out_shape=outs,
                in_specs=[SM] * n_scalar + [VM] * n_array,
                out_specs=out_specs if out_specs is not None else jax.tree.map(lambda _: VM, outs),
                scratch_shapes=scratch,
                input_output_aliases=aliases,
                cost_estimate=cost,
                compiler_params=PARAMS,
                name=name,
            )(*args)

        return call

    wave_v = pltpu.VMEM(wave, F32)
    cell_rows = receiver_cell.reshape(total_recv // LANES, LANES)
    record_rows = records.reshape(shots, 2, total_recv // LANES, LANES).transpose(0, 2, 1, 3)
    record_rows = record_rows.reshape(shots, 2 * total_recv // LANES, LANES)
    far = lambda value: pltpu.with_memory_space_constraint(value, pltpu.HBM)
    left = sum(packed_sizes(counts))
    pad = left + 2
    now, old, speed, cells, partial_res, xa, xb = pl.pallas_call(
        functools.partial(bring_kernel, float(span * span), counts),
        out_shape=(
            wave_v, wave_v, pltpu.VMEM(courant.shape, F32), pltpu.VMEM(cell_rows.shape, jnp.int32), tiles_of(tiles),
            face_x, face_x,
        ),
        in_specs=[pl.BlockSpec(memory_space=pltpu.HBM)] * 8,
        out_specs=(VM,) * 7,
        scratch_shapes=[
            pltpu.VMEM(record_rows.shape, BF16),
            pltpu.SMEM(signs.shape, jnp.int32), pltpu.SMEM((shots,), jnp.int32), pltpu.SMEM((shots,), jnp.int32),
            pltpu.SemaphoreType.DMA((8,)),
        ],
        compiler_params=PARAMS,
        name="bring",
    )(*(far(a) for a in (signs, source_x, source_y, record_rows, cell_rows, wave_now, wave_before, courant)))
    xb_in, other = send(xb, swap_xb), send(partial_res, swap_xa)
    ya, yb = kernel(pack_kernel, (face_y, tiles_of(faces + pad)), 0, 1)(now)
    yb_in = send(yb, swap_yb)
    partial_res, keep, xa = kernel(
        join_kernel, (tiles_of(faces + left), tiles_of(packed_sizes(counts)[1]), face_x), 0, 4, aliases={3: 2},
    )(ya, partial_res, other, xa)
    ya_in, xa_in = send(partial_res, swap_ya), send(xa, swap_xa)
    other = ya_in
    base = kernel(local_kernel, wave_v, 0, 3)(now, old, speed)
    for axis, step in steps:
        partial_res = kernel(sum_kernel, tiles_of(left), 0, 5)(partial_res, keep, other, base, cells)
        keep = partial_res
        other = send(partial_res, swap_along[axis](step))
    wave_middle, xa, xb, ya, yb = kernel(middle_kernel, (wave_v, face_x, face_x, face_y, face_y), 0, 6, [wave_v])(
        base, speed, xa_in, xb_in, ya_in, yb_in
    )
    wanted, keep, ya, yb = kernel(
        needed_kernel, (tiles_of(5), tiles_of(5), face_y, face_y), 0, 5, aliases={3: 2, 4: 3}, cost=pl.CostEstimate(flops=30*10**8, bytes_accessed=0, transcendentals=0)
    )(partial_res, other, wave_middle, ya, yb)
    xb_in, xa_in = send(xb, swap_xb), send(xa, swap_xa)
    res_in = send(wanted, swap_along["gy"](tiles_y // 2))
    ya_in, yb_in = send(ya, swap_ya), send(yb, swap_yb)
    base = kernel(second_local_kernel, wave_v, 0, 4, cost=pl.CostEstimate(flops=0*10**8, bytes_accessed=0, transcendentals=0))(wave_middle, now, speed, keep)
    plane = (2, 1, cells_x, cells_y)
    layers = kernel(inject_kernel, tiles_of(4), 0, 4)(keep, res_in, cells, speed)
    wave_after, wave_middle = kernel(
        after_kernel, (jax.ShapeDtypeStruct(wave, F32),) * 2, 0, 8,
        [wave_v, wave_v, pltpu.VMEM(plane, F32), pltpu.SemaphoreType.DMA((11,))],
        out_specs=(pl.BlockSpec(memory_space=pl.ANY),) * 2,
    )(base, wave_middle, speed, xa_in, xb_in, ya_in, yb_in, layers)
    return (wave_after, wave_middle)


def solution(mesh):
    return jax.shard_map(
        on_device,
        mesh=mesh,
        in_specs=(
            P("group", None, "gx", "gy"),
            P("group", None, "gx", "gy"),
            P("group", "gx", "gy"),
            P(("group", "gx", "gy"), None, None),
            P("group", ("gx", "gy")),
            P(("group", "gx", "gy")),
            P(("group", "gx", "gy")),
            P("group"),
        ),
        out_specs=(P("group", None, "gx", "gy"), P("group", None, "gx", "gy")),
        check_vma=False,
    )
```

```python
import functools

import jax
import jax.numpy as jnp
import ml_dtypes
import numpy as np
from jax import lax
from jax.experimental import pallas as pl
from jax.experimental.pallas import tpu as pltpu
from jax.sharding import PartitionSpec as P

REC_DEV = 256
RDEPTH = 2
HALO = 4
LANES = 128
SUB = 8
GROUP = 16
AXES = ("group", "gx", "gy")
F32, BF16 = jnp.float32, jnp.bfloat16

coef_zero = -205.0 / 72.0
coef_rest = (8.0 / 5.0, -1.0 / 5.0, 8.0 / 315.0, -1.0 / 560.0)
coef_high = [float(np.float32(c).astype(ml_dtypes.bfloat16)) for c in coef_rest]
coef_low = [float(np.float32(c - h).astype(ml_dtypes.bfloat16)) for c, h in zip(coef_rest, coef_high)]

VM = pl.BlockSpec(memory_space=pltpu.VMEM)
SM = pl.BlockSpec(memory_space=pltpu.SMEM)
PARAMS = pltpu.CompilerParams(vmem_limit_bytes=16 * 1024 * 1024)


def near_memory(value):
    return pltpu.with_memory_space_constraint(value, pltpu.VMEM)


def rows_of(shape):
    return lax.broadcasted_iota(jnp.int32, shape, len(shape) - 2)


def lanes_of(shape):
    return lax.broadcasted_iota(jnp.int32, shape, len(shape) - 1)


def dot(left, right):
    return jnp.dot(left, right, preferred_element_type=F32)


def split(value):
    first = value.astype(BF16)
    rest = value - first.astype(F32)
    second = rest.astype(BF16)
    return first, second, (rest - second.astype(F32)).astype(BF16)


def pick(step, coefs):
    out = jnp.zeros(step.shape, F32)
    for m in range(1, HALO + 1):
        out = jnp.where(step == m, coefs[m - 1], out)
    return out.astype(BF16)


def band(coefs):
    shape = (LANES, LANES)
    return pick(jnp.abs(rows_of(shape) - lanes_of(shape)), coefs)


def side():
    shape = (LANES, LANES)
    c = rows_of(shape) & 7
    j = lanes_of(shape)
    step = jnp.where(c < HALO, j + HALO - c, LANES + c - HALO - j)
    return jnp.where(rows_of(shape) < LANES // 2, pick(step, coef_high).astype(F32), pick(step, coef_low).astype(F32)).astype(BF16)


def pack_columns(ref, odd, ya_ref, yb_ref):
    lane_group = lanes_of((SUB, LANES)) >> 3
    low = (lanes_of((SUB, LANES)) & 7) < HALO
    pairs = ref.shape[1] // GROUP // 2

    def step(pair, carry):
        for field in range(2):
            both = []
            for group in range(2):
                tile = None
                for q in range(GROUP):
                    cells = ref[field, (pair * 2 + group) * GROUP + q]
                    turned = pltpu.roll(cells, (q * 2 * HALO + HALO) % LANES, 1)
                    tile = turned if tile is None else jnp.where(lane_group == q, turned, tile)
                both.append(tile)
            last = jnp.where(low, both[0], pltpu.roll(both[1], HALO, 1))
            first = jnp.where(low, pltpu.roll(both[0], LANES - HALO, 1), both[1])
            ya_ref[field * pairs + pair] = jnp.where(odd, first, last)
            yb_ref[field * pairs + pair] = jnp.where(odd, last, first)
        return carry

    lax.fori_loop(0, pairs, step, 0)


def sides_y(ya, yb, odd, no_next, no_prev):
    after = jnp.where(no_next, 0.0, jnp.where(odd, yb, ya))
    before = jnp.where(no_prev, 0.0, jnp.where(odd, ya, yb))
    low = (lanes_of(ya.shape) & 7) < HALO
    return (
        jnp.where(low, before, pltpu.roll(after, HALO, 1)),
        jnp.where(low, pltpu.roll(before, LANES - HALO, 1), after),
    )


def local_y(cells, high, low):
    first, second, _ = split(cells)
    return dot(jnp.concatenate([first, second, first], axis=1), jnp.concatenate([high, high, low], axis=0))


def halo_y(ya_ref, yb_ref, place, out_ref):
    weights = side()
    _, odd, _, _, no_next, no_prev = place
    groups = out_ref.shape[1] // GROUP
    lane_group = lanes_of((SUB, LANES)) >> 3
    half, quarter = GROUP // 2, GROUP // 4
    for field in range(2):
        rows = []
        for pair in range(groups // 2):
            at = field * (groups // 2) + pair
            for beside in sides_y(ya_ref[at], yb_ref[at], odd, no_next, no_prev):
                first = beside.astype(BF16).astype(F32)
                second = (beside - first).astype(BF16).astype(F32)
                turned = pltpu.roll(first, LANES // 2, 1)
                seconds = [pltpu.roll(second, turn, 1) for turn in (LANES // 4, LANES - LANES // 4)]
                for q in range(GROUP):
                    other = (q + half) % GROUP
                    at_second = (q % half + quarter) % half
                    tile = jnp.where(lane_group == q, first, 0.0)
                    tile = jnp.where(lane_group == other, turned, tile)
                    turn = 0 if (at_second - q) % GROUP == quarter else 1
                    rows.append(jnp.where(lane_group == at_second, seconds[turn], tile))
        total = dot(jnp.concatenate(rows, axis=0).astype(BF16), weights)
        out_ref[field] = total.reshape(groups * GROUP, SUB, LANES)


def where_am_i(counts):
    at_x, at_y = lax.axis_index("gx"), lax.axis_index("gy")
    return (
        lax.rem(at_x, 2) == 1, lax.rem(at_y, 2) == 1,
        at_x == counts[0] - 1, at_x == 0, at_y == counts[1] - 1, at_y == 0,
    )


def head_rows(first, second):
    return jnp.where(rows_of(first.shape) < HALO, first, pltpu.roll(second, HALO, 0))


def tail_rows(first, second):
    return jnp.where(rows_of(first.shape) < HALO, pltpu.roll(first, HALO, 0), second)


def face_turns(place):
    _, _, no_next, no_prev, _, _ = place
    row = rows_of((SUB, LANES)) % HALO
    after = [jnp.where((row >= d) & jnp.logical_not(no_next), coef_rest[HALO - 1 - d], 0.0) for d in range(HALO)]
    before = [jnp.where((row + d < HALO) & jnp.logical_not(no_prev), coef_rest[HALO - 1 - d], 0.0) for d in range(HALO)]
    return after, before


def from_faces(xa, xb, odd, coefs):
    after, before = jnp.where(odd, xb, xa), jnp.where(odd, xa, xb)
    after_sum, before_sum = coefs[0][0] * after, coefs[1][0] * before
    for d in range(1, HALO):
        after_sum = after_sum + coefs[0][d] * pltpu.roll(after, d, 0)
        before_sum = before_sum + coefs[1][d] * pltpu.roll(before, SUB - d, 0)
    low = rows_of(after.shape) < HALO
    return (
        jnp.where(low, before_sum, pltpu.roll(after_sum, HALO, 0)),
        jnp.where(low, pltpu.roll(before_sum, HALO, 0), after_sum),
    )


def turns(kept):
    row = rows_of((SUB, LANES))
    out = []
    for turn in range(1, SUB):
        coef = coef_rest[min(turn, SUB - turn) - 1]
        inside = row >= turn if turn < HALO else row < turn if turn > HALO else row >= 0
        out.append(jnp.where(inside if kept else jnp.logical_not(inside) | (turn == HALO), coef, 0.0))
    return out


def along_x(cells, coefs):
    total = coefs[0] * pltpu.roll(cells, 1, 0)
    for turn in range(2, SUB):
        total = total + coefs[turn - 1] * pltpu.roll(cells, turn, 0)
    return total


def local_step(now_ref, old_ref, courant_ref, out_ref):
    deep = now_ref.shape[1]
    high, low = band(coef_high), band(coef_low)
    for field in range(2):
        cells = now_ref[field].reshape(deep * SUB, LANES)
        out_ref[field] = local_y(cells, high, low).reshape(deep, SUB, LANES)
    coefs = turns(True)

    def body(depth, static_depth):
        for field in range(2):
            cells = now_ref[field, depth]
            total = 3.0 * coef_zero * cells + out_ref[field, depth] + along_x(cells, coefs)
            for step in range(1, HALO + 1):
                near = None
                if static_depth is None or static_depth + step < deep:
                    near = now_ref[field, depth + step]
                if static_depth is None or static_depth >= step:
                    before = now_ref[field, depth - step]
                    near = before if near is None else near + before
                total = total + coef_rest[step - 1] * near
            out_ref[field, depth] = 2.0 * cells - old_ref[field, depth] + courant_ref[depth] * total

    over_depth(deep, body)


def halo_step(depth, base_ref, courant_ref, xa_ref, xb_ref, part_y_ref, odd, coefs):
    sides = from_faces(xa_ref[depth], xb_ref[depth], odd, coefs)
    return [
        base_ref[field, depth] + courant_ref[depth] * (part_y_ref[field, depth] + sides[field]) for field in range(2)
    ]


def over_depth(deep, body):
    def inner(depth, carry):
        body(depth, None)
        return carry

    for depth in range(HALO):
        body(depth, depth)
    lax.fori_loop(HALO, deep - HALO, inner, 0, unroll=8)
    for depth in range(deep - HALO, deep):
        body(depth, depth)


def residual(counts, cells_x, cells_y, radius_sq, signs_ref, sx_ref, sy_ref, records_ref, cell_ref, out_ref, first):
    shots, rows, _ = records_ref.shape
    chunk = min(rows, 64)
    per = 2 * REC_DEV // LANES
    twice = (rows_of((chunk, chunk // 2)) >> 1 == lanes_of((chunk, chunk // 2))).astype(F32).astype(BF16)

    def chunk_step(c, carry):
        cell = cell_ref[pl.ds(pl.multiple_of(c * (chunk // 2), chunk // 2), chunk // 2), :]
        row, column = lax.shift_right_logical(cell, cells_y.bit_length() - 1), cell & (cells_y - 1)
        row, column = [dot(twice, v.astype(F32).astype(BF16)) for v in (row, column)]
        tile = c * (chunk // per) + rows_of((chunk, LANES)) // per
        tile_x, tile_y = tile // counts[1], tile % counts[1]
        pos_x = (tile_x * cells_x).astype(F32) + row
        pos_y = (tile_y * cells_y).astype(F32) + column
        start = pl.multiple_of(c * chunk, chunk)

        def shot_step(shot, sums):
            dx = pos_x - sx_ref[shot].astype(F32)
            dy = pos_y - sy_ref[shot].astype(F32)
            dist = dx * dx + dy * dy
            whole = dist + radius_sq
            inverse = pl.reciprocal(whole, approx=True)
            inverse = inverse * (2.0 - whole * inverse)
            taped = records_ref[shot, pl.ds(start, chunk), :].astype(F32) * (dist * inverse)
            return tuple(s + signs_ref[code, shot].astype(F32) * taped for code, s in enumerate(sums))

        sums = lax.fori_loop(0, shots, shot_step, (jnp.zeros((chunk, LANES), F32),) * 2, unroll=2)
        for t in range(chunk // per):
            both = [s[t * per : (t + 1) * per] for s in sums]
            out_ref[first + c * (chunk // per) + t] = jnp.concatenate(both, axis=0)
        return carry

    lax.fori_loop(0, rows // chunk, chunk_step, 0)


def bring_kernel(
    radius_sq, counts, signs_hbm, sx_hbm, sy_hbm, records_hbm, cell_hbm, now_hbm, old_hbm, courant_hbm,
    now_ref, old_ref, courant_ref, cell_ref, xa_ref, xb_ref, records_ref, signs_ref, sx_ref, sy_ref, sems,
):
    copies = []

    def bring(source, target):
        copy = pltpu.make_async_copy(source, target, sems.at[len(copies)])
        copy.start()
        copies.append(copy)

    for source, target in (
        (cell_hbm, cell_ref), (signs_hbm, signs_ref), (sx_hbm, sx_ref), (sy_hbm, sy_ref), (records_hbm, records_ref),
        (now_hbm, now_ref), (old_hbm, old_ref), (courant_hbm, courant_ref),
    ):
        bring(source, target)
    for copy in copies[:5]:
        copy.wait()
    _, deep, cells_x, cells_y = now_ref.shape
    residual(counts, cells_x, cells_y, radius_sq, signs_ref, sx_ref, sy_ref, records_ref, cell_ref, xa_ref, deep)
    copies[5].wait()
    odd = where_am_i(counts)[0]

    def body(depth, carry):
        first, second = now_ref[0, depth], now_ref[1, depth]
        head, tail = head_rows(first, second), tail_rows(first, second)
        xb_ref[depth] = jnp.where(odd, tail, head)
        xa_ref[depth] = jnp.where(odd, head, tail)
        return carry

    lax.fori_loop(0, deep, body, 0, unroll=8)
    for copy in copies[6:]:
        copy.wait()


def pack_kernel(counts, now_ref, ya_ref, yb_ref):
    pack_columns(now_ref, where_am_i(counts)[1], ya_ref, yb_ref)


def needed_tiles(counts, x, y):
    return (
        (x, y),
        (jnp.minimum(x + 1, counts[0] - 1), y), (jnp.maximum(x - 1, 0), y),
        (x, jnp.minimum(y + 1, counts[1] - 1)), (x, jnp.maximum(y - 1, 0)),
    )


def inject(pieces, samples, cells_y):
    values, hots = [], []
    for res, cells, row_kept, column_kept in pieces:
        for half in range(REC_DEV // LANES):
            row = lax.shift_right_logical(cells[half], cells_y.bit_length() - 1)
            column = cells[half] & (cells_y - 1)
            in_row = (rows_of((SUB, LANES)) == row) & row_kept(rows_of((SUB, LANES)))
            values.append(jnp.concatenate(
                [
                    jnp.where(in_row, res[code * 4 + half * 2 + sample][None, :], 0.0)
                    for code in range(2)
                    for sample in range(samples)
                ],
                axis=0,
            ))
            at = rows_of((cells_y, LANES))
            hots.append(((at == column) & column_kept(at)).astype(F32).astype(BF16))
    values = jnp.concatenate(split(jnp.concatenate(values, axis=1)), axis=0)
    got = lax.dot_general(
        values, jnp.concatenate(hots, axis=1), (((1,), (1,)), ((), ())), preferred_element_type=F32
    )
    count = 2 * samples * SUB
    return got[:count] + got[count : 2 * count] + got[2 * count :]


def second_local_kernel(counts, now_ref, old_ref, courant_ref, before_ref, out_ref):
    del before_ref
    local_step(now_ref, old_ref, courant_ref, out_ref)


def local_kernel(counts, now_ref, old_ref, courant_ref, out_ref):
    local_step(now_ref, old_ref, courant_ref, out_ref)


def packed_sizes(counts):
    return counts[0] * counts[1] // 2, counts[0] * counts[1] // 8


def pack_samples(first, second):
    even = rows_of((SUB, LANES)) % 2 == 0
    return (
        jnp.where(even, first, pltpu.roll(second, 1, 0)),
        jnp.where(even, pltpu.roll(first, SUB - 1, 0), second),
    )


def join_kernel(counts, face_ref, own_ref, other_ref, out_ref, keep_ref):
    faces, at = face_ref.shape[0], own_ref.shape[0] - counts[0] * counts[1]
    at_other = other_ref.shape[0] - counts[0] * counts[1]
    out_ref[:faces] = face_ref[...]
    total = lambda x, y: own_ref[at + x * counts[1] + y] + other_ref[at_other + x * counts[1] + y]
    here = faces
    for high in range(0, counts[0], 4):
        for x in range(high, high + 2):
            for y in range(counts[1]):
                out_ref[here] = pack_samples(total(x, y), total(x + 2, y))[0]
                here += 1
    odd_x, odd_y = [lax.rem(lax.axis_index(axis), 2) for axis in AXES[1:]]
    i = 0
    for high in range(0, counts[0], 4):
        for y in range(0, counts[1], 2):
            x = high + odd_x
            out_ref[here + i] = pack_samples(total(x, y + 1 - odd_y), total(x + 2, y + 1 - odd_y))[1]
            keep_ref[i] = pack_samples(total(x, y + odd_y), total(x + 2, y + odd_y))[1]
            i += 1


def sum_kernel(counts, own_ref, keep_ref, other_ref, before_ref, more_ref, out_ref):
    del before_ref, more_ref
    firsts, seconds = packed_sizes(counts)
    at, at_other = [ref.shape[0] - firsts - seconds for ref in (own_ref, other_ref)]
    out_ref[:firsts] = own_ref[pl.ds(at, firsts)] + other_ref[pl.ds(at_other, firsts)]
    at_keep = keep_ref.shape[0] - seconds
    out_ref[firsts:] = keep_ref[pl.ds(at_keep, seconds)] + other_ref[pl.ds(at_other + firsts, seconds)]


def needed_kernel(counts, own_ref, other_ref, before_ref, ya_ref, yb_ref, out_ref, keep_ref, *handed_on):
    del before_ref, ya_ref, yb_ref, handed_on
    firsts, _ = packed_sizes(counts)
    at_x, at_y = lax.axis_index("gx"), lax.axis_index("gy")
    half = counts[1] // 2
    even = rows_of((SUB, LANES)) % 2 == 0
    total = lambda i: own_ref[i] + other_ref[i]

    def collect(target_ref, y_here):
        for i, (x, y) in enumerate(needed_tiles(counts, at_x, y_here)):
            second_of_pair = lax.rem(lax.div(x, 2), 2) == 1
            got = total((lax.div(x, 4) * 2 + lax.rem(x, 2)) * counts[1] + y)
            got = jnp.where(second_of_pair, pltpu.roll(got, SUB - 1, 0), got)
            if i == 0:
                more = total(firsts + lax.div(x, 4) * half + lax.div(y, 2))
                got = jnp.where(even, got, jnp.where(second_of_pair, more, pltpu.roll(more, 1, 0)))
            target_ref[i] = got

    collect(out_ref, lax.rem(at_y + half, counts[1]))
    collect(keep_ref, at_y)


def middle_kernel(
    counts, base_ref, courant_ref, xa_ref, xb_ref, ya_ref, yb_ref,
    mid_ref, xa_out, xb_out, ya_out, yb_out, part_y_ref,
):
    place = where_am_i(counts)
    deep = base_ref.shape[1]
    halo_y(ya_ref, yb_ref, place, part_y_ref)
    coefs = face_turns(place)

    def body(depth, carry):
        fields = halo_step(depth, base_ref, courant_ref, xa_ref, xb_ref, part_y_ref, place[0], coefs)
        for field in range(2):
            mid_ref[field, depth] = fields[field]
        head, tail = head_rows(*fields), tail_rows(*fields)
        xa_out[depth] = jnp.where(place[0], head, tail)
        xb_out[depth] = jnp.where(place[0], tail, head)
        return carry

    lax.fori_loop(0, deep, body, 0, unroll=8)
    pack_columns(mid_ref, place[1], ya_out, yb_out)


def inject_kernel(counts, keep_ref, res_ref, cell_ref, courant_ref, layer_ref):
    _, _, no_next_x, no_prev_x, no_next_y, no_prev_y = where_am_i(counts)
    _, cells_x, cells_y = courant_ref.shape
    tiles = needed_tiles(counts, lax.axis_index("gx"), lax.axis_index("gy"))
    halves = REC_DEV // LANES
    res = [keep_ref[i] + res_ref[i] for i in range(len(tiles))]
    for i, absent in enumerate((no_next_x, no_prev_x, no_next_y, no_prev_y)):
        res[i + 1] = jnp.where(absent, 0.0, res[i + 1])
    cells = [
        [cell_ref[pl.ds((x * counts[1] + y) * halves + half, 1), :] for half in range(halves)] for x, y in tiles
    ]
    every = lambda at: at >= 0
    own = inject([(res[0], cells[0], every, every)], 2, cells_y)
    beside_x = inject(
        [(res[1], cells[1], lambda at: at < HALO, every), (res[2], cells[2], lambda at: at >= SUB - HALO, every)],
        1, cells_y,
    )
    beside_y = inject(
        [(res[3], cells[3], every, lambda at: at < HALO), (res[4], cells[4], every, lambda at: at >= cells_y - HALO)],
        1, cells_y,
    )
    kept, beside = turns(True), turns(False)
    lane = lanes_of((cells_x, cells_y))
    for field in range(2):
        layer = own[2 * field * cells_x : (2 * field + 1) * cells_x]
        side_x, side_y = [v[field * cells_x : (field + 1) * cells_x] for v in (beside_x, beside_y)]
        total = 3.0 * coef_zero * layer + along_x(layer, kept) + along_x(side_x, beside)
        for step in range(1, HALO + 1):
            up = pltpu.roll(jnp.where(lane < step, side_y, layer), cells_y - step, 1)
            down = pltpu.roll(jnp.where(lane >= cells_y - step, side_y, layer), step, 1)
            total = total + coef_rest[step - 1] * (up + down)
        layer_ref[field] = layer
        second = own[(2 * field + 1) * cells_x : (2 * field + 2) * cells_x]
        layer_ref[2 + field] = 2.0 * layer + courant_ref[RDEPTH] * total + second


def after_kernel(
    counts, base_ref, mid_ref, courant_ref, xa_ref, xb_ref, ya_ref, yb_ref, layer_ref,
    out_ref, mid_out, part_y_ref, held_ref, plane_ref, sems,
):
    place = where_am_i(counts)
    deep = base_ref.shape[1]
    coefs = face_turns(place)
    copies = []

    def send_out(source, target):
        copy = pltpu.make_async_copy(source, target, sems.at[len(copies)])
        copy.start()
        copies.append(copy)

    send_out(mid_ref.at[:, pl.ds(0, RDEPTH)], mid_out.at[:, pl.ds(0, RDEPTH)])
    rest = pl.ds(RDEPTH + 1, deep - RDEPTH - 1)
    send_out(mid_ref.at[:, rest], mid_out.at[:, rest])
    for field in range(2):
        plane_ref[field, 0] = mid_ref[field, RDEPTH] + layer_ref[field]
    plane = pl.ds(RDEPTH, 1)
    send_out(plane_ref, mid_out.at[:, plane])

    halo_y(ya_ref, yb_ref, place, part_y_ref)
    size = deep // 8
    for part in range(8):
        def body(depth, carry):
            fields = halo_step(depth, base_ref, courant_ref, xa_ref, xb_ref, part_y_ref, place[0], coefs)
            for field in range(2):
                held_ref[field, depth] = fields[field]
            return carry

        lax.fori_loop(part * size, (part + 1) * size, body, 0, unroll=8)
        if part == 0:
            for field in range(2):
                held_ref[field, RDEPTH] = held_ref[field, RDEPTH] + layer_ref[2 + field]
                for step in range(1, HALO + 1):
                    change = coef_rest[step - 1] * layer_ref[field]
                    for depth in (RDEPTH - step, RDEPTH + step):
                        if depth >= 0:
                            held_ref[field, depth] = held_ref[field, depth] + courant_ref[depth] * change
        depths = pl.ds(part * size, size)
        send_out(held_ref.at[:, depths], out_ref.at[:, depths])
    for copy in copies:
        copy.wait()


def paired(groups, count_x, count_y, partner):
    index = lambda g, x, y: (g * count_x + x) * count_y + y
    return [
        (index(g, x, y), index(*partner(g, x, y)))
        for g in range(groups)
        for x in range(count_x)
        for y in range(count_y)
    ]


def on_device(wave_now, wave_before, courant, records, signs, source_x, source_y, receiver_cell):
    _, deep, cells_x, cells_y = wave_now.shape
    groups, tiles_x, tiles_y = [lax.axis_size(axis) for axis in AXES]
    counts = (tiles_x, tiles_y)
    total_recv = receiver_cell.shape[0]
    tiles = total_recv // REC_DEV
    shots = records.shape[0]
    span = (cells_x * tiles_x + cells_y * tiles_y) // 4

    perms = functools.partial(paired, groups, tiles_x, tiles_y)
    swap_xa = perms(lambda g, x, y: (g, x ^ 1, y))
    swap_ya = perms(lambda g, x, y: (g, x, y ^ 1))
    swap_xb = perms(
        lambda g, x, y: ((g + groups // 2) % groups, x, y) if x in (0, tiles_x - 1) else (g, ((x + 1) ^ 1) - 1, y)
    )
    swap_yb = perms(lambda g, x, y: (g, x ^ 1, y) if y in (0, tiles_y - 1) else (g, x, ((y + 1) ^ 1) - 1))
    swap_along = {
        "gx": lambda step: perms(lambda g, x, y: (g, x ^ step, y)),
        "gy": lambda step: perms(lambda g, x, y: (g, x, y ^ step)),
    }
    steps = [("gx", 1 << i) for i in range(1, (tiles_x - 1).bit_length())]
    steps += [("gy", 1 << i) for i in range(1, (tiles_y - 1).bit_length() - 1)]
    send = lambda value, pairs: lax.ppermute(value, AXES, pairs)

    face_x = pltpu.VMEM((deep, cells_x, cells_y), F32)
    faces = deep // GROUP
    face_y = pltpu.VMEM((faces, cells_x, cells_y), F32)
    tiles_of = lambda count: pltpu.VMEM((count, SUB, LANES), F32)
    wave = wave_now.shape

    def kernel(body, outs, n_scalar, n_array, scratch=(), out_specs=None, aliases={}, cost=None):
        name = body.__name__.removesuffix("_kernel")

        def call(*args):
            args = args[:n_scalar] + tuple(near_memory(a) for a in args[n_scalar:])
            return pl.pallas_call(
                functools.partial(body, counts),
                out_shape=outs,
                in_specs=[SM] * n_scalar + [VM] * n_array,
                out_specs=out_specs if out_specs is not None else jax.tree.map(lambda _: VM, outs),
                scratch_shapes=scratch,
                input_output_aliases=aliases,
                cost_estimate=cost,
                compiler_params=PARAMS,
                name=name,
            )(*args)

        return call

    wave_v = pltpu.VMEM(wave, F32)
    cell_rows = receiver_cell.reshape(total_recv // LANES, LANES)
    record_rows = records.reshape(shots, 2, total_recv // LANES, LANES).transpose(0, 2, 1, 3)
    record_rows = record_rows.reshape(shots, 2 * total_recv // LANES, LANES)
    far = lambda value: pltpu.with_memory_space_constraint(value, pltpu.HBM)
    left = sum(packed_sizes(counts))
    now, old, speed, cells, xa, xb = pl.pallas_call(
        functools.partial(bring_kernel, float(span * span), counts),
        out_shape=(
            wave_v, wave_v, pltpu.VMEM(courant.shape, F32), pltpu.VMEM(cell_rows.shape, jnp.int32),
            tiles_of(deep + tiles), face_x,
        ),
        in_specs=[pl.BlockSpec(memory_space=pltpu.HBM)] * 8,
        out_specs=(VM,) * 6,
        scratch_shapes=[
            pltpu.VMEM(record_rows.shape, BF16),
            pltpu.SMEM(signs.shape, jnp.int32), pltpu.SMEM((shots,), jnp.int32), pltpu.SMEM((shots,), jnp.int32),
            pltpu.SemaphoreType.DMA((8,)),
        ],
        compiler_params=PARAMS,
        name="bring",
    )(*(far(a) for a in (signs, source_x, source_y, record_rows, cell_rows, wave_now, wave_before, courant)))
    xb_in, xa_in = send(xb, swap_xb), send(xa, swap_xa)
    ya, yb = kernel(pack_kernel, (face_y, face_y), 0, 1)(now)
    yb_in = send(yb, swap_yb)
    partial_res, keep = kernel(join_kernel, (tiles_of(faces + left), tiles_of(packed_sizes(counts)[1])), 0, 3)(
        ya, xa, xa_in
    )
    ya_in = send(partial_res, swap_ya)
    other = ya_in
    base = kernel(local_kernel, wave_v, 0, 3)(now, old, speed)
    for axis, step in steps:
        partial_res = kernel(sum_kernel, tiles_of(left), 0, 5)(partial_res, keep, other, base, cells)
        keep = partial_res
        other = send(partial_res, swap_along[axis](step))
    wave_middle, xa, xb, ya, yb = kernel(middle_kernel, (wave_v, face_x, face_x, face_y, face_y), 0, 6, [wave_v], cost=pl.CostEstimate(flops=10*10**8, bytes_accessed=0, transcendentals=0))(
        base, speed, xa_in, xb_in, ya_in, yb_in
    )
    wanted, keep, ya, yb = kernel(
        needed_kernel, (tiles_of(5), tiles_of(5), face_y, face_y), 0, 5, aliases={3: 2, 4: 3}, cost=pl.CostEstimate(flops=30*10**8, bytes_accessed=0, transcendentals=0)
    )(partial_res, other, wave_middle, ya, yb)
    xb_in, xa_in = send(xb, swap_xb), send(xa, swap_xa)
    res_in = send(wanted, swap_along["gy"](tiles_y // 2))
    ya_in, yb_in = send(ya, swap_ya), send(yb, swap_yb)
    base = kernel(second_local_kernel, wave_v, 0, 4, cost=pl.CostEstimate(flops=0*10**8, bytes_accessed=0, transcendentals=0))(wave_middle, now, speed, keep)
    plane = (2, 1, cells_x, cells_y)
    layers = kernel(inject_kernel, tiles_of(4), 0, 4)(keep, res_in, cells, speed)
    wave_after, wave_middle = kernel(
        after_kernel, (jax.ShapeDtypeStruct(wave, F32),) * 2, 0, 8,
        [wave_v, wave_v, pltpu.VMEM(plane, F32), pltpu.SemaphoreType.DMA((11,))],
        out_specs=(pl.BlockSpec(memory_space=pl.ANY),) * 2,
    )(base, wave_middle, speed, xa_in, xb_in, ya_in, yb_in, layers)
    return (wave_after, wave_middle)


def solution(mesh):
    return jax.shard_map(
        on_device,
        mesh=mesh,
        in_specs=(
            P("group", None, "gx", "gy"),
            P("group", None, "gx", "gy"),
            P("group", "gx", "gy"),
            P(("group", "gx", "gy"), None, None),
            P("group", ("gx", "gy")),
            P(("group", "gx", "gy")),
            P(("group", "gx", "gy")),
            P("group"),
        ),
        out_specs=(P("group", None, "gx", "gy"), P("group", None, "gx", "gy")),
        check_vma=False,
    )
```

```python
import functools

import jax
import jax.numpy as jnp
import ml_dtypes
import numpy as np
from jax import lax
from jax.experimental import pallas as pl
from jax.experimental.pallas import tpu as pltpu
from jax.sharding import PartitionSpec as P

REC_DEV = 256
RDEPTH = 2
HALO = 4
LANES = 128
SUB = 8
GROUP = 16
AXES = ("group", "gx", "gy")
F32, BF16 = jnp.float32, jnp.bfloat16

coef_zero = -205.0 / 72.0
coef_rest = (8.0 / 5.0, -1.0 / 5.0, 8.0 / 315.0, -1.0 / 560.0)
coef_high = [float(np.float32(c).astype(ml_dtypes.bfloat16)) for c in coef_rest]
coef_low = [float(np.float32(c - h).astype(ml_dtypes.bfloat16)) for c, h in zip(coef_rest, coef_high)]

VM = pl.BlockSpec(memory_space=pltpu.VMEM)
SM = pl.BlockSpec(memory_space=pltpu.SMEM)
PARAMS = pltpu.CompilerParams(vmem_limit_bytes=16 * 1024 * 1024)


def near_memory(value):
    return pltpu.with_memory_space_constraint(value, pltpu.VMEM)


def rows_of(shape):
    return lax.broadcasted_iota(jnp.int32, shape, len(shape) - 2)


def lanes_of(shape):
    return lax.broadcasted_iota(jnp.int32, shape, len(shape) - 1)


def dot(left, right):
    return jnp.dot(left, right, preferred_element_type=F32)


def split(value):
    first = value.astype(BF16)
    rest = value - first.astype(F32)
    second = rest.astype(BF16)
    return first, second, (rest - second.astype(F32)).astype(BF16)


def pick(step, coefs):
    out = jnp.zeros(step.shape, F32)
    for m in range(1, HALO + 1):
        out = jnp.where(step == m, coefs[m - 1], out)
    return out.astype(BF16)


def band(coefs):
    shape = (LANES, LANES)
    return pick(jnp.abs(rows_of(shape) - lanes_of(shape)), coefs)


def side():
    shape = (LANES, LANES)
    c = rows_of(shape) & 7
    j = lanes_of(shape)
    step = jnp.where(c < HALO, j + HALO - c, LANES + c - HALO - j)
    return jnp.where(rows_of(shape) < LANES // 2, pick(step, coef_high).astype(F32), pick(step, coef_low).astype(F32)).astype(BF16)


def pack_columns(ref, odd, ya_ref, yb_ref):
    lane_group = lanes_of((SUB, LANES)) >> 3
    low = (lanes_of((SUB, LANES)) & 7) < HALO
    pairs = ref.shape[1] // GROUP // 2

    def step(pair, carry):
        for field in range(2):
            both = []
            for group in range(2):
                tile = None
                for q in range(GROUP):
                    cells = ref[field, (pair * 2 + group) * GROUP + q]
                    turned = pltpu.roll(cells, (q * 2 * HALO + HALO) % LANES, 1)
                    tile = turned if tile is None else jnp.where(lane_group == q, turned, tile)
                both.append(tile)
            last = jnp.where(low, both[0], pltpu.roll(both[1], HALO, 1))
            first = jnp.where(low, pltpu.roll(both[0], LANES - HALO, 1), both[1])
            ya_ref[field * pairs + pair] = jnp.where(odd, first, last)
            yb_ref[field * pairs + pair] = jnp.where(odd, last, first)
        return carry

    lax.fori_loop(0, pairs, step, 0)


def sides_y(ya, yb, odd, no_next, no_prev):
    after = jnp.where(no_next, 0.0, jnp.where(odd, yb, ya))
    before = jnp.where(no_prev, 0.0, jnp.where(odd, ya, yb))
    low = (lanes_of(ya.shape) & 7) < HALO
    return (
        jnp.where(low, before, pltpu.roll(after, HALO, 1)),
        jnp.where(low, pltpu.roll(before, LANES - HALO, 1), after),
    )


def local_y(cells, high, low):
    first, second, _ = split(cells)
    return dot(jnp.concatenate([first, second, first], axis=1), jnp.concatenate([high, high, low], axis=0))


def halo_y(ya_ref, yb_ref, place, out_ref):
    weights = side()
    _, odd, _, _, no_next, no_prev = place
    groups = out_ref.shape[1] // GROUP
    lane_group = lanes_of((SUB, LANES)) >> 3
    half, quarter = GROUP // 2, GROUP // 4
    for field in range(2):
        rows = []
        for pair in range(groups // 2):
            at = field * (groups // 2) + pair
            for beside in sides_y(ya_ref[at], yb_ref[at], odd, no_next, no_prev):
                first = beside.astype(BF16).astype(F32)
                second = (beside - first).astype(BF16).astype(F32)
                turned = pltpu.roll(first, LANES // 2, 1)
                seconds = [pltpu.roll(second, turn, 1) for turn in (LANES // 4, LANES - LANES // 4)]
                for q in range(GROUP):
                    other = (q + half) % GROUP
                    at_second = (q % half + quarter) % half
                    tile = jnp.where(lane_group == q, first, 0.0)
                    tile = jnp.where(lane_group == other, turned, tile)
                    turn = 0 if (at_second - q) % GROUP == quarter else 1
                    rows.append(jnp.where(lane_group == at_second, seconds[turn], tile))
        total = dot(jnp.concatenate(rows, axis=0).astype(BF16), weights)
        out_ref[field] = total.reshape(groups * GROUP, SUB, LANES)


def where_am_i(counts):
    at_x, at_y = lax.axis_index("gx"), lax.axis_index("gy")
    return (
        lax.rem(at_x, 2) == 1, lax.rem(at_y, 2) == 1,
        at_x == counts[0] - 1, at_x == 0, at_y == counts[1] - 1, at_y == 0,
    )


def head_rows(first, second):
    return jnp.where(rows_of(first.shape) < HALO, first, pltpu.roll(second, HALO, 0))


def tail_rows(first, second):
    return jnp.where(rows_of(first.shape) < HALO, pltpu.roll(first, HALO, 0), second)


def face_turns(place):
    _, _, no_next, no_prev, _, _ = place
    row = rows_of((SUB, LANES)) % HALO
    after = [jnp.where((row >= d) & jnp.logical_not(no_next), coef_rest[HALO - 1 - d], 0.0) for d in range(HALO)]
    before = [jnp.where((row + d < HALO) & jnp.logical_not(no_prev), coef_rest[HALO - 1 - d], 0.0) for d in range(HALO)]
    return after, before


def from_faces(xa, xb, odd, coefs):
    after, before = jnp.where(odd, xb, xa), jnp.where(odd, xa, xb)
    after_sum, before_sum = coefs[0][0] * after, coefs[1][0] * before
    for d in range(1, HALO):
        after_sum = after_sum + coefs[0][d] * pltpu.roll(after, d, 0)
        before_sum = before_sum + coefs[1][d] * pltpu.roll(before, SUB - d, 0)
    low = rows_of(after.shape) < HALO
    return (
        jnp.where(low, before_sum, pltpu.roll(after_sum, HALO, 0)),
        jnp.where(low, pltpu.roll(before_sum, HALO, 0), after_sum),
    )


def turns(kept):
    row = rows_of((SUB, LANES))
    out = []
    for turn in range(1, SUB):
        coef = coef_rest[min(turn, SUB - turn) - 1]
        inside = row >= turn if turn < HALO else row < turn if turn > HALO else row >= 0
        out.append(jnp.where(inside if kept else jnp.logical_not(inside) | (turn == HALO), coef, 0.0))
    return out


def along_x(cells, coefs):
    total = coefs[0] * pltpu.roll(cells, 1, 0)
    for turn in range(2, SUB):
        total = total + coefs[turn - 1] * pltpu.roll(cells, turn, 0)
    return total


def local_step(now_ref, old_ref, courant_ref, out_ref):
    deep = now_ref.shape[1]
    high, low = band(coef_high), band(coef_low)
    for field in range(2):
        cells = now_ref[field].reshape(deep * SUB, LANES)
        out_ref[field] = local_y(cells, high, low).reshape(deep, SUB, LANES)
    coefs = turns(True)

    def body(depth, static_depth):
        for field in range(2):
            cells = now_ref[field, depth]
            total = 3.0 * coef_zero * cells + out_ref[field, depth] + along_x(cells, coefs)
            for step in range(1, HALO + 1):
                near = None
                if static_depth is None or static_depth + step < deep:
                    near = now_ref[field, depth + step]
                if static_depth is None or static_depth >= step:
                    before = now_ref[field, depth - step]
                    near = before if near is None else near + before
                total = total + coef_rest[step - 1] * near
            out_ref[field, depth] = 2.0 * cells - old_ref[field, depth] + courant_ref[depth] * total

    over_depth(deep, body)


def halo_step(depth, base_ref, courant_ref, xa_ref, xb_ref, part_y_ref, odd, coefs):
    sides = from_faces(xa_ref[depth], xb_ref[depth], odd, coefs)
    return [
        base_ref[field, depth] + courant_ref[depth] * (part_y_ref[field, depth] + sides[field]) for field in range(2)
    ]


def over_depth(deep, body):
    def inner(depth, carry):
        body(depth, None)
        return carry

    for depth in range(HALO):
        body(depth, depth)
    lax.fori_loop(HALO, deep - HALO, inner, 0, unroll=8)
    for depth in range(deep - HALO, deep):
        body(depth, depth)


def residual(counts, cells_x, cells_y, radius_sq, signs_ref, sx_ref, sy_ref, records_ref, cell_ref, out_ref, first):
    shots, rows, _ = records_ref.shape
    chunk = min(rows, 64)
    per = 2 * REC_DEV // LANES
    twice = (rows_of((chunk, chunk // 2)) >> 1 == lanes_of((chunk, chunk // 2))).astype(F32).astype(BF16)

    def chunk_step(c, carry):
        cell = cell_ref[pl.ds(pl.multiple_of(c * (chunk // 2), chunk // 2), chunk // 2), :]
        row, column = lax.shift_right_logical(cell, cells_y.bit_length() - 1), cell & (cells_y - 1)
        row, column = [dot(twice, v.astype(F32).astype(BF16)) for v in (row, column)]
        tile = c * (chunk // per) + rows_of((chunk, LANES)) // per
        tile_x, tile_y = tile // counts[1], tile % counts[1]
        pos_x = (tile_x * cells_x).astype(F32) + row
        pos_y = (tile_y * cells_y).astype(F32) + column
        start = pl.multiple_of(c * chunk, chunk)

        def shot_step(shot, sums):
            dx = pos_x - sx_ref[shot].astype(F32)
            dy = pos_y - sy_ref[shot].astype(F32)
            dist = dx * dx + dy * dy
            whole = dist + radius_sq
            inverse = pl.reciprocal(whole, approx=True)
            inverse = inverse * (2.0 - whole * inverse)
            taped = records_ref[shot, pl.ds(start, chunk), :].astype(F32) * (dist * inverse)
            return tuple(s + signs_ref[code, shot].astype(F32) * taped for code, s in enumerate(sums))

        sums = lax.fori_loop(0, shots, shot_step, (jnp.zeros((chunk, LANES), F32),) * 2, unroll=8)
        for t in range(chunk // per):
            both = [s[t * per : (t + 1) * per] for s in sums]
            out_ref[first + c * (chunk // per) + t] = jnp.concatenate(both, axis=0)
        return carry

    lax.fori_loop(0, rows // chunk, chunk_step, 0)


def bring_kernel(
    radius_sq, counts, signs_hbm, sx_hbm, sy_hbm, records_hbm, cell_hbm, now_hbm, old_hbm, courant_hbm,
    now_ref, old_ref, courant_ref, cell_ref, xa_ref, xb_ref, records_ref, signs_ref, sx_ref, sy_ref, sems,
):
    copies = []

    def bring(source, target):
        copy = pltpu.make_async_copy(source, target, sems.at[len(copies)])
        copy.start()
        copies.append(copy)

    for source, target in (
        (cell_hbm, cell_ref), (signs_hbm, signs_ref), (sx_hbm, sx_ref), (sy_hbm, sy_ref), (records_hbm, records_ref),
        (now_hbm, now_ref), (old_hbm, old_ref), (courant_hbm, courant_ref),
    ):
        bring(source, target)
    for copy in copies[:5]:
        copy.wait()
    _, deep, cells_x, cells_y = now_ref.shape
    residual(counts, cells_x, cells_y, radius_sq, signs_ref, sx_ref, sy_ref, records_ref, cell_ref, xa_ref, deep)
    copies[5].wait()
    odd = where_am_i(counts)[0]

    def body(depth, carry):
        first, second = now_ref[0, depth], now_ref[1, depth]
        head, tail = head_rows(first, second), tail_rows(first, second)
        xb_ref[depth] = jnp.where(odd, tail, head)
        xa_ref[depth] = jnp.where(odd, head, tail)
        return carry

    lax.fori_loop(0, deep, body, 0, unroll=8)
    for copy in copies[6:]:
        copy.wait()


def pack_kernel(counts, now_ref, ya_ref, yb_ref):
    pack_columns(now_ref, where_am_i(counts)[1], ya_ref, yb_ref)


def needed_tiles(counts, x, y):
    return (
        (x, y),
        (jnp.minimum(x + 1, counts[0] - 1), y), (jnp.maximum(x - 1, 0), y),
        (x, jnp.minimum(y + 1, counts[1] - 1)), (x, jnp.maximum(y - 1, 0)),
    )


def inject(pieces, samples, cells_y):
    values, hots = [], []
    for res, cells, row_kept, column_kept in pieces:
        for half in range(REC_DEV // LANES):
            row = lax.shift_right_logical(cells[half], cells_y.bit_length() - 1)
            column = cells[half] & (cells_y - 1)
            in_row = (rows_of((SUB, LANES)) == row) & row_kept(rows_of((SUB, LANES)))
            values.append(jnp.concatenate(
                [
                    jnp.where(in_row, res[code * 4 + half * 2 + sample][None, :], 0.0)
                    for code in range(2)
                    for sample in range(samples)
                ],
                axis=0,
            ))
            at = rows_of((cells_y, LANES))
            hots.append(((at == column) & column_kept(at)).astype(F32).astype(BF16))
    values = jnp.concatenate(split(jnp.concatenate(values, axis=1)), axis=0)
    got = lax.dot_general(
        values, jnp.concatenate(hots, axis=1), (((1,), (1,)), ((), ())), preferred_element_type=F32
    )
    count = 2 * samples * SUB
    return got[:count] + got[count : 2 * count] + got[2 * count :]


def second_local_kernel(counts, now_ref, old_ref, courant_ref, before_ref, out_ref):
    del before_ref
    local_step(now_ref, old_ref, courant_ref, out_ref)


def local_kernel(counts, now_ref, old_ref, courant_ref, out_ref):
    local_step(now_ref, old_ref, courant_ref, out_ref)


def block_parts(counts, block):
    pairs, own = counts[0] // 2, counts[0] // 4
    return pairs, own, block * pairs, block * pairs + 2 * own, block * pairs + 2 * own + block * own


def pack_samples(first, second):
    even = rows_of((SUB, LANES)) % 2 == 0
    return (
        jnp.where(even, first, pltpu.roll(second, 1, 0)),
        jnp.where(even, pltpu.roll(first, SUB - 1, 0), second),
    )


def outside(counts, start, block):
    return jnp.minimum(start + block, counts[1] - 1), jnp.maximum(start - 1, 0)


def partner_block(at_y, half):
    mine = lax.div(at_y, half) * half
    return mine, lax.div(at_y, 2 * half) * (4 * half) + half - mine


def join_kernel(counts, own_ref, other_ref, before_ref, out_ref, keep_ref):
    del before_ref
    at_x, at_y = lax.axis_index("gx"), lax.axis_index("gy")
    at, at_other = [ref.shape[0] - counts[0] * counts[1] for ref in (own_ref, other_ref)]
    half = counts[1] // 2
    pairs, own, at_outside, at_second, _ = block_parts(counts, half)
    total = lambda x, y: own_ref[at + x * counts[1] + y] + other_ref[at_other + x * counts[1] + y]
    row = lambda m: 4 * m + lax.rem(at_x, 2)
    mine, partner = partner_block(at_y, half)
    for ref, start in ((keep_ref, mine), (out_ref, partner)):
        for i in range(half):
            for j in range(pairs):
                x = j // 2 * 4 + j % 2
                ref[i * pairs + j] = pack_samples(total(x, start + i), total(x + 2, start + i))[0]
            for m in range(own):
                ref[at_second + i * own + m] = pack_samples(total(row(m), start + i), total(row(m) + 2, start + i))[1]
        for side, y in enumerate(outside(counts, start, half)):
            for m in range(own):
                ref[at_outside + side * own + m] = pack_samples(total(row(m), y), total(row(m) + 2, y))[0]


def fold_kernel(block, counts, own_ref, other_ref, out_ref, keep_ref):
    at_x, at_y = lax.axis_index("gx"), lax.axis_index("gy")
    half = block // 2
    pairs, own, at_outside, at_second, _ = block_parts(counts, block)
    _, _, new_outside, new_second, _ = block_parts(counts, half)
    total = lambda i: own_ref[i] + other_ref[i]
    first = lax.div(at_y, block) * block
    mine, partner = partner_block(at_y, half)
    for ref, start in ((keep_ref, mine), (out_ref, partner)):
        for i in range(half):
            for j in range(pairs):
                ref[i * pairs + j] = total((start - first + i) * pairs + j)
            for m in range(own):
                ref[new_second + i * own + m] = total(at_second + (start - first + i) * own + m)
        for side, y in enumerate(outside(counts, start, half)):
            for m in range(own):
                inside = (y - first) * pairs + 2 * m + lax.rem(at_x, 2)
                after, before = at_outside + m, at_outside + own + m
                ref[new_outside + side * own + m] = total(
                    jnp.where(y < first, before, jnp.where(y >= first + block, after, inside))
                )


def sum_kernel(counts, own_ref, other_ref, before_ref, out_ref):
    del before_ref
    out_ref[...] = own_ref[...] + other_ref[...]


def needed_kernel(counts, own_ref, other_ref, before_ref, ya_ref, yb_ref, out_ref, keep_ref, yb_out):
    del before_ref, yb_ref, yb_out
    at_x, at_y = lax.axis_index("gx"), lax.axis_index("gy")
    pairs, own, at_outside, at_second, _ = block_parts(counts, 2)
    even = rows_of((SUB, LANES)) % 2 == 0
    total = lambda i: own_ref[i] + other_ref[i]
    is_second = lambda x: lax.rem(lax.div(x, 2), 2) == 1
    pick_first = lambda got, x: jnp.where(is_second(x), pltpu.roll(got, SUB - 1, 0), got)
    faces = ya_ref.shape[0]
    out_ref[:faces] = ya_ref[...]

    def inside(x, column):
        return pick_first(total(column * pairs + lax.div(x, 4) * 2 + lax.rem(x, 2)), x)

    def collect(target_ref, first, column):
        more = total(at_second + column * own + lax.div(at_x, 4))
        more = jnp.where(is_second(at_x), more, pltpu.roll(more, 1, 0))
        target_ref[first] = jnp.where(even, inside(at_x, column), more)
        beside = inside(jnp.minimum(at_x + 1, counts[0] - 1), column), inside(jnp.maximum(at_x - 1, 0), column)
        target_ref[first + 1] = jnp.where(even, beside[0], pltpu.roll(beside[1], 1, 0))
        after, before = [pick_first(total(at_outside + side * own + lax.div(at_x, 4)), at_x) for side in range(2)]
        after = jnp.where(column == 0, inside(at_x, 1), after)
        before = jnp.where(column == 0, before, inside(at_x, 0))
        target_ref[first + 2] = jnp.where(even, after, pltpu.roll(before, 1, 0))

    column = lax.rem(at_y, 2)
    collect(out_ref, faces, 1 - column)
    collect(keep_ref, 0, column)


def middle_kernel(
    counts, base_ref, courant_ref, xa_ref, xb_ref, ya_ref, yb_ref,
    mid_ref, xa_out, xb_out, ya_out, yb_out, part_y_ref,
):
    place = where_am_i(counts)
    deep = base_ref.shape[1]
    halo_y(ya_ref, yb_ref, place, part_y_ref)
    coefs = face_turns(place)

    def body(depth, carry):
        fields = halo_step(depth, base_ref, courant_ref, xa_ref, xb_ref, part_y_ref, place[0], coefs)
        for field in range(2):
            mid_ref[field, depth] = fields[field]
        head, tail = head_rows(*fields), tail_rows(*fields)
        xa_out[depth] = jnp.where(place[0], head, tail)
        xb_out[depth] = jnp.where(place[0], tail, head)
        return carry

    lax.fori_loop(0, deep, body, 0, unroll=8)
    pack_columns(mid_ref, place[1], ya_out, yb_out)


def inject_kernel(counts, keep_ref, res_ref, cell_ref, courant_ref, layer_ref):
    _, _, no_next_x, no_prev_x, no_next_y, no_prev_y = where_am_i(counts)
    _, cells_x, cells_y = courant_ref.shape
    tiles = needed_tiles(counts, lax.axis_index("gx"), lax.axis_index("gy"))
    halves = REC_DEV // LANES
    at = res_ref.shape[0] - 3
    own, *pairs = [keep_ref[i] + res_ref[at + i] for i in range(3)]
    res = [own] + [half for pair in pairs for half in (pair, pltpu.roll(pair, SUB - 1, 0))]
    for i, absent in enumerate((no_next_x, no_prev_x, no_next_y, no_prev_y)):
        res[i + 1] = jnp.where(absent, 0.0, res[i + 1])
    cells = [
        [cell_ref[pl.ds((x * counts[1] + y) * halves + half, 1), :] for half in range(halves)] for x, y in tiles
    ]
    every = lambda at: at >= 0
    own = inject([(res[0], cells[0], every, every)], 2, cells_y)
    beside_x = inject(
        [(res[1], cells[1], lambda at: at < HALO, every), (res[2], cells[2], lambda at: at >= SUB - HALO, every)],
        1, cells_y,
    )
    beside_y = inject(
        [(res[3], cells[3], every, lambda at: at < HALO), (res[4], cells[4], every, lambda at: at >= cells_y - HALO)],
        1, cells_y,
    )
    kept, beside = turns(True), turns(False)
    lane = lanes_of((cells_x, cells_y))
    for field in range(2):
        layer = own[2 * field * cells_x : (2 * field + 1) * cells_x]
        side_x, side_y = [v[field * cells_x : (field + 1) * cells_x] for v in (beside_x, beside_y)]
        total = 3.0 * coef_zero * layer + along_x(layer, kept) + along_x(side_x, beside)
        for step in range(1, HALO + 1):
            up = pltpu.roll(jnp.where(lane < step, side_y, layer), cells_y - step, 1)
            down = pltpu.roll(jnp.where(lane >= cells_y - step, side_y, layer), step, 1)
            total = total + coef_rest[step - 1] * (up + down)
        layer_ref[field] = layer
        second = own[(2 * field + 1) * cells_x : (2 * field + 2) * cells_x]
        layer_ref[2 + field] = 2.0 * layer + courant_ref[RDEPTH] * total + second


def after_kernel(
    counts, base_ref, mid_ref, courant_ref, xa_ref, xb_ref, ya_ref, yb_ref, layer_ref,
    out_ref, mid_out, part_y_ref, held_ref, plane_ref, sems,
):
    place = where_am_i(counts)
    deep = base_ref.shape[1]
    coefs = face_turns(place)
    copies = []

    def send_out(source, target):
        copy = pltpu.make_async_copy(source, target, sems.at[len(copies)])
        copy.start()
        copies.append(copy)

    send_out(mid_ref.at[:, pl.ds(0, RDEPTH)], mid_out.at[:, pl.ds(0, RDEPTH)])
    rest = pl.ds(RDEPTH + 1, deep - RDEPTH - 1)
    send_out(mid_ref.at[:, rest], mid_out.at[:, rest])
    for field in range(2):
        plane_ref[field, 0] = mid_ref[field, RDEPTH] + layer_ref[field]
    plane = pl.ds(RDEPTH, 1)
    send_out(plane_ref, mid_out.at[:, plane])

    halo_y(ya_ref, yb_ref, place, part_y_ref)
    size = deep // 8
    for part in range(8):
        def body(depth, carry):
            fields = halo_step(depth, base_ref, courant_ref, xa_ref, xb_ref, part_y_ref, place[0], coefs)
            for field in range(2):
                held_ref[field, depth] = fields[field]
            return carry

        lax.fori_loop(part * size, (part + 1) * size, body, 0, unroll=8)
        if part == 0:
            for field in range(2):
                held_ref[field, RDEPTH] = held_ref[field, RDEPTH] + layer_ref[2 + field]
                for step in range(1, HALO + 1):
                    change = coef_rest[step - 1] * layer_ref[field]
                    for depth in (RDEPTH - step, RDEPTH + step):
                        if depth >= 0:
                            held_ref[field, depth] = held_ref[field, depth] + courant_ref[depth] * change
        depths = pl.ds(part * size, size)
        send_out(held_ref.at[:, depths], out_ref.at[:, depths])
    for copy in copies:
        copy.wait()


def paired(groups, count_x, count_y, partner):
    index = lambda g, x, y: (g * count_x + x) * count_y + y
    return [
        (index(g, x, y), index(*partner(g, x, y)))
        for g in range(groups)
        for x in range(count_x)
        for y in range(count_y)
    ]


def on_device(wave_now, wave_before, courant, records, signs, source_x, source_y, receiver_cell):
    _, deep, cells_x, cells_y = wave_now.shape
    groups, tiles_x, tiles_y = [lax.axis_size(axis) for axis in AXES]
    counts = (tiles_x, tiles_y)
    total_recv = receiver_cell.shape[0]
    tiles = total_recv // REC_DEV
    shots = records.shape[0]
    span = (cells_x * tiles_x + cells_y * tiles_y) // 4

    perms = functools.partial(paired, groups, tiles_x, tiles_y)
    swap_xa = perms(lambda g, x, y: (g, x ^ 1, y))
    swap_ya = perms(lambda g, x, y: (g, x, y ^ 1))
    swap_xb = perms(
        lambda g, x, y: ((g + groups // 2) % groups, x, y) if x in (0, tiles_x - 1) else (g, ((x + 1) ^ 1) - 1, y)
    )
    swap_yb = perms(lambda g, x, y: (g, x ^ 1, y) if y in (0, tiles_y - 1) else (g, x, ((y + 1) ^ 1) - 1))
    swap_along = {
        "gx": lambda step: perms(lambda g, x, y: (g, x ^ step, y)),
        "gy": lambda step: perms(lambda g, x, y: (g, x, y ^ step)),
    }
    steps_x = [1 << i for i in range(1, (tiles_x - 1).bit_length())]
    blocks = [tiles_y >> i for i in range(1, (tiles_y - 1).bit_length())]
    send = lambda value, pairs: lax.ppermute(value, AXES, pairs)

    face_x = pltpu.VMEM((deep, cells_x, cells_y), F32)
    faces = deep // GROUP
    face_y = pltpu.VMEM((faces, cells_x, cells_y), F32)
    tiles_of = lambda count: pltpu.VMEM((count, SUB, LANES), F32)
    wave = wave_now.shape

    def kernel(body, outs, n_scalar, n_array, scratch=(), out_specs=None, aliases={}, cost=None):
        name = getattr(body, "func", body).__name__.removesuffix("_kernel")

        def call(*args):
            args = args[:n_scalar] + tuple(near_memory(a) for a in args[n_scalar:])
            return pl.pallas_call(
                functools.partial(body, counts),
                out_shape=outs,
                in_specs=[SM] * n_scalar + [VM] * n_array,
                out_specs=out_specs if out_specs is not None else jax.tree.map(lambda _: VM, outs),
                scratch_shapes=scratch,
                input_output_aliases=aliases,
                cost_estimate=cost,
                compiler_params=PARAMS,
                name=name,
            )(*args)

        return call

    wave_v = pltpu.VMEM(wave, F32)
    cell_rows = receiver_cell.reshape(total_recv // LANES, LANES)
    record_rows = records.reshape(shots, 2, total_recv // LANES, LANES).transpose(0, 2, 1, 3)
    record_rows = record_rows.reshape(shots, 2 * total_recv // LANES, LANES)
    far = lambda value: pltpu.with_memory_space_constraint(value, pltpu.HBM)
    now, old, speed, cells, xa, xb = pl.pallas_call(
        functools.partial(bring_kernel, float(span * span), counts),
        out_shape=(
            wave_v, wave_v, pltpu.VMEM(courant.shape, F32), pltpu.VMEM(cell_rows.shape, jnp.int32),
            tiles_of(deep + tiles), face_x,
        ),
        in_specs=[pl.BlockSpec(memory_space=pltpu.HBM)] * 8,
        out_specs=(VM,) * 6,
        scratch_shapes=[
            pltpu.VMEM(record_rows.shape, BF16),
            pltpu.SMEM(signs.shape, jnp.int32), pltpu.SMEM((shots,), jnp.int32), pltpu.SMEM((shots,), jnp.int32),
            pltpu.SemaphoreType.DMA((8,)),
        ],
        compiler_params=PARAMS,
        name="bring",
    )(*(far(a) for a in (signs, source_x, source_y, record_rows, cell_rows, wave_now, wave_before, courant)))
    xb_in, xa_in = send(xb, swap_xb), send(xa, swap_xa)
    ya, yb = kernel(pack_kernel, (face_y, face_y), 0, 1)(now)
    yb_in = send(yb, swap_yb)
    sums = tiles_of(block_parts(counts, blocks[0])[-1])
    wanted, partial_res = kernel(join_kernel, (sums, sums), 0, 3)(xa, xa_in, ya)
    other = send(wanted, swap_along["gy"](blocks[0]))
    for block in blocks[:-1]:
        sums = tiles_of(block_parts(counts, block // 2)[-1])
        fold = functools.partial(fold_kernel, block)
        wanted, partial_res = kernel(fold, (sums, sums), 0, 2)(partial_res, other)
        other = send(wanted, swap_along["gy"](block // 2))
    ya_in = send(ya, swap_ya)
    base = kernel(local_kernel, wave_v, 0, 3)(now, old, speed)
    for step in steps_x:
        partial_res = kernel(sum_kernel, sums, 0, 3)(partial_res, other, base)
        other = send(partial_res, swap_along["gx"](step))
    wave_middle, xa, xb, ya, yb = kernel(middle_kernel, (wave_v, face_x, face_x, face_y, face_y), 0, 6, [wave_v], cost=pl.CostEstimate(flops=10*10**8, bytes_accessed=0, transcendentals=0))(
        base, speed, xa_in, xb_in, ya_in, yb_in
    )
    y_more, keep, yb = kernel(
        needed_kernel, (tiles_of(faces + 3), tiles_of(3), face_y), 0, 5, aliases={4: 2}, cost=pl.CostEstimate(flops=30*10**8, bytes_accessed=0, transcendentals=0)
    )(partial_res, other, wave_middle, ya, yb)
    xb_in, xa_in = send(xb, swap_xb), send(xa, swap_xa)
    ya_in, yb_in = send(y_more, swap_ya), send(yb, swap_yb)
    base = kernel(second_local_kernel, wave_v, 0, 4, cost=pl.CostEstimate(flops=0*10**8, bytes_accessed=0, transcendentals=0))(wave_middle, now, speed, keep)
    plane = (2, 1, cells_x, cells_y)
    layers = kernel(inject_kernel, tiles_of(4), 0, 4)(keep, ya_in, cells, speed)
    wave_after, wave_middle = kernel(
        after_kernel, (jax.ShapeDtypeStruct(wave, F32),) * 2, 0, 8,
        [wave_v, wave_v, pltpu.VMEM(plane, F32), pltpu.SemaphoreType.DMA((11,))],
        out_specs=(pl.BlockSpec(memory_space=pl.ANY),) * 2,
    )(base, wave_middle, speed, xa_in, xb_in, ya_in, yb_in, layers)
    return (wave_after, wave_middle)


def solution(mesh):
    return jax.shard_map(
        on_device,
        mesh=mesh,
        in_specs=(
            P("group", None, "gx", "gy"),
            P("group", None, "gx", "gy"),
            P("group", "gx", "gy"),
            P(("group", "gx", "gy"), None, None),
            P("group", ("gx", "gy")),
            P(("group", "gx", "gy")),
            P(("group", "gx", "gy")),
            P("group"),
        ),
        out_specs=(P("group", None, "gx", "gy"), P("group", None, "gx", "gy")),
        check_vma=False,
    )
```

```python
import functools

import jax
import jax.numpy as jnp
import ml_dtypes
import numpy as np
from jax import lax
from jax.experimental import pallas as pl
from jax.experimental.pallas import tpu as pltpu
from jax.sharding import PartitionSpec as P

REC_DEV = 256
RDEPTH = 2
HALO = 4
LANES = 128
SUB = 8
GROUP = 16
AXES = ("group", "gx", "gy")
F32, BF16 = jnp.float32, jnp.bfloat16

coef_zero = -205.0 / 72.0
coef_rest = (8.0 / 5.0, -1.0 / 5.0, 8.0 / 315.0, -1.0 / 560.0)
coef_high = [float(np.float32(c).astype(ml_dtypes.bfloat16)) for c in coef_rest]
coef_low = [float(np.float32(c - h).astype(ml_dtypes.bfloat16)) for c, h in zip(coef_rest, coef_high)]

VM = pl.BlockSpec(memory_space=pltpu.VMEM)
SM = pl.BlockSpec(memory_space=pltpu.SMEM)
PARAMS = pltpu.CompilerParams(vmem_limit_bytes=16 * 1024 * 1024)


def near_memory(value):
    return pltpu.with_memory_space_constraint(value, pltpu.VMEM)


def rows_of(shape):
    return lax.broadcasted_iota(jnp.int32, shape, len(shape) - 2)


def lanes_of(shape):
    return lax.broadcasted_iota(jnp.int32, shape, len(shape) - 1)


def dot(left, right):
    return jnp.dot(left, right, preferred_element_type=F32)


def split(value):
    first = value.astype(BF16)
    rest = value - first.astype(F32)
    second = rest.astype(BF16)
    return first, second, (rest - second.astype(F32)).astype(BF16)


def pick(step, coefs):
    out = jnp.zeros(step.shape, F32)
    for m in range(1, HALO + 1):
        out = jnp.where(step == m, coefs[m - 1], out)
    return out.astype(BF16)


def band(coefs):
    shape = (LANES, LANES)
    return pick(jnp.abs(rows_of(shape) - lanes_of(shape)), coefs)


def side():
    shape = (LANES, LANES)
    c = rows_of(shape) & 7
    j = lanes_of(shape)
    step = jnp.where(c < HALO, j + HALO - c, LANES + c - HALO - j)
    return jnp.where(rows_of(shape) < LANES // 2, pick(step, coef_high).astype(F32), pick(step, coef_low).astype(F32)).astype(BF16)


def pack_columns(ref, odd, ya_ref, yb_ref):
    lane_group = lanes_of((SUB, LANES)) >> 3
    low = (lanes_of((SUB, LANES)) & 7) < HALO
    pairs = ref.shape[1] // GROUP // 2

    def step(pair, carry):
        for field in range(2):
            both = []
            for group in range(2):
                tile = None
                for q in range(GROUP):
                    cells = ref[field, (pair * 2 + group) * GROUP + q]
                    turned = pltpu.roll(cells, (q * 2 * HALO + HALO) % LANES, 1)
                    tile = turned if tile is None else jnp.where(lane_group == q, turned, tile)
                both.append(tile)
            last = jnp.where(low, both[0], pltpu.roll(both[1], HALO, 1))
            first = jnp.where(low, pltpu.roll(both[0], LANES - HALO, 1), both[1])
            ya_ref[field * pairs + pair] = jnp.where(odd, first, last)
            yb_ref[field * pairs + pair] = jnp.where(odd, last, first)
        return carry

    lax.fori_loop(0, pairs, step, 0)


def sides_y(ya, yb, odd, no_next, no_prev):
    after = jnp.where(no_next, 0.0, jnp.where(odd, yb, ya))
    before = jnp.where(no_prev, 0.0, jnp.where(odd, ya, yb))
    low = (lanes_of(ya.shape) & 7) < HALO
    return (
        jnp.where(low, before, pltpu.roll(after, HALO, 1)),
        jnp.where(low, pltpu.roll(before, LANES - HALO, 1), after),
    )


def local_y(cells, high, low):
    first, second, _ = split(cells)
    return dot(jnp.concatenate([first, second, first], axis=1), jnp.concatenate([high, high, low], axis=0))


def halo_y(ya_ref, yb_ref, place, out_ref):
    weights = side()
    _, odd, _, _, no_next, no_prev = place
    groups = out_ref.shape[1] // GROUP
    lane_group = lanes_of((SUB, LANES)) >> 3
    half, quarter = GROUP // 2, GROUP // 4
    for field in range(2):
        rows = []
        for pair in range(groups // 2):
            at = field * (groups // 2) + pair
            for beside in sides_y(ya_ref[at], yb_ref[at], odd, no_next, no_prev):
                first = beside.astype(BF16).astype(F32)
                second = (beside - first).astype(BF16).astype(F32)
                turned = pltpu.roll(first, LANES // 2, 1)
                seconds = [pltpu.roll(second, turn, 1) for turn in (LANES // 4, LANES - LANES // 4)]
                for q in range(GROUP):
                    other = (q + half) % GROUP
                    at_second = (q % half + quarter) % half
                    tile = jnp.where(lane_group == q, first, 0.0)
                    tile = jnp.where(lane_group == other, turned, tile)
                    turn = 0 if (at_second - q) % GROUP == quarter else 1
                    rows.append(jnp.where(lane_group == at_second, seconds[turn], tile))
        total = dot(jnp.concatenate(rows, axis=0).astype(BF16), weights)
        out_ref[field] = total.reshape(groups * GROUP, SUB, LANES)


def where_am_i(counts):
    at_x, at_y = lax.axis_index("gx"), lax.axis_index("gy")
    return (
        lax.rem(at_x, 2) == 1, lax.rem(at_y, 2) == 1,
        at_x == counts[0] - 1, at_x == 0, at_y == counts[1] - 1, at_y == 0,
    )


def head_rows(first, second):
    return jnp.where(rows_of(first.shape) < HALO, first, pltpu.roll(second, HALO, 0))


def tail_rows(first, second):
    return jnp.where(rows_of(first.shape) < HALO, pltpu.roll(first, HALO, 0), second)


def face_turns(place):
    _, _, no_next, no_prev, _, _ = place
    row = rows_of((SUB, LANES)) % HALO
    after = [jnp.where((row >= d) & jnp.logical_not(no_next), coef_rest[HALO - 1 - d], 0.0) for d in range(HALO)]
    before = [jnp.where((row + d < HALO) & jnp.logical_not(no_prev), coef_rest[HALO - 1 - d], 0.0) for d in range(HALO)]
    return after, before


def from_faces(xa, xb, odd, coefs):
    after, before = jnp.where(odd, xb, xa), jnp.where(odd, xa, xb)
    after_sum, before_sum = coefs[0][0] * after, coefs[1][0] * before
    for d in range(1, HALO):
        after_sum = after_sum + coefs[0][d] * pltpu.roll(after, d, 0)
        before_sum = before_sum + coefs[1][d] * pltpu.roll(before, SUB - d, 0)
    low = rows_of(after.shape) < HALO
    return (
        jnp.where(low, before_sum, pltpu.roll(after_sum, HALO, 0)),
        jnp.where(low, pltpu.roll(before_sum, HALO, 0), after_sum),
    )


def turns(kept):
    row = rows_of((SUB, LANES))
    out = []
    for turn in range(1, SUB):
        coef = coef_rest[min(turn, SUB - turn) - 1]
        inside = row >= turn if turn < HALO else row < turn if turn > HALO else row >= 0
        out.append(jnp.where(inside if kept else jnp.logical_not(inside) | (turn == HALO), coef, 0.0))
    return out


def along_x(cells, coefs):
    total = coefs[0] * pltpu.roll(cells, 1, 0)
    for turn in range(2, SUB):
        total = total + coefs[turn - 1] * pltpu.roll(cells, turn, 0)
    return total


def local_step(now_ref, old_ref, courant_ref, out_ref):
    deep = now_ref.shape[1]
    high, low = band(coef_high), band(coef_low)
    for field in range(2):
        cells = now_ref[field].reshape(deep * SUB, LANES)
        out_ref[field] = local_y(cells, high, low).reshape(deep, SUB, LANES)
    coefs = turns(True)

    def body(depth, static_depth):
        for field in range(2):
            cells = now_ref[field, depth]
            total = 3.0 * coef_zero * cells + out_ref[field, depth] + along_x(cells, coefs)
            for step in range(1, HALO + 1):
                near = None
                if static_depth is None or static_depth + step < deep:
                    near = now_ref[field, depth + step]
                if static_depth is None or static_depth >= step:
                    before = now_ref[field, depth - step]
                    near = before if near is None else near + before
                total = total + coef_rest[step - 1] * near
            out_ref[field, depth] = 2.0 * cells - old_ref[field, depth] + courant_ref[depth] * total

    over_depth(deep, body)


def halo_step(depth, base_ref, courant_ref, xa_ref, xb_ref, part_y_ref, odd, coefs):
    sides = from_faces(xa_ref[depth], xb_ref[depth], odd, coefs)
    return [
        base_ref[field, depth] + courant_ref[depth] * (part_y_ref[field, depth] + sides[field]) for field in range(2)
    ]


def over_depth(deep, body):
    def inner(depth, carry):
        body(depth, None)
        return carry

    for depth in range(HALO):
        body(depth, depth)
    lax.fori_loop(HALO, deep - HALO, inner, 0, unroll=8)
    for depth in range(deep - HALO, deep):
        body(depth, depth)


def residual(counts, cells_x, cells_y, radius_sq, signs_ref, sx_ref, sy_ref, records_ref, cell_ref, out_ref, first):
    shots, rows, _ = records_ref.shape
    chunk = min(rows, 64)
    per = 2 * REC_DEV // LANES
    twice = (rows_of((chunk, chunk // 2)) >> 1 == lanes_of((chunk, chunk // 2))).astype(F32).astype(BF16)

    def chunk_step(c, carry):
        cell = cell_ref[pl.ds(pl.multiple_of(c * (chunk // 2), chunk // 2), chunk // 2), :]
        row, column = lax.shift_right_logical(cell, cells_y.bit_length() - 1), cell & (cells_y - 1)
        row, column = [dot(twice, v.astype(F32).astype(BF16)) for v in (row, column)]
        tile = c * (chunk // per) + rows_of((chunk, LANES)) // per
        tile_x, tile_y = tile // counts[1], tile % counts[1]
        pos_x = (tile_x * cells_x).astype(F32) + row
        pos_y = (tile_y * cells_y).astype(F32) + column
        start = pl.multiple_of(c * chunk, chunk)

        def shot_step(shot, sums):
            dx = pos_x - sx_ref[shot].astype(F32)
            dy = pos_y - sy_ref[shot].astype(F32)
            dist = dx * dx + dy * dy
            whole = dist + radius_sq
            inverse = pl.reciprocal(whole, approx=True)
            inverse = inverse * (2.0 - whole * inverse)
            taped = records_ref[shot, pl.ds(start, chunk), :].astype(F32) * (dist * inverse)
            return tuple(s + signs_ref[code, shot].astype(F32) * taped for code, s in enumerate(sums))

        sums = lax.fori_loop(0, shots, shot_step, (jnp.zeros((chunk, LANES), F32),) * 2, unroll=8)
        for t in range(chunk // per):
            both = [s[t * per : (t + 1) * per] for s in sums]
            out_ref[first + c * (chunk // per) + t] = jnp.concatenate(both, axis=0)
        return carry

    lax.fori_loop(0, rows // chunk, chunk_step, 0)


def bring_kernel(
    radius_sq, counts, signs_hbm, sx_hbm, sy_hbm, records_hbm, cell_hbm, now_hbm, old_hbm, courant_hbm,
    now_ref, old_ref, courant_ref, cell_ref, xa_ref, xb_ref, records_ref, signs_ref, sx_ref, sy_ref, sems,
):
    copies = []

    def bring(source, target):
        copy = pltpu.make_async_copy(source, target, sems.at[len(copies)])
        copy.start()
        copies.append(copy)

    for source, target in (
        (cell_hbm, cell_ref), (signs_hbm, signs_ref), (sx_hbm, sx_ref), (sy_hbm, sy_ref), (records_hbm, records_ref),
        (now_hbm, now_ref), (old_hbm, old_ref), (courant_hbm, courant_ref),
    ):
        bring(source, target)
    for copy in copies[:5]:
        copy.wait()
    _, deep, cells_x, cells_y = now_ref.shape
    residual(counts, cells_x, cells_y, radius_sq, signs_ref, sx_ref, sy_ref, records_ref, cell_ref, xa_ref, deep)
    copies[5].wait()
    odd = where_am_i(counts)[0]

    def body(depth, carry):
        first, second = now_ref[0, depth], now_ref[1, depth]
        head, tail = head_rows(first, second), tail_rows(first, second)
        xb_ref[depth] = jnp.where(odd, tail, head)
        xa_ref[depth] = jnp.where(odd, head, tail)
        return carry

    lax.fori_loop(0, deep, body, 0, unroll=8)
    for copy in copies[6:]:
        copy.wait()


def pack_kernel(counts, now_ref, ya_ref, yb_ref):
    pack_columns(now_ref, where_am_i(counts)[1], ya_ref, yb_ref)


def needed_tiles(counts, x, y):
    return (
        (x, y),
        (jnp.minimum(x + 1, counts[0] - 1), y), (jnp.maximum(x - 1, 0), y),
        (x, jnp.minimum(y + 1, counts[1] - 1)), (x, jnp.maximum(y - 1, 0)),
    )


def inject(pieces, samples, cells_y):
    values, hots = [], []
    for res, cells, row_kept, column_kept in pieces:
        for half in range(REC_DEV // LANES):
            row = lax.shift_right_logical(cells[half], cells_y.bit_length() - 1)
            column = cells[half] & (cells_y - 1)
            in_row = (rows_of((SUB, LANES)) == row) & row_kept(rows_of((SUB, LANES)))
            values.append(jnp.concatenate(
                [
                    jnp.where(in_row, res[code * 4 + half * 2 + sample][None, :], 0.0)
                    for code in range(2)
                    for sample in range(samples)
                ],
                axis=0,
            ))
            at = rows_of((cells_y, LANES))
            hots.append(((at == column) & column_kept(at)).astype(F32).astype(BF16))
    values = jnp.concatenate(split(jnp.concatenate(values, axis=1)), axis=0)
    got = lax.dot_general(
        values, jnp.concatenate(hots, axis=1), (((1,), (1,)), ((), ())), preferred_element_type=F32
    )
    count = 2 * samples * SUB
    return got[:count] + got[count : 2 * count] + got[2 * count :]


def second_local_kernel(counts, now_ref, old_ref, courant_ref, before_ref, out_ref):
    del before_ref
    local_step(now_ref, old_ref, courant_ref, out_ref)


def local_kernel(counts, now_ref, old_ref, courant_ref, out_ref):
    local_step(now_ref, old_ref, courant_ref, out_ref)


def block_parts(counts, block):
    pairs, own = counts[0] // 2, counts[0] // 4
    return pairs, own, block * pairs, block * pairs + 2 * own, block * pairs + 2 * own + block * own


def pack_samples(first, second):
    even = rows_of((SUB, LANES)) % 2 == 0
    return (
        jnp.where(even, first, pltpu.roll(second, 1, 0)),
        jnp.where(even, pltpu.roll(first, SUB - 1, 0), second),
    )


def outside(counts, start, block):
    return jnp.minimum(start + block, counts[1] - 1), jnp.maximum(start - 1, 0)


def partner_block(at_y, half):
    mine = lax.div(at_y, half) * half
    return mine, lax.div(at_y, 2 * half) * (4 * half) + half - mine


def join_kernel(counts, own_ref, other_ref, before_ref, out_ref, keep_ref):
    del before_ref
    at_x, at_y = lax.axis_index("gx"), lax.axis_index("gy")
    at, at_other = [ref.shape[0] - counts[0] * counts[1] for ref in (own_ref, other_ref)]
    half = counts[1] // 2
    pairs, own, at_outside, at_second, _ = block_parts(counts, half)
    total = lambda x, y: own_ref[at + x * counts[1] + y] + other_ref[at_other + x * counts[1] + y]
    row = lambda m: 4 * m + lax.rem(at_x, 2)
    mine, partner = partner_block(at_y, half)
    for ref, start in ((keep_ref, mine), (out_ref, partner)):
        for i in range(half):
            for j in range(pairs):
                x = j // 2 * 4 + j % 2
                ref[i * pairs + j] = pack_samples(total(x, start + i), total(x + 2, start + i))[0]
            for m in range(own):
                ref[at_second + i * own + m] = pack_samples(total(row(m), start + i), total(row(m) + 2, start + i))[1]
        for side, y in enumerate(outside(counts, start, half)):
            for m in range(own):
                ref[at_outside + side * own + m] = pack_samples(total(row(m), y), total(row(m) + 2, y))[0]


def fold_kernel(block, counts, own_ref, other_ref, out_ref, keep_ref):
    at_x, at_y = lax.axis_index("gx"), lax.axis_index("gy")
    half = block // 2
    pairs, own, at_outside, at_second, _ = block_parts(counts, block)
    _, _, new_outside, new_second, _ = block_parts(counts, half)
    total = lambda i: own_ref[i] + other_ref[i]
    first = lax.div(at_y, block) * block
    mine, partner = partner_block(at_y, half)
    for ref, start in ((keep_ref, mine), (out_ref, partner)):
        for i in range(half):
            for j in range(pairs):
                ref[i * pairs + j] = total((start - first + i) * pairs + j)
            for m in range(own):
                ref[new_second + i * own + m] = total(at_second + (start - first + i) * own + m)
        for side, y in enumerate(outside(counts, start, half)):
            for m in range(own):
                inside = (y - first) * pairs + 2 * m + lax.rem(at_x, 2)
                after, before = at_outside + m, at_outside + own + m
                ref[new_outside + side * own + m] = total(
                    jnp.where(y < first, before, jnp.where(y >= first + block, after, inside))
                )


def sum_kernel(counts, own_ref, other_ref, before_ref, out_ref):
    del before_ref
    out_ref[...] = own_ref[...] + other_ref[...]


def needed_kernel(counts, own_ref, other_ref, before_ref, ya_ref, yb_ref, xa_ref, out_ref, keep_ref, yb_out, xa_out):
    del before_ref, yb_ref, yb_out, xa_ref, xa_out
    at_x, at_y = lax.axis_index("gx"), lax.axis_index("gy")
    pairs, own, at_outside, at_second, _ = block_parts(counts, 2)
    even = rows_of((SUB, LANES)) % 2 == 0
    total = lambda i: own_ref[i] + other_ref[i]
    is_second = lambda x: lax.rem(lax.div(x, 2), 2) == 1
    pick_first = lambda got, x: jnp.where(is_second(x), pltpu.roll(got, SUB - 1, 0), got)
    faces = ya_ref.shape[0]
    out_ref[:faces] = ya_ref[...]

    def inside(x, column):
        return pick_first(total(column * pairs + lax.div(x, 4) * 2 + lax.rem(x, 2)), x)

    def collect(target_ref, first, column):
        more = total(at_second + column * own + lax.div(at_x, 4))
        more = jnp.where(is_second(at_x), more, pltpu.roll(more, 1, 0))
        target_ref[first] = jnp.where(even, inside(at_x, column), more)
        beside = inside(jnp.minimum(at_x + 1, counts[0] - 1), column), inside(jnp.maximum(at_x - 1, 0), column)
        target_ref[first + 1] = jnp.where(even, beside[0], pltpu.roll(beside[1], 1, 0))
        after, before = [pick_first(total(at_outside + side * own + lax.div(at_x, 4)), at_x) for side in range(2)]
        after = jnp.where(column == 0, inside(at_x, 1), after)
        before = jnp.where(column == 0, before, inside(at_x, 0))
        target_ref[first + 2] = jnp.where(even, after, pltpu.roll(before, 1, 0))

    column = lax.rem(at_y, 2)
    collect(out_ref, faces, 1 - column)
    collect(keep_ref, 0, column)


def middle_kernel(
    counts, base_ref, courant_ref, xa_ref, xb_ref, ya_ref, yb_ref,
    mid_ref, xa_out, xb_out, ya_out, yb_out, part_y_ref,
):
    place = where_am_i(counts)
    deep = base_ref.shape[1]
    halo_y(ya_ref, yb_ref, place, part_y_ref)
    coefs = face_turns(place)

    def body(depth, carry):
        fields = halo_step(depth, base_ref, courant_ref, xa_ref, xb_ref, part_y_ref, place[0], coefs)
        for field in range(2):
            mid_ref[field, depth] = fields[field]
        head, tail = head_rows(*fields), tail_rows(*fields)
        xa_out[depth] = jnp.where(place[0], head, tail)
        xb_out[depth] = jnp.where(place[0], tail, head)
        return carry

    lax.fori_loop(0, deep, body, 0, unroll=8)
    pack_columns(mid_ref, place[1], ya_out, yb_out)


def inject_kernel(counts, keep_ref, res_ref, cell_ref, courant_ref, layer_ref):
    _, _, no_next_x, no_prev_x, no_next_y, no_prev_y = where_am_i(counts)
    _, cells_x, cells_y = courant_ref.shape
    tiles = needed_tiles(counts, lax.axis_index("gx"), lax.axis_index("gy"))
    halves = REC_DEV // LANES
    at = res_ref.shape[0] - 3
    own, *pairs = [keep_ref[i] + res_ref[at + i] for i in range(3)]
    res = [own] + [half for pair in pairs for half in (pair, pltpu.roll(pair, SUB - 1, 0))]
    for i, absent in enumerate((no_next_x, no_prev_x, no_next_y, no_prev_y)):
        res[i + 1] = jnp.where(absent, 0.0, res[i + 1])
    cells = [
        [cell_ref[pl.ds((x * counts[1] + y) * halves + half, 1), :] for half in range(halves)] for x, y in tiles
    ]
    every = lambda at: at >= 0
    own = inject([(res[0], cells[0], every, every)], 2, cells_y)
    beside_x = inject(
        [(res[1], cells[1], lambda at: at < HALO, every), (res[2], cells[2], lambda at: at >= SUB - HALO, every)],
        1, cells_y,
    )
    beside_y = inject(
        [(res[3], cells[3], every, lambda at: at < HALO), (res[4], cells[4], every, lambda at: at >= cells_y - HALO)],
        1, cells_y,
    )
    kept, beside = turns(True), turns(False)
    lane = lanes_of((cells_x, cells_y))
    for field in range(2):
        layer = own[2 * field * cells_x : (2 * field + 1) * cells_x]
        side_x, side_y = [v[field * cells_x : (field + 1) * cells_x] for v in (beside_x, beside_y)]
        total = 3.0 * coef_zero * layer + along_x(layer, kept) + along_x(side_x, beside)
        for step in range(1, HALO + 1):
            up = pltpu.roll(jnp.where(lane < step, side_y, layer), cells_y - step, 1)
            down = pltpu.roll(jnp.where(lane >= cells_y - step, side_y, layer), step, 1)
            total = total + coef_rest[step - 1] * (up + down)
        layer_ref[field] = layer
        second = own[(2 * field + 1) * cells_x : (2 * field + 2) * cells_x]
        layer_ref[2 + field] = 2.0 * layer + courant_ref[RDEPTH] * total + second


def after_kernel(
    counts, base_ref, mid_ref, courant_ref, xa_ref, xb_ref, ya_ref, yb_ref, layer_ref,
    out_ref, mid_out, part_y_ref, held_ref, plane_ref, sems,
):
    place = where_am_i(counts)
    deep = base_ref.shape[1]
    coefs = face_turns(place)
    copies = []

    def send_out(source, target):
        copy = pltpu.make_async_copy(source, target, sems.at[len(copies)])
        copy.start()
        copies.append(copy)

    send_out(mid_ref.at[:, pl.ds(0, RDEPTH)], mid_out.at[:, pl.ds(0, RDEPTH)])
    rest = pl.ds(RDEPTH + 1, deep - RDEPTH - 1)
    send_out(mid_ref.at[:, rest], mid_out.at[:, rest])
    for field in range(2):
        plane_ref[field, 0] = mid_ref[field, RDEPTH] + layer_ref[field]
    plane = pl.ds(RDEPTH, 1)
    send_out(plane_ref, mid_out.at[:, plane])

    halo_y(ya_ref, yb_ref, place, part_y_ref)
    size = deep // 8
    for part in range(8):
        def body(depth, carry):
            fields = halo_step(depth, base_ref, courant_ref, xa_ref, xb_ref, part_y_ref, place[0], coefs)
            for field in range(2):
                held_ref[field, depth] = fields[field]
            return carry

        lax.fori_loop(part * size, (part + 1) * size, body, 0, unroll=8)
        if part == 0:
            for field in range(2):
                held_ref[field, RDEPTH] = held_ref[field, RDEPTH] + layer_ref[2 + field]
                for step in range(1, HALO + 1):
                    change = coef_rest[step - 1] * layer_ref[field]
                    for depth in (RDEPTH - step, RDEPTH + step):
                        if depth >= 0:
                            held_ref[field, depth] = held_ref[field, depth] + courant_ref[depth] * change
        depths = pl.ds(part * size, size)
        send_out(held_ref.at[:, depths], out_ref.at[:, depths])
    for copy in copies:
        copy.wait()


def paired(groups, count_x, count_y, partner):
    index = lambda g, x, y: (g * count_x + x) * count_y + y
    return [
        (index(g, x, y), index(*partner(g, x, y)))
        for g in range(groups)
        for x in range(count_x)
        for y in range(count_y)
    ]


def on_device(wave_now, wave_before, courant, records, signs, source_x, source_y, receiver_cell):
    _, deep, cells_x, cells_y = wave_now.shape
    groups, tiles_x, tiles_y = [lax.axis_size(axis) for axis in AXES]
    counts = (tiles_x, tiles_y)
    total_recv = receiver_cell.shape[0]
    tiles = total_recv // REC_DEV
    shots = records.shape[0]
    span = (cells_x * tiles_x + cells_y * tiles_y) // 4

    perms = functools.partial(paired, groups, tiles_x, tiles_y)
    swap_xa = perms(lambda g, x, y: (g, x ^ 1, y))
    swap_ya = perms(lambda g, x, y: (g, x, y ^ 1))
    swap_xb = perms(
        lambda g, x, y: ((g + groups // 2) % groups, x, y) if x in (0, tiles_x - 1) else (g, ((x + 1) ^ 1) - 1, y)
    )
    swap_yb = perms(lambda g, x, y: (g, x ^ 1, y) if y in (0, tiles_y - 1) else (g, x, ((y + 1) ^ 1) - 1))
    swap_along = {
        "gx": lambda step: perms(lambda g, x, y: (g, x ^ step, y)),
        "gy": lambda step: perms(lambda g, x, y: (g, x, y ^ step)),
    }
    steps_x = [1 << i for i in range(1, (tiles_x - 1).bit_length())]
    blocks = [tiles_y >> i for i in range(1, (tiles_y - 1).bit_length())]
    send = lambda value, pairs: lax.ppermute(value, AXES, pairs)

    face_x = pltpu.VMEM((deep, cells_x, cells_y), F32)
    faces = deep // GROUP
    face_y = pltpu.VMEM((faces, cells_x, cells_y), F32)
    tiles_of = lambda count: pltpu.VMEM((count, SUB, LANES), F32)
    wave = wave_now.shape

    def kernel(body, outs, n_scalar, n_array, scratch=(), out_specs=None, aliases={}, cost=None):
        name = getattr(body, "func", body).__name__.removesuffix("_kernel")

        def call(*args):
            args = args[:n_scalar] + tuple(near_memory(a) for a in args[n_scalar:])
            return pl.pallas_call(
                functools.partial(body, counts),
                out_shape=outs,
                in_specs=[SM] * n_scalar + [VM] * n_array,
                out_specs=out_specs if out_specs is not None else jax.tree.map(lambda _: VM, outs),
                scratch_shapes=scratch,
                input_output_aliases=aliases,
                cost_estimate=cost,
                compiler_params=PARAMS,
                name=name,
            )(*args)

        return call

    wave_v = pltpu.VMEM(wave, F32)
    cell_rows = receiver_cell.reshape(total_recv // LANES, LANES)
    record_rows = records.reshape(shots, 2, total_recv // LANES, LANES).transpose(0, 2, 1, 3)
    record_rows = record_rows.reshape(shots, 2 * total_recv // LANES, LANES)
    far = lambda value: pltpu.with_memory_space_constraint(value, pltpu.HBM)
    now, old, speed, cells, xa, xb = pl.pallas_call(
        functools.partial(bring_kernel, float(span * span), counts),
        out_shape=(
            wave_v, wave_v, pltpu.VMEM(courant.shape, F32), pltpu.VMEM(cell_rows.shape, jnp.int32),
            tiles_of(deep + tiles), face_x,
        ),
        in_specs=[pl.BlockSpec(memory_space=pltpu.HBM)] * 8,
        out_specs=(VM,) * 6,
        scratch_shapes=[
            pltpu.VMEM(record_rows.shape, BF16),
            pltpu.SMEM(signs.shape, jnp.int32), pltpu.SMEM((shots,), jnp.int32), pltpu.SMEM((shots,), jnp.int32),
            pltpu.SemaphoreType.DMA((8,)),
        ],
        compiler_params=PARAMS,
        name="bring",
    )(*(far(a) for a in (signs, source_x, source_y, record_rows, cell_rows, wave_now, wave_before, courant)))
    xb_in, xa_in = send(xb, swap_xb), send(xa, swap_xa)
    ya, yb = kernel(pack_kernel, (face_y, face_y), 0, 1)(now)
    yb_in = send(yb, swap_yb)
    sums = tiles_of(block_parts(counts, blocks[0])[-1])
    wanted, partial_res = kernel(join_kernel, (sums, sums), 0, 3)(xa, xa_in, ya)
    other = send(wanted, swap_along["gy"](blocks[0]))
    for block in blocks[:-1]:
        sums = tiles_of(block_parts(counts, block // 2)[-1])
        fold = functools.partial(fold_kernel, block)
        wanted, partial_res = kernel(fold, (sums, sums), 0, 2)(partial_res, other)
        other = send(wanted, swap_along["gy"](block // 2))
    ya_in = send(ya, swap_ya)
    base = kernel(local_kernel, wave_v, 0, 3)(now, old, speed)
    for step in steps_x:
        partial_res = kernel(sum_kernel, sums, 0, 3)(partial_res, other, cells)
        other = send(partial_res, swap_along["gx"](step))
    wave_middle, xa, xb, ya, yb = kernel(middle_kernel, (wave_v, face_x, face_x, face_y, face_y), 0, 6, [wave_v], cost=pl.CostEstimate(flops=10*10**8, bytes_accessed=0, transcendentals=0))(
        base, speed, xa_in, xb_in, ya_in, yb_in
    )
    y_more, keep, yb, xa = kernel(
        needed_kernel, (tiles_of(faces + 3), tiles_of(3), face_y, face_x), 0, 6, aliases={4: 2, 5: 3}, cost=pl.CostEstimate(flops=30*10**8, bytes_accessed=0, transcendentals=0)
    )(partial_res, other, wave_middle, ya, yb, xa)
    xb_in, xa_in = send(xb, swap_xb), send(xa, swap_xa)
    ya_in, yb_in = send(y_more, swap_ya), send(yb, swap_yb)
    base = kernel(second_local_kernel, wave_v, 0, 4, cost=pl.CostEstimate(flops=0*10**8, bytes_accessed=0, transcendentals=0))(wave_middle, now, speed, keep)
    plane = (2, 1, cells_x, cells_y)
    layers = kernel(inject_kernel, tiles_of(4), 0, 4)(keep, ya_in, cells, speed)
    wave_after, wave_middle = kernel(
        after_kernel, (jax.ShapeDtypeStruct(wave, F32),) * 2, 0, 8,
        [wave_v, wave_v, pltpu.VMEM(plane, F32), pltpu.SemaphoreType.DMA((11,))],
        out_specs=(pl.BlockSpec(memory_space=pl.ANY),) * 2,
    )(base, wave_middle, speed, xa_in, xb_in, ya_in, yb_in, layers)
    return (wave_after, wave_middle)


def solution(mesh):
    return jax.shard_map(
        on_device,
        mesh=mesh,
        in_specs=(
            P("group", None, "gx", "gy"),
            P("group", None, "gx", "gy"),
            P("group", "gx", "gy"),
            P(("group", "gx", "gy"), None, None),
            P("group", ("gx", "gy")),
            P(("group", "gx", "gy")),
            P(("group", "gx", "gy")),
            P("group"),
        ),
        out_specs=(P("group", None, "gx", "gy"), P("group", None, "gx", "gy")),
        check_vma=False,
    )
```

```python
import functools

import jax
import jax.numpy as jnp
import ml_dtypes
import numpy as np
from jax import lax
from jax.experimental import pallas as pl
from jax.experimental.pallas import tpu as pltpu
from jax.sharding import PartitionSpec as P

REC_DEV = 256
RDEPTH = 2
HALO = 4
LANES = 128
SUB = 8
GROUP = 16
AXES = ("group", "gx", "gy")
F32, BF16 = jnp.float32, jnp.bfloat16

coef_zero = -205.0 / 72.0
coef_rest = (8.0 / 5.0, -1.0 / 5.0, 8.0 / 315.0, -1.0 / 560.0)
coef_high = [float(np.float32(c).astype(ml_dtypes.bfloat16)) for c in coef_rest]
coef_low = [float(np.float32(c - h).astype(ml_dtypes.bfloat16)) for c, h in zip(coef_rest, coef_high)]

VM = pl.BlockSpec(memory_space=pltpu.VMEM)
SM = pl.BlockSpec(memory_space=pltpu.SMEM)
PARAMS = pltpu.CompilerParams(vmem_limit_bytes=16 * 1024 * 1024)


def near_memory(value):
    return pltpu.with_memory_space_constraint(value, pltpu.VMEM)


def rows_of(shape):
    return lax.broadcasted_iota(jnp.int32, shape, len(shape) - 2)


def lanes_of(shape):
    return lax.broadcasted_iota(jnp.int32, shape, len(shape) - 1)


def dot(left, right):
    return jnp.dot(left, right, preferred_element_type=F32)


def split(value):
    first = value.astype(BF16)
    rest = value - first.astype(F32)
    second = rest.astype(BF16)
    return first, second, (rest - second.astype(F32)).astype(BF16)


def pick(step, coefs):
    out = jnp.zeros(step.shape, F32)
    for m in range(1, HALO + 1):
        out = jnp.where(step == m, coefs[m - 1], out)
    return out.astype(BF16)


def band(coefs):
    shape = (LANES, LANES)
    return pick(jnp.abs(rows_of(shape) - lanes_of(shape)), coefs)


def side():
    shape = (LANES, LANES)
    c = rows_of(shape) & 7
    j = lanes_of(shape)
    step = jnp.where(c < HALO, j + HALO - c, LANES + c - HALO - j)
    return jnp.where(rows_of(shape) < LANES // 2, pick(step, coef_high).astype(F32), pick(step, coef_low).astype(F32)).astype(BF16)


def pack_columns(ref, odd, ya_ref, yb_ref):
    lane_group = lanes_of((SUB, LANES)) >> 3
    low = (lanes_of((SUB, LANES)) & 7) < HALO
    pairs = ref.shape[1] // GROUP // 2

    def step(pair, carry):
        for field in range(2):
            both = []
            for group in range(2):
                tile = None
                for q in range(GROUP):
                    cells = ref[field, (pair * 2 + group) * GROUP + q]
                    turned = pltpu.roll(cells, (q * 2 * HALO + HALO) % LANES, 1)
                    tile = turned if tile is None else jnp.where(lane_group == q, turned, tile)
                both.append(tile)
            last = jnp.where(low, both[0], pltpu.roll(both[1], HALO, 1))
            first = jnp.where(low, pltpu.roll(both[0], LANES - HALO, 1), both[1])
            ya_ref[field * pairs + pair] = jnp.where(odd, first, last)
            yb_ref[field * pairs + pair] = jnp.where(odd, last, first)
        return carry

    lax.fori_loop(0, pairs, step, 0)


def sides_y(ya, yb, odd, no_next, no_prev):
    after = jnp.where(no_next, 0.0, jnp.where(odd, yb, ya))
    before = jnp.where(no_prev, 0.0, jnp.where(odd, ya, yb))
    low = (lanes_of(ya.shape) & 7) < HALO
    return (
        jnp.where(low, before, pltpu.roll(after, HALO, 1)),
        jnp.where(low, pltpu.roll(before, LANES - HALO, 1), after),
    )


def local_y(cells, high, low):
    first, second, _ = split(cells)
    return dot(jnp.concatenate([first, second, first], axis=1), jnp.concatenate([high, high, low], axis=0))


def halo_y(ya_ref, yb_ref, place, out_ref):
    weights = side()
    _, odd, _, _, no_next, no_prev = place
    groups = out_ref.shape[1] // GROUP
    lane_group = lanes_of((SUB, LANES)) >> 3
    half, quarter = GROUP // 2, GROUP // 4
    for field in range(2):
        rows = []
        for pair in range(groups // 2):
            at = field * (groups // 2) + pair
            for beside in sides_y(ya_ref[at], yb_ref[at], odd, no_next, no_prev):
                first = beside.astype(BF16).astype(F32)
                second = (beside - first).astype(BF16).astype(F32)
                turned = pltpu.roll(first, LANES // 2, 1)
                seconds = [pltpu.roll(second, turn, 1) for turn in (LANES // 4, LANES - LANES // 4)]
                for q in range(GROUP):
                    other = (q + half) % GROUP
                    at_second = (q % half + quarter) % half
                    tile = jnp.where(lane_group == q, first, 0.0)
                    tile = jnp.where(lane_group == other, turned, tile)
                    turn = 0 if (at_second - q) % GROUP == quarter else 1
                    rows.append(jnp.where(lane_group == at_second, seconds[turn], tile))
        total = dot(jnp.concatenate(rows, axis=0).astype(BF16), weights)
        out_ref[field] = total.reshape(groups * GROUP, SUB, LANES)


def where_am_i(counts):
    at_x, at_y = lax.axis_index("gx"), lax.axis_index("gy")
    return (
        lax.rem(at_x, 2) == 1, lax.rem(at_y, 2) == 1,
        at_x == counts[0] - 1, at_x == 0, at_y == counts[1] - 1, at_y == 0,
    )


def head_rows(first, second):
    return jnp.where(rows_of(first.shape) < HALO, first, pltpu.roll(second, HALO, 0))


def tail_rows(first, second):
    return jnp.where(rows_of(first.shape) < HALO, pltpu.roll(first, HALO, 0), second)


def face_turns(place):
    _, _, no_next, no_prev, _, _ = place
    row = rows_of((SUB, LANES)) % HALO
    after = [jnp.where((row >= d) & jnp.logical_not(no_next), coef_rest[HALO - 1 - d], 0.0) for d in range(HALO)]
    before = [jnp.where((row + d < HALO) & jnp.logical_not(no_prev), coef_rest[HALO - 1 - d], 0.0) for d in range(HALO)]
    return after, before


def from_faces(xa, xb, odd, coefs):
    after, before = jnp.where(odd, xb, xa), jnp.where(odd, xa, xb)
    after_sum, before_sum = coefs[0][0] * after, coefs[1][0] * before
    for d in range(1, HALO):
        after_sum = after_sum + coefs[0][d] * pltpu.roll(after, d, 0)
        before_sum = before_sum + coefs[1][d] * pltpu.roll(before, SUB - d, 0)
    low = rows_of(after.shape) < HALO
    return (
        jnp.where(low, before_sum, pltpu.roll(after_sum, HALO, 0)),
        jnp.where(low, pltpu.roll(before_sum, HALO, 0), after_sum),
    )


def turns(kept):
    row = rows_of((SUB, LANES))
    out = []
    for turn in range(1, SUB):
        coef = coef_rest[min(turn, SUB - turn) - 1]
        inside = row >= turn if turn < HALO else row < turn if turn > HALO else row >= 0
        out.append(jnp.where(inside if kept else jnp.logical_not(inside) | (turn == HALO), coef, 0.0))
    return out


def along_x(cells, coefs):
    total = coefs[0] * pltpu.roll(cells, 1, 0)
    for turn in range(2, SUB):
        total = total + coefs[turn - 1] * pltpu.roll(cells, turn, 0)
    return total


def local_step(now_ref, old_ref, courant_ref, out_ref):
    deep = now_ref.shape[1]
    high, low = band(coef_high), band(coef_low)
    for field in range(2):
        cells = now_ref[field].reshape(deep * SUB, LANES)
        out_ref[field] = local_y(cells, high, low).reshape(deep, SUB, LANES)
    coefs = turns(True)

    def body(depth, static_depth):
        for field in range(2):
            cells = now_ref[field, depth]
            total = 3.0 * coef_zero * cells + out_ref[field, depth] + along_x(cells, coefs)
            for step in range(1, HALO + 1):
                near = None
                if static_depth is None or static_depth + step < deep:
                    near = now_ref[field, depth + step]
                if static_depth is None or static_depth >= step:
                    before = now_ref[field, depth - step]
                    near = before if near is None else near + before
                total = total + coef_rest[step - 1] * near
            out_ref[field, depth] = 2.0 * cells - old_ref[field, depth] + courant_ref[depth] * total

    over_depth(deep, body)


def halo_step(depth, base_ref, courant_ref, xa_ref, xb_ref, part_y_ref, odd, coefs):
    sides = from_faces(xa_ref[depth], xb_ref[depth], odd, coefs)
    return [
        base_ref[field, depth] + courant_ref[depth] * (part_y_ref[field, depth] + sides[field]) for field in range(2)
    ]


def over_depth(deep, body):
    def inner(depth, carry):
        body(depth, None)
        return carry

    for depth in range(HALO):
        body(depth, depth)
    lax.fori_loop(HALO, deep - HALO, inner, 0, unroll=8)
    for depth in range(deep - HALO, deep):
        body(depth, depth)


def residual(counts, cells_x, cells_y, radius_sq, signs_ref, sx_ref, sy_ref, records_ref, cell_ref, out_ref, first):
    shots, rows, _ = records_ref.shape
    chunk = min(rows, 64)
    per = 2 * REC_DEV // LANES
    twice = (rows_of((chunk, chunk // 2)) >> 1 == lanes_of((chunk, chunk // 2))).astype(F32).astype(BF16)

    def chunk_step(c, carry):
        cell = cell_ref[pl.ds(pl.multiple_of(c * (chunk // 2), chunk // 2), chunk // 2), :]
        row, column = lax.shift_right_logical(cell, cells_y.bit_length() - 1), cell & (cells_y - 1)
        row, column = [dot(twice, v.astype(F32).astype(BF16)) for v in (row, column)]
        tile = c * (chunk // per) + rows_of((chunk, LANES)) // per
        tile_x, tile_y = tile // counts[1], tile % counts[1]
        pos_x = (tile_x * cells_x).astype(F32) + row
        pos_y = (tile_y * cells_y).astype(F32) + column
        start = pl.multiple_of(c * chunk, chunk)

        def shot_step(shot, sums):
            dx = pos_x - sx_ref[shot].astype(F32)
            dy = pos_y - sy_ref[shot].astype(F32)
            dist = dx * dx + dy * dy
            whole = dist + radius_sq
            inverse = pl.reciprocal(whole, approx=True)
            inverse = inverse * (2.0 - whole * inverse)
            taped = records_ref[shot, pl.ds(start, chunk), :].astype(F32) * (dist * inverse)
            return tuple(s + signs_ref[code, shot].astype(F32) * taped for code, s in enumerate(sums))

        sums = lax.fori_loop(0, shots, shot_step, (jnp.zeros((chunk, LANES), F32),) * 2, unroll=8)
        for t in range(chunk // per):
            both = [s[t * per : (t + 1) * per] for s in sums]
            out_ref[first + c * (chunk // per) + t] = jnp.concatenate(both, axis=0)
        return carry

    lax.fori_loop(0, rows // chunk, chunk_step, 0)


def bring_kernel(
    radius_sq, counts, signs_hbm, sx_hbm, sy_hbm, records_hbm, cell_hbm, now_hbm, old_hbm, courant_hbm,
    now_ref, old_ref, courant_ref, cell_ref, xa_ref, xb_ref, records_ref, signs_ref, sx_ref, sy_ref, sems,
):
    copies = []

    def bring(source, target):
        copy = pltpu.make_async_copy(source, target, sems.at[len(copies)])
        copy.start()
        copies.append(copy)

    for source, target in (
        (cell_hbm, cell_ref), (signs_hbm, signs_ref), (sx_hbm, sx_ref), (sy_hbm, sy_ref), (records_hbm, records_ref),
        (now_hbm, now_ref), (old_hbm, old_ref), (courant_hbm, courant_ref),
    ):
        bring(source, target)
    for copy in copies[:5]:
        copy.wait()
    _, deep, cells_x, cells_y = now_ref.shape
    residual(counts, cells_x, cells_y, radius_sq, signs_ref, sx_ref, sy_ref, records_ref, cell_ref, xa_ref, deep)
    copies[5].wait()
    odd = where_am_i(counts)[0]

    def body(depth, carry):
        first, second = now_ref[0, depth], now_ref[1, depth]
        head, tail = head_rows(first, second), tail_rows(first, second)
        xb_ref[depth] = jnp.where(odd, tail, head)
        xa_ref[depth] = jnp.where(odd, head, tail)
        return carry

    lax.fori_loop(0, deep, body, 0, unroll=8)
    for copy in copies[6:]:
        copy.wait()


def pack_kernel(counts, now_ref, ya_ref, yb_ref):
    pack_columns(now_ref, where_am_i(counts)[1], ya_ref, yb_ref)


def needed_tiles(counts, x, y):
    return (
        (x, y),
        (jnp.minimum(x + 1, counts[0] - 1), y), (jnp.maximum(x - 1, 0), y),
        (x, jnp.minimum(y + 1, counts[1] - 1)), (x, jnp.maximum(y - 1, 0)),
    )


def inject(pieces, samples, cells_y):
    values, hots = [], []
    for res, cells, row_kept, column_kept in pieces:
        for half in range(REC_DEV // LANES):
            row = lax.shift_right_logical(cells[half], cells_y.bit_length() - 1)
            column = cells[half] & (cells_y - 1)
            in_row = (rows_of((SUB, LANES)) == row) & row_kept(rows_of((SUB, LANES)))
            values.append(jnp.concatenate(
                [
                    jnp.where(in_row, res[code * 4 + half * 2 + sample][None, :], 0.0)
                    for code in range(2)
                    for sample in range(samples)
                ],
                axis=0,
            ))
            at = rows_of((cells_y, LANES))
            hots.append(((at == column) & column_kept(at)).astype(F32).astype(BF16))
    values = jnp.concatenate(split(jnp.concatenate(values, axis=1)), axis=0)
    got = lax.dot_general(
        values, jnp.concatenate(hots, axis=1), (((1,), (1,)), ((), ())), preferred_element_type=F32
    )
    count = 2 * samples * SUB
    return got[:count] + got[count : 2 * count] + got[2 * count :]


def second_local_kernel(counts, now_ref, old_ref, courant_ref, before_ref, out_ref):
    del before_ref
    local_step(now_ref, old_ref, courant_ref, out_ref)


def local_kernel(counts, now_ref, old_ref, courant_ref, out_ref):
    local_step(now_ref, old_ref, courant_ref, out_ref)


def block_parts(counts, block):
    pairs, own = counts[0] // 2, counts[0] // 4
    return pairs, own, block * pairs, block * pairs + 2 * own, block * pairs + 2 * own + block * own


def pack_samples(first, second):
    even = rows_of((SUB, LANES)) % 2 == 0
    return (
        jnp.where(even, first, pltpu.roll(second, 1, 0)),
        jnp.where(even, pltpu.roll(first, SUB - 1, 0), second),
    )


def outside(counts, start, block):
    return jnp.minimum(start + block, counts[1] - 1), jnp.maximum(start - 1, 0)


def partner_block(at_y, half):
    mine = lax.div(at_y, half) * half
    return mine, lax.div(at_y, 2 * half) * (4 * half) + half - mine


def join_kernel(counts, own_ref, other_ref, before_ref, out_ref, keep_ref):
    del before_ref
    at_x, at_y = lax.axis_index("gx"), lax.axis_index("gy")
    at, at_other = [ref.shape[0] - counts[0] * counts[1] for ref in (own_ref, other_ref)]
    half = counts[1] // 2
    pairs, own, at_outside, at_second, _ = block_parts(counts, half)
    total = lambda x, y: own_ref[at + x * counts[1] + y] + other_ref[at_other + x * counts[1] + y]
    row = lambda m: 4 * m + lax.rem(at_x, 2)
    mine, partner = partner_block(at_y, half)
    for ref, start in ((keep_ref, mine), (out_ref, partner)):
        for i in range(half):
            for j in range(pairs):
                x = j // 2 * 4 + j % 2
                ref[i * pairs + j] = pack_samples(total(x, start + i), total(x + 2, start + i))[0]
            for m in range(own):
                ref[at_second + i * own + m] = pack_samples(total(row(m), start + i), total(row(m) + 2, start + i))[1]
        for side, y in enumerate(outside(counts, start, half)):
            for m in range(own):
                ref[at_outside + side * own + m] = pack_samples(total(row(m), y), total(row(m) + 2, y))[0]


def fold_kernel(block, counts, own_ref, other_ref, out_ref, keep_ref):
    at_x, at_y = lax.axis_index("gx"), lax.axis_index("gy")
    half = block // 2
    pairs, own, at_outside, at_second, _ = block_parts(counts, block)
    _, _, new_outside, new_second, _ = block_parts(counts, half)
    total = lambda i: own_ref[i] + other_ref[i]
    first = lax.div(at_y, block) * block
    mine, partner = partner_block(at_y, half)
    for ref, start in ((keep_ref, mine), (out_ref, partner)):
        for i in range(half):
            for j in range(pairs):
                ref[i * pairs + j] = total((start - first + i) * pairs + j)
            for m in range(own):
                ref[new_second + i * own + m] = total(at_second + (start - first + i) * own + m)
        for side, y in enumerate(outside(counts, start, half)):
            for m in range(own):
                inside = (y - first) * pairs + 2 * m + lax.rem(at_x, 2)
                after, before = at_outside + m, at_outside + own + m
                ref[new_outside + side * own + m] = total(
                    jnp.where(y < first, before, jnp.where(y >= first + block, after, inside))
                )


def sum_kernel(counts, own_ref, other_ref, before_ref, out_ref):
    del before_ref
    out_ref[...] = own_ref[...] + other_ref[...]


def needed_kernel(counts, own_ref, other_ref, before_ref, ya_ref, yb_ref, xa_ref, out_ref, keep_ref, yb_out, xa_out):
    del before_ref, yb_ref, yb_out, xa_ref, xa_out
    at_x, at_y = lax.axis_index("gx"), lax.axis_index("gy")
    pairs, own, at_outside, at_second, _ = block_parts(counts, 2)
    even = rows_of((SUB, LANES)) % 2 == 0
    total = lambda i: own_ref[i] + other_ref[i]
    is_second = lambda x: lax.rem(lax.div(x, 2), 2) == 1
    pick_first = lambda got, x: jnp.where(is_second(x), pltpu.roll(got, SUB - 1, 0), got)
    faces = ya_ref.shape[0]
    out_ref[:faces] = ya_ref[...]

    def inside(x, column):
        return pick_first(total(column * pairs + lax.div(x, 4) * 2 + lax.rem(x, 2)), x)

    def collect(target_ref, first, column):
        more = total(at_second + column * own + lax.div(at_x, 4))
        more = jnp.where(is_second(at_x), more, pltpu.roll(more, 1, 0))
        target_ref[first] = jnp.where(even, inside(at_x, column), more)
        beside = inside(jnp.minimum(at_x + 1, counts[0] - 1), column), inside(jnp.maximum(at_x - 1, 0), column)
        target_ref[first + 1] = jnp.where(even, beside[0], pltpu.roll(beside[1], 1, 0))
        after, before = [pick_first(total(at_outside + side * own + lax.div(at_x, 4)), at_x) for side in range(2)]
        after = jnp.where(column == 0, inside(at_x, 1), after)
        before = jnp.where(column == 0, before, inside(at_x, 0))
        target_ref[first + 2] = jnp.where(even, after, pltpu.roll(before, 1, 0))

    column = lax.rem(at_y, 2)
    collect(out_ref, faces, 1 - column)
    collect(keep_ref, 0, column)


def middle_kernel(
    counts, base_ref, courant_ref, xa_ref, xb_ref, ya_ref, yb_ref,
    mid_ref, xa_out, xb_out, ya_out, yb_out, part_y_ref,
):
    place = where_am_i(counts)
    deep = base_ref.shape[1]
    halo_y(ya_ref, yb_ref, place, part_y_ref)
    coefs = face_turns(place)

    def body(depth, carry):
        fields = halo_step(depth, base_ref, courant_ref, xa_ref, xb_ref, part_y_ref, place[0], coefs)
        for field in range(2):
            mid_ref[field, depth] = fields[field]
        head, tail = head_rows(*fields), tail_rows(*fields)
        xa_out[depth] = jnp.where(place[0], head, tail)
        xb_out[depth] = jnp.where(place[0], tail, head)
        return carry

    lax.fori_loop(0, deep, body, 0, unroll=8)
    pack_columns(mid_ref, place[1], ya_out, yb_out)


def inject_kernel(counts, keep_ref, res_ref, cell_ref, courant_ref, layer_ref):
    _, _, no_next_x, no_prev_x, no_next_y, no_prev_y = where_am_i(counts)
    _, cells_x, cells_y = courant_ref.shape
    tiles = needed_tiles(counts, lax.axis_index("gx"), lax.axis_index("gy"))
    halves = REC_DEV // LANES
    at = res_ref.shape[0] - 3
    own, *pairs = [keep_ref[i] + res_ref[at + i] for i in range(3)]
    res = [own] + [half for pair in pairs for half in (pair, pltpu.roll(pair, SUB - 1, 0))]
    for i, absent in enumerate((no_next_x, no_prev_x, no_next_y, no_prev_y)):
        res[i + 1] = jnp.where(absent, 0.0, res[i + 1])
    cells = [
        [cell_ref[pl.ds((x * counts[1] + y) * halves + half, 1), :] for half in range(halves)] for x, y in tiles
    ]
    every = lambda at: at >= 0
    own = inject([(res[0], cells[0], every, every)], 2, cells_y)
    beside_x = inject(
        [(res[1], cells[1], lambda at: at < HALO, every), (res[2], cells[2], lambda at: at >= SUB - HALO, every)],
        1, cells_y,
    )
    beside_y = inject(
        [(res[3], cells[3], every, lambda at: at < HALO), (res[4], cells[4], every, lambda at: at >= cells_y - HALO)],
        1, cells_y,
    )
    kept, beside = turns(True), turns(False)
    lane = lanes_of((cells_x, cells_y))
    for field in range(2):
        layer = own[2 * field * cells_x : (2 * field + 1) * cells_x]
        side_x, side_y = [v[field * cells_x : (field + 1) * cells_x] for v in (beside_x, beside_y)]
        total = 3.0 * coef_zero * layer + along_x(layer, kept) + along_x(side_x, beside)
        for step in range(1, HALO + 1):
            up = pltpu.roll(jnp.where(lane < step, side_y, layer), cells_y - step, 1)
            down = pltpu.roll(jnp.where(lane >= cells_y - step, side_y, layer), step, 1)
            total = total + coef_rest[step - 1] * (up + down)
        layer_ref[field] = layer
        second = own[(2 * field + 1) * cells_x : (2 * field + 2) * cells_x]
        layer_ref[2 + field] = 2.0 * layer + courant_ref[RDEPTH] * total + second


def after_kernel(
    counts, base_ref, mid_ref, courant_ref, xa_ref, xb_ref, ya_ref, yb_ref, layer_ref,
    out_ref, mid_out, part_y_ref, held_ref, plane_ref, sems,
):
    place = where_am_i(counts)
    deep = base_ref.shape[1]
    coefs = face_turns(place)
    copies = []

    def send_out(source, target):
        copy = pltpu.make_async_copy(source, target, sems.at[len(copies)])
        copy.start()
        copies.append(copy)

    send_out(mid_ref.at[:, pl.ds(0, RDEPTH)], mid_out.at[:, pl.ds(0, RDEPTH)])
    rest = pl.ds(RDEPTH + 1, deep - RDEPTH - 1)
    send_out(mid_ref.at[:, rest], mid_out.at[:, rest])
    for field in range(2):
        plane_ref[field, 0] = mid_ref[field, RDEPTH] + layer_ref[field]
    plane = pl.ds(RDEPTH, 1)
    send_out(plane_ref, mid_out.at[:, plane])

    halo_y(ya_ref, yb_ref, place, part_y_ref)
    size = deep // 8
    for part in range(8):
        def body(depth, carry):
            fields = halo_step(depth, base_ref, courant_ref, xa_ref, xb_ref, part_y_ref, place[0], coefs)
            for field in range(2):
                held_ref[field, depth] = fields[field]
            return carry

        lax.fori_loop(part * size, (part + 1) * size, body, 0, unroll=8)
        if part == 0:
            for field in range(2):
                held_ref[field, RDEPTH] = held_ref[field, RDEPTH] + layer_ref[2 + field]
                for step in range(1, HALO + 1):
                    change = coef_rest[step - 1] * layer_ref[field]
                    for depth in (RDEPTH - step, RDEPTH + step):
                        if depth >= 0:
                            held_ref[field, depth] = held_ref[field, depth] + courant_ref[depth] * change
        depths = pl.ds(part * size, size)
        send_out(held_ref.at[:, depths], out_ref.at[:, depths])
    for copy in copies:
        copy.wait()


def paired(groups, count_x, count_y, partner):
    index = lambda g, x, y: (g * count_x + x) * count_y + y
    return [
        (index(g, x, y), index(*partner(g, x, y)))
        for g in range(groups)
        for x in range(count_x)
        for y in range(count_y)
    ]


def on_device(wave_now, wave_before, courant, records, signs, source_x, source_y, receiver_cell):
    _, deep, cells_x, cells_y = wave_now.shape
    groups, tiles_x, tiles_y = [lax.axis_size(axis) for axis in AXES]
    counts = (tiles_x, tiles_y)
    total_recv = receiver_cell.shape[0]
    tiles = total_recv // REC_DEV
    shots = records.shape[0]
    span = (cells_x * tiles_x + cells_y * tiles_y) // 4

    perms = functools.partial(paired, groups, tiles_x, tiles_y)
    swap_xa = perms(lambda g, x, y: (g, x ^ 1, y))
    swap_ya = perms(lambda g, x, y: (g, x, y ^ 1))
    swap_xb = perms(
        lambda g, x, y: ((g + groups // 2) % groups, x, y) if x in (0, tiles_x - 1) else (g, ((x + 1) ^ 1) - 1, y)
    )
    swap_yb = perms(lambda g, x, y: (g, x ^ 1, y) if y in (0, tiles_y - 1) else (g, x, ((y + 1) ^ 1) - 1))
    swap_along = {
        "gx": lambda step: perms(lambda g, x, y: (g, x ^ step, y)),
        "gy": lambda step: perms(lambda g, x, y: (g, x, y ^ step)),
    }
    steps_x = [1 << i for i in range(1, (tiles_x - 1).bit_length())]
    blocks = [tiles_y >> i for i in range(1, (tiles_y - 1).bit_length())]
    send = lambda value, pairs: lax.ppermute(value, AXES, pairs)

    face_x = pltpu.VMEM((deep, cells_x, cells_y), F32)
    faces = deep // GROUP
    face_y = pltpu.VMEM((faces, cells_x, cells_y), F32)
    tiles_of = lambda count: pltpu.VMEM((count, SUB, LANES), F32)
    wave = wave_now.shape

    def kernel(body, outs, n_scalar, n_array, scratch=(), out_specs=None, aliases={}, cost=None):
        name = getattr(body, "func", body).__name__.removesuffix("_kernel")

        def call(*args):
            args = args[:n_scalar] + tuple(near_memory(a) for a in args[n_scalar:])
            return pl.pallas_call(
                functools.partial(body, counts),
                out_shape=outs,
                in_specs=[SM] * n_scalar + [VM] * n_array,
                out_specs=out_specs if out_specs is not None else jax.tree.map(lambda _: VM, outs),
                scratch_shapes=scratch,
                input_output_aliases=aliases,
                cost_estimate=cost,
                compiler_params=PARAMS,
                name=name,
            )(*args)

        return call

    wave_v = pltpu.VMEM(wave, F32)
    cell_rows = receiver_cell.reshape(total_recv // LANES, LANES)
    record_rows = records.reshape(shots, 2, total_recv // LANES, LANES).transpose(0, 2, 1, 3)
    record_rows = record_rows.reshape(shots, 2 * total_recv // LANES, LANES)
    far = lambda value: pltpu.with_memory_space_constraint(value, pltpu.HBM)
    now, old, speed, cells, xa, xb = pl.pallas_call(
        functools.partial(bring_kernel, float(span * span), counts),
        out_shape=(
            wave_v, wave_v, pltpu.VMEM(courant.shape, F32), pltpu.VMEM(cell_rows.shape, jnp.int32),
            tiles_of(deep + tiles), face_x,
        ),
        in_specs=[pl.BlockSpec(memory_space=pltpu.HBM)] * 8,
        out_specs=(VM,) * 6,
        scratch_shapes=[
            pltpu.VMEM(record_rows.shape, BF16),
            pltpu.SMEM(signs.shape, jnp.int32), pltpu.SMEM((shots,), jnp.int32), pltpu.SMEM((shots,), jnp.int32),
            pltpu.SemaphoreType.DMA((8,)),
        ],
        compiler_params=PARAMS,
        name="bring",
    )(*(far(a) for a in (signs, source_x, source_y, record_rows, cell_rows, wave_now, wave_before, courant)))
    xb_in, xa_in = send(xb, swap_xb), send(xa, swap_xa)
    ya, yb = kernel(pack_kernel, (tiles_of(faces + 1), face_y), 0, 1)(now)
    yb_in = send(yb, swap_yb)
    sums = tiles_of(block_parts(counts, blocks[0])[-1])
    wanted, partial_res = kernel(join_kernel, (sums, sums), 0, 3)(xa, xa_in, ya)
    other = send(wanted, swap_along["gy"](blocks[0]))
    for block in blocks[:-1]:
        sums = tiles_of(block_parts(counts, block // 2)[-1])
        fold = functools.partial(fold_kernel, block)
        wanted, partial_res = kernel(fold, (sums, sums), 0, 2)(partial_res, other)
        other = send(wanted, swap_along["gy"](block // 2))
    ya_in = send(ya, swap_ya)
    base = kernel(local_kernel, wave_v, 0, 3)(now, old, speed)
    for step in steps_x:
        partial_res = kernel(sum_kernel, sums, 0, 3)(partial_res, other, cells)
        other = send(partial_res, swap_along["gx"](step))
    wave_middle, xa, xb, ya, yb = kernel(middle_kernel, (wave_v, face_x, face_x, face_y, face_y), 0, 6, [wave_v], cost=pl.CostEstimate(flops=10*10**8, bytes_accessed=0, transcendentals=0))(
        base, speed, xa_in, xb_in, ya_in, yb_in
    )
    y_more, keep, yb, xa = kernel(
        needed_kernel, (tiles_of(faces + 3), tiles_of(3), face_y, face_x), 0, 6, aliases={4: 2, 5: 3}, cost=pl.CostEstimate(flops=30*10**8, bytes_accessed=0, transcendentals=0)
    )(partial_res, other, wave_middle, ya, yb, xa)
    xb_in, xa_in = send(xb, swap_xb), send(xa, swap_xa)
    ya_in, yb_in = send(y_more, swap_ya), send(yb, swap_yb)
    base = kernel(second_local_kernel, wave_v, 0, 4, cost=pl.CostEstimate(flops=0*10**8, bytes_accessed=0, transcendentals=0))(wave_middle, now, speed, keep)
    plane = (2, 1, cells_x, cells_y)
    layers = kernel(inject_kernel, tiles_of(4), 0, 4)(keep, ya_in, cells, speed)
    wave_after, wave_middle = kernel(
        after_kernel, (jax.ShapeDtypeStruct(wave, F32),) * 2, 0, 8,
        [wave_v, wave_v, pltpu.VMEM(plane, F32), pltpu.SemaphoreType.DMA((11,))],
        out_specs=(pl.BlockSpec(memory_space=pl.ANY),) * 2,
    )(base, wave_middle, speed, xa_in, xb_in, ya_in, yb_in, layers)
    return (wave_after, wave_middle)


def solution(mesh):
    return jax.shard_map(
        on_device,
        mesh=mesh,
        in_specs=(
            P("group", None, "gx", "gy"),
            P("group", None, "gx", "gy"),
            P("group", "gx", "gy"),
            P(("group", "gx", "gy"), None, None),
            P("group", ("gx", "gy")),
            P(("group", "gx", "gy")),
            P(("group", "gx", "gy")),
            P("group"),
        ),
        out_specs=(P("group", None, "gx", "gy"), P("group", None, "gx", "gy")),
        check_vma=False,
    )
```
